32 devices in a mesh: dp: 8 (over z, x), tensor: 4 (over y, core).
Axes of the slice: x: 2, y: 2, z: 4, core: 2. Of those that a mesh axis runs over, the one named last changes fastest.
Arguments:
- layer_input: bfloat16 [8, 1032, 1024], P('dp', 'tensor'), may hold values from -6 to 6
- query_weight: bfloat16 [1024, 1024], P('dp', 'tensor'), may hold values from -0.1875 to 0.1875
- key_weight: bfloat16 [1024, 1024], P('dp', 'tensor'), may hold values from -0.1875 to 0.1875
- value_weight: bfloat16 [1024, 1024], P('dp', 'tensor'), may hold values from -0.1875 to 0.1875
- query_bias: bfloat16 [1024], P('dp'), may hold values from -3 to 3
- value_bias: bfloat16 [1024], P('dp'), may hold values from -3 to 3
- first_gain: bfloat16 [1024], P('dp'), may hold values from 0.099609375 to 1.8984375
- first_bias: bfloat16 [1024], P('dp'), may hold values from -3 to 3
- mixer_gain: bfloat16 [1024], P('dp'), may hold values from 0.099609375 to 1.8984375
- mixer_bias: bfloat16 [1024], P('dp'), may hold values from -3 to 3
- output_weight: bfloat16 [1024, 1024], P('tensor', 'dp'), may hold values from -0.1875 to 0.1875
- output_bias: bfloat16 [1024], P('dp'), may hold values from -3 to 3
- second_gain: bfloat16 [1024], P('dp'), may hold values from 0.099609375 to 1.8984375
- second_bias: bfloat16 [1024], P('dp'), may hold values from -3 to 3
- gate_weight: bfloat16 [1024, 2736], P('dp', 'tensor'), may hold values from -0.1875 to 0.1875
- up_weight: bfloat16 [1024, 2736], P('dp', 'tensor'), may hold values from -0.1875 to 0.1875
- gate_bias: bfloat16 [2736], P('tensor'), may hold values from -3 to 3
- up_bias: bfloat16 [2736], P('tensor'), may hold values from -3 to 3
- inner_gain: bfloat16 [2736], P('tensor'), may hold values from 0.099609375 to 1.8984375
- inner_bias: bfloat16 [2736], P('tensor'), may hold values from -3 to 3
- down_weight: bfloat16 [2736, 1024], P('tensor', 'dp'), may hold values from -0.109375 to 0.109375
- down_bias: bfloat16 [1024], P('dp'), may hold values from -3 to 3
- cotangent: bfloat16 [8, 1032, 1024], P('dp', 'tensor'), may hold values from -6 to 6
- key_valid: int32 [8, 1032], P('dp'), may hold values from 0 to 1, as said below
- patch_row: int32 [8, 1032], P('dp'), may hold values from 0 to 31
- patch_column: int32 [8, 1032], P('dp'), may hold values from 0 to 31
Outputs:
- layer_output: bfloat16 [8, 1032, 1024], P('dp', 'tensor')
- input_grad: float32 [8, 1032, 1024], P('dp', 'tensor')
- query_weight_grad: float32 [1024, 1024], P('dp', 'tensor')
- key_weight_grad: float32 [1024, 1024], P('dp', 'tensor')
- value_weight_grad: float32 [1024, 1024], P('dp', 'tensor')
- query_bias_grad: float32 [1024], P('dp')
- value_bias_grad: float32 [1024], P('dp')
- first_gain_grad: float32 [1024], P('dp')
- first_bias_grad: float32 [1024], P('dp')
- mixer_gain_grad: float32 [1024], P('dp')
- mixer_bias_grad: float32 [1024], P('dp')
- output_weight_grad: float32 [1024, 1024], P('tensor', 'dp')
- output_bias_grad: float32 [1024], P('dp')
- second_gain_grad: float32 [1024], P('dp')
- second_bias_grad: float32 [1024], P('dp')
- gate_weight_grad: float32 [1024, 2736], P('dp', 'tensor')
- up_weight_grad: float32 [1024, 2736], P('dp', 'tensor')
- gate_bias_grad: float32 [2736], P('tensor')
- up_bias_grad: float32 [2736], P('tensor')
- inner_gain_grad: float32 [2736], P('tensor')
- inner_bias_grad: float32 [2736], P('tensor')
- down_weight_grad: float32 [2736, 1024], P('tensor', 'dp')
- down_bias_grad: float32 [1024], P('dp')
The draws below stay inside these ranges and needn't reach their ends.
Inputs may be any that keep to these rules, and one draw needn't show every extreme that they name: `key_valid`: slot 0 of every image, the class token, is a valid key.
All inputs are finite; a program needn't handle non-finite values.
Results may differ from the reference program's by a relative error of at most 0.015.
Values may be sent and summed in bfloat16 or wider, within the bound.
No kernel may reach another device: no remote copies, remote signals or barrier semaphores. Data moves between devices by JAX's collectives and lax.ppermute only.
A program may use at most 128 MiB of HBM per device.

```python
import math
import jax
import jax.numpy as jnp
from jax import lax

D = 1024
HD = 64
FF = 2736
LEN = 1032
GRID = 32
IMAGES = 8


def draw_key_valid(key, part):
    levels = jax.random.randint(key, (IMAGES, LEN), 0, 8)
    valid_keys = (levels < 7).astype(jnp.int32)
    places = jnp.arange(LEN)[None, :]
    return jnp.where(places == 0, 1, valid_keys).astype(jnp.int32)


def plant(drawn, own_key, least, top_value):
    dims = drawn.shape
    index_at = [jax.random.randint(jax.random.fold_in(own_key, axis), (), 0, dims[axis]) for axis in range(len(dims))]
    drawn = drawn.at[tuple(index_at)].set(least)
    longest = dims.index(max(dims))
    index_at[longest] = (index_at[longest] + 1) % dims[longest]
    return drawn.at[tuple(index_at)].set(top_value)


def spiked(values, stream_key, source, target, parts, factor):
    owner, partner = [(jnp.arange(values.shape[axis_at]) // (values.shape[axis_at] // parts)).reshape([-1 if axis == axis_at else 1 for axis in range(values.ndim)]) for axis_at in (source, target)]
    chosen = jax.random.permutation(stream_key, parts)[partner]
    strong = (owner == chosen) | (owner == (partner + parts // 2) % parts)
    return jnp.where(strong, factor * values, values)


def block_scale(rng, extent, pieces, low, high):
    def one(position, blocks):
        heights = jax.random.uniform(jax.random.fold_in(jax.random.fold_in(rng, 6), position), (blocks,), jnp.float32, low / len(pieces), high / len(pieces))
        return jnp.repeat(jnp.exp(heights), extent[position] // blocks).reshape((-1,) + (1,) * (len(extent) - position - 1))

    factor_of = one(*pieces[0])
    for cut in pieces[1:]:
        factor_of = factor_of * one(*cut)
    return factor_of


def normal_values(rng, extent, deviation, limit, split=(), kind=jnp.bfloat16):
    entries = deviation * jax.random.normal(rng, extent, jnp.float32)
    if split:
        entries = entries * block_scale(rng, extent, split, -0.22, 0.18)
    return jnp.clip(entries, -limit, limit).astype(kind)


def gaussian_with(key, extent, width, reach, pieces, heavy, held_as=jnp.bfloat16):
    entries = width * jax.random.normal(key, extent, jnp.float32)
    if pieces:
        entries = entries * block_scale(key, extent, pieces, -0.22, 0.18)
    return jnp.clip(spiked(entries, jax.random.fold_in(key, 3), *heavy), -reach, reach).astype(held_as)


def setup_inputs(seed: int = 0) -> dict:
    seeds = jax.random.split(jax.random.key(seed), 27)
    return {
        "layer_input": normal_values(seeds[0], (IMAGES, LEN, D), 1.0, 6.0, ((0, 8), (1, 4))),
        "query_weight": normal_values(seeds[1], (D, D), D ** -0.5, 0.1875, ((0, 8), (1, 4))),
        "key_weight": normal_values(seeds[2], (D, D), D ** -0.5, 0.1875, ((0, 8), (1, 4))),
        "value_weight": normal_values(seeds[3], (D, D), D ** -0.5, 0.1875, ((0, 8), (1, 4))),
        "query_bias": normal_values(seeds[4], (D,), 0.5, 3.0, ((0, 8),)),
        "value_bias": normal_values(seeds[5], (D,), 0.5, 3.0, ((0, 8),)),
        "first_gain": jnp.clip(1.0 + 0.18 * jax.random.normal(seeds[6], (D,), jnp.float32), 0.099609375, 1.8984375).astype(jnp.bfloat16),
        "first_bias": normal_values(seeds[7], (D,), 0.5, 3.0, ((0, 8),)),
        "mixer_gain": jnp.clip(1.0 + 0.18 * jax.random.normal(seeds[8], (D,), jnp.float32), 0.099609375, 1.8984375).astype(jnp.bfloat16),
        "mixer_bias": normal_values(seeds[9], (D,), 0.5, 3.0, ((0, 8),)),
        "output_weight": normal_values(seeds[10], (D, D), D ** -0.5, 0.1875, ((0, 4), (1, 8))),
        "output_bias": normal_values(seeds[11], (D,), 0.5, 3.0, ((0, 8),)),
        "second_gain": jnp.clip(1.0 + 0.18 * jax.random.normal(seeds[12], (D,), jnp.float32), 0.099609375, 1.8984375).astype(jnp.bfloat16),
        "second_bias": normal_values(seeds[13], (D,), 0.5, 3.0, ((0, 8),)),
        "gate_weight": normal_values(seeds[14], (D, FF), D ** -0.5, 0.1875, ((0, 8), (1, 4))),
        "up_weight": normal_values(seeds[15], (D, FF), D ** -0.5, 0.1875, ((0, 8), (1, 4))),
        "gate_bias": normal_values(seeds[16], (FF,), 0.5, 3.0, ((0, 4),)),
        "up_bias": normal_values(seeds[17], (FF,), 0.5, 3.0, ((0, 4),)),
        "inner_gain": jnp.clip(1.0 + 0.18 * jax.random.normal(seeds[18], (FF,), jnp.float32), 0.099609375, 1.8984375).astype(jnp.bfloat16),
        "inner_bias": normal_values(seeds[19], (FF,), 0.5, 3.0, ((0, 4),)),
        "down_weight": normal_values(seeds[20], (FF, D), FF ** -0.5, 0.109375, ((0, 4), (1, 8))),
        "down_bias": normal_values(seeds[21], (D,), 0.5, 3.0, ((0, 8),)),
        "cotangent": gaussian_with(seeds[22], (IMAGES, LEN, D), 1.0, 6.0, ((0, 8), (1, 4)), (0, 2, 8, 2.0)),
        "key_valid": draw_key_valid(jax.random.fold_in(seeds[26], 71), 0),
        "patch_row": plant(jax.random.randint(seeds[24], (IMAGES, LEN), 0, GRID), jax.random.fold_in(seeds[24], 1), 0, GRID - 1).astype(jnp.int32),
        "patch_column": plant(jax.random.randint(seeds[25], (IMAGES, LEN), 0, GRID), jax.random.fold_in(seeds[25], 1), 0, GRID - 1).astype(jnp.int32),
    }


@jax.custom_vjp
def low(v):
    return lax.optimization_barrier(v.astype(jnp.bfloat16)).astype(jnp.float32)

@jax.custom_vjp
def low_back(v):
    return v

def low_keep(v):
    return (low(v), None)

def low_pass(kept, grad):
    return (grad,)

def back_keep(v):
    return (v, None)

def back_low(kept, grad):
    return (low(grad),)
low.defvjp(low_keep, low_pass)
low_back.defvjp(back_keep, back_low)
EPSILON = 1e-06
PRECISE = lax.Precision.HIGHEST

def layer_norm(values):
    center = lax.optimization_barrier(jnp.mean(values, axis=-1, keepdims=True))
    spread = lax.optimization_barrier(jnp.mean(values * values, axis=-1, keepdims=True)) - center * center
    return (values - center) * lax.rsqrt(spread + EPSILON)

def matmul(former, latter):
    return jnp.dot(former, latter, precision=PRECISE, preferred_element_type=jnp.float32)

def rotary_tables(patch_row, patch_column):
    quarter = HD // 4
    indices = jnp.arange(quarter).astype(jnp.float32)
    frequency = jnp.power(jnp.float32(10000.0), -indices / quarter)
    row_part = patch_row.astype(jnp.float32)[..., None] * frequency
    column_part = patch_column.astype(jnp.float32)[..., None] * frequency
    angles = 0.5 * jnp.concatenate([row_part, column_part], axis=-1)
    places = jnp.arange(patch_row.shape[-1])
    angles = jnp.where((places > 0)[:, None], angles, 0.0)
    return (jnp.cos(angles), jnp.sin(angles))

def rotate_pairs(values, cosine_table, sine_table):
    paired = values.reshape(values.shape[:-1] + (values.shape[-1] // 2, 2))
    even_part = paired[..., 0]
    odd_part = paired[..., 1]
    cosine_wide = cosine_table[..., None, :]
    sine_wide = sine_table[..., None, :]
    turned = jnp.stack([even_part * cosine_wide - odd_part * sine_wide, even_part * sine_wide + odd_part * cosine_wide], axis=-1)
    return turned.reshape(values.shape)

def image_forward(residual, valid_keys, row_pos, column_pos, params):
    query_weight, key_weight, value_weight, query_bias, value_bias, first_gain, first_bias, mixer_gain, mixer_bias, output_weight, output_bias, second_gain, second_bias, gate_weight, up_weight, gate_bias, up_bias, inner_gain, inner_bias, down_weight, down_bias = params
    length = residual.shape[0]
    head_count = residual.shape[1] // HD
    cosine_table, sine_table = rotary_tables(row_pos, column_pos)
    normed_one = low(layer_norm(residual) * first_gain + first_bias)
    query_pre = low_back(matmul(normed_one, query_weight) + query_bias)
    key_pre = low_back(matmul(normed_one, key_weight))
    value_pre = low(low_back(matmul(normed_one, value_weight) + value_bias))
    queries = low(rotate_pairs(query_pre.reshape(length, head_count, HD), cosine_table, sine_table))
    keys = low(rotate_pairs(key_pre.reshape(length, head_count, HD), cosine_table, sine_table))
    values = value_pre.reshape(length, head_count, HD)
    score_scale = 1.0 / math.sqrt(HD)
    scores = low_back(jnp.einsum('qhd,khd->hqk', queries, keys, precision=PRECISE) * score_scale)
    keep_mask = (valid_keys == 1)[None, None, :]
    row_max = lax.optimization_barrier(jnp.max(jnp.where(keep_mask, scores, -1e+30), axis=-1, keepdims=True))
    exp_terms = jnp.where(keep_mask, jnp.exp(scores - row_max), 0.0)
    probabilities = exp_terms / lax.optimization_barrier(jnp.sum(exp_terms, axis=-1, keepdims=True))
    attended = low_back(jnp.einsum('hqk,khd->qhd', low(probabilities), values, precision=PRECISE).reshape(length, -1))
    mixer_result = low(layer_norm(attended) * mixer_gain + mixer_bias)
    branch_one = low_back(matmul(mixer_result, output_weight) + output_bias)
    hidden_state = residual + branch_one
    normed_two = low(layer_norm(hidden_state) * second_gain + second_bias)
    gate_pre = low_back(matmul(normed_two, gate_weight) + gate_bias)
    up_pre = low_back(matmul(normed_two, up_weight) + up_bias)
    activated = jax.nn.silu(gate_pre) * up_pre
    inner_result = low(layer_norm(activated) * inner_gain + inner_bias)
    branch_two = low_back(matmul(inner_result, down_weight) + down_bias)
    return hidden_state + branch_two

def reference(layer_input, query_weight, key_weight, value_weight, query_bias, value_bias, first_gain, first_bias, mixer_gain, mixer_bias, output_weight, output_bias, second_gain, second_bias, gate_weight, up_weight, gate_bias, up_bias, inner_gain, inner_bias, down_weight, down_bias, cotangent, key_valid, patch_row, patch_column):
    params = tuple((element.astype(jnp.float32) for element in (query_weight, key_weight, value_weight, query_bias, value_bias, first_gain, first_bias, mixer_gain, mixer_bias, output_weight, output_bias, second_gain, second_bias, gate_weight, up_weight, gate_bias, up_bias, inner_gain, inner_bias, down_weight, down_bias)))

    def one_image(totals, element):
        residual, grad_output, valid_keys, row_pos, column_pos = element

        def forward_fn(inputs, weights):
            return image_forward(inputs, valid_keys, row_pos, column_pos, weights)
        output, pullback = jax.vjp(forward_fn, residual.astype(jnp.float32), params)
        grad_input, weight_grads = pullback(grad_output.astype(jnp.float32))
        totals = jax.tree.map(lambda former, latter: former + latter, totals, weight_grads)
        return (totals, (output.astype(jnp.bfloat16), grad_input))
    zeros_start = jax.tree.map(jnp.zeros_like, params)
    totals, outputs = lax.scan(one_image, zeros_start, (layer_input, cotangent, key_valid, patch_row, patch_column))
    layer_output, input_grad = outputs
    grad_query, grad_key, grad_value, grad_qbias, grad_vbias, grad_fgain, grad_fbias, grad_mgain, grad_mbias, grad_output, grad_obias, grad_sgain, grad_sbias, grad_gate, grad_up, grad_gbias, grad_ubias, grad_igain, grad_ibias, grad_down, grad_dbias = totals
    return (layer_output, input_grad, grad_query, grad_key, grad_value, grad_qbias, grad_vbias, grad_fgain, grad_fbias, grad_mgain, grad_mbias, grad_output, grad_obias, grad_sgain, grad_sbias, grad_gate, grad_up, grad_gbias, grad_ubias, grad_igain, grad_ibias, grad_down, grad_dbias)
```

```python
import math

import jax
import jax.numpy as jnp
from jax import lax
from jax.sharding import PartitionSpec as P

HD = 64
EPSILON = 1e-06
BF = jnp.bfloat16
F32 = jnp.float32


def swap(value, axis, offset):
    count = lax.axis_size(axis)
    return lax.ppermute(value, axis, [(i, i ^ offset) for i in range(count)])


def tensor_gather(block):
    core = swap(block, "tensor", 1)
    far = swap(block, "tensor", 2)
    diagonal = swap(far, "tensor", 1)
    return [block, core, far, diagonal]


def tensor_scatter(parts):
    core = [swap(parts[k].astype(BF), "tensor", 1) for k in (3, 1)]
    to_far = (parts[2].astype(F32) + core[0].astype(F32)).astype(BF)
    far = swap(to_far, "tensor", 2)
    return parts[0].astype(F32) + core[1].astype(F32) + far.astype(F32)


def tensor_sum(value):
    blocks = value.reshape(value.shape[0], 4, -1)
    total = blocks
    for k in (1, 2, 3):
        other = swap(blocks, "tensor", k)
        total = total + jnp.stack([other[:, r ^ k] for r in range(4)], axis=1)
    return total.reshape(value.shape)


def dp_gather(block):
    count = lax.axis_size("dp")
    column = [block] + [swap(block, "dp", 2 * k) for k in range(1, count // 2)]
    across = [swap(one, "dp", 1) for one in column]
    return [one for pair in zip(column, across) for one in pair]


def dp_order(chunks):
    stacked = jnp.stack(chunks) if isinstance(chunks, list) else chunks
    me = lax.axis_index("dp")
    count = stacked.shape[0]
    return jnp.stack([lax.dynamic_index_in_dim(stacked, me ^ r, 0, False) for r in range(count)])


def dp_scatter(chunks):
    count = chunks.shape[0]
    pairs = chunks.reshape((count // 2, 2) + chunks.shape[1:])
    across = swap(pairs[:, 1], "dp", 1)
    halves = pairs[:, 0].astype(F32) + across.astype(F32)
    total = halves[0]
    for k in range(1, count // 2):
        total = total + swap(halves[k].astype(BF), "dp", 2 * k).astype(F32)
    return total


def stats(values):
    center = jnp.mean(values, axis=-1, keepdims=True)
    spread = jnp.mean(values * values, axis=-1, keepdims=True) - center * center
    return center, lax.rsqrt(spread + EPSILON)


def normalize_back(grad_hat, unit_hat, inverse):
    return inverse * (
        grad_hat
        - jnp.mean(grad_hat, axis=-1, keepdims=True)
        - unit_hat * jnp.mean(grad_hat * unit_hat, axis=-1, keepdims=True)
    )


def mm(a, b):
    return jnp.einsum("ij,jk->ik", a, b, preferred_element_type=F32)


def mm_nt(a, b):
    return jnp.einsum("ij,kj->ik", a, b, preferred_element_type=F32)


def mm_tn(a, b):
    return jnp.einsum("ji,jk->ik", a, b, preferred_element_type=F32)


def rotary(patch_row, patch_column, place):
    quarter = HD // 4
    indices = jnp.arange(quarter).astype(F32)
    frequency = jnp.power(F32(10000.0), -indices / quarter)
    row_part = patch_row.astype(F32)[:, None] * frequency
    column_part = patch_column.astype(F32)[:, None] * frequency
    angles = 0.5 * jnp.concatenate([row_part, column_part], axis=-1)
    angles = jnp.where((place > 0)[:, None], angles, 0.0)
    return jnp.cos(angles), jnp.sin(angles)


def turn(values, cosine, sine):
    paired = values.reshape(values.shape[0], -1, HD // 2, 2)
    even, odd = paired[..., 0], paired[..., 1]
    c, s = cosine[:, None, :], sine[:, None, :]
    return jnp.stack([even * c - odd * s, even * s + odd * c], axis=-1).reshape(values.shape)


def attend(element):
    query, key, value, keep = element
    scale = 1.0 / math.sqrt(HD)
    scores = jnp.where(keep[None, :], mm_nt(query, key) * scale, -1e30)
    row_max = jnp.max(scores, axis=-1, keepdims=True)
    terms = jnp.exp(scores - row_max)
    denominator = jnp.sum(terms, axis=-1, keepdims=True)
    attended = mm((terms / denominator).astype(BF), value)
    return attended, (row_max + jnp.log(denominator))[:, 0]


def attend_back(element):
    query, key, value, keep, logsum, grad = element
    scale = 1.0 / math.sqrt(HD)
    scores = jnp.where(keep[None, :], mm_nt(query, key) * scale, -1e30)
    probs = jnp.exp(scores - logsum[:, None])
    grad_value = mm_tn(probs.astype(BF), grad)
    grad_probs = mm_nt(grad, value)
    grad_scores = (
        probs * (grad_probs - jnp.sum(probs * grad_probs, axis=-1, keepdims=True))
    ).astype(BF)
    return mm(grad_scores, key) * scale, mm_tn(grad_scores, query) * scale, grad_value


def heads(values):
    return values.reshape(values.shape[0], -1, HD).transpose(1, 0, 2)


def unheads(items):
    return items.transpose(1, 0, 2).reshape(items.shape[1], -1)


def local(
    layer_input, query_weight, key_weight, value_weight, query_bias, value_bias, first_gain, first_bias,
    mixer_gain, mixer_bias, output_weight, output_bias, second_gain, second_bias, gate_weight, up_weight,
    gate_bias, up_bias, inner_gain, inner_bias, down_weight, down_bias, cotangent, key_valid, patch_row, patch_column,
):
    ranks = lax.axis_size("tensor")
    me_t, me_d, count_d = lax.axis_index("tensor"), lax.axis_index("dp"), lax.axis_size("dp")
    width = layer_input.shape[2]
    block = layer_input.shape[1]
    padded = -(-block // 16) * 16
    head_width = query_weight.shape[1]
    hidden = gate_weight.shape[1]

    def pad(rows):
        return jnp.pad(rows, ((0, padded - block), (0, 0)))

    def cut(rows):
        return [rows[k * padded : k * padded + block] for k in range(ranks)]

    x_own = layer_input[0]
    cot_own = cotangent[0]
    small = jnp.stack(
        [query_bias, value_bias, first_gain, first_bias, mixer_gain, mixer_bias, output_bias, second_gain,
         second_bias, down_bias]
    )
    rows = jnp.concatenate([query_weight, key_weight, value_weight], axis=1)
    x_all = jnp.concatenate([pad(b) for b in tensor_gather(x_own)]).astype(F32)
    small_all = dp_order(dp_gather(small)).transpose(1, 0, 2).reshape(-1, width)
    qkv_full = dp_order(dp_gather(rows)).reshape(width, -1)
    cot_all = jnp.concatenate([pad(b) for b in tensor_gather(cot_own)])
    out_full = dp_order(dp_gather(output_weight)).transpose(1, 0, 2).reshape(head_width, width)
    gate_full = dp_order(dp_gather(gate_weight)).reshape(width, hidden)
    up_full = dp_order(dp_gather(up_weight)).reshape(width, hidden)
    down_full = dp_order(dp_gather(down_weight)).transpose(1, 0, 2).reshape(hidden, width)
    vec = small_all.astype(F32)
    own = [lax.dynamic_slice_in_dim(vec[k], me_t * head_width, head_width) for k in range(10)]
    q_bias, v_bias, m_gain, m_bias = own[0], own[1], own[4], own[5]
    f_gain, f_bias, o_bias, s_gain, s_bias, d_bias = vec[2], vec[3], vec[6], vec[7], vec[8], vec[9]
    gate_b, up_b, i_gain, i_bias = (v.astype(F32) for v in (gate_bias, up_bias, inner_gain, inner_bias))

    def tokens(vector):
        blocks = vector.reshape(ranks, block)
        picked = [jnp.pad(lax.dynamic_index_in_dim(blocks, me_t ^ r, 0, False), (0, padded - block)) for r in range(ranks)]
        return jnp.concatenate(picked)

    keep = tokens(key_valid[0]) == 1
    place = tokens(jnp.arange(ranks * block))
    cosine, sine = rotary(tokens(patch_row[0]), tokens(patch_column[0]), place)

    center, inverse_one = stats(x_all)
    unit_one = (x_all - center) * inverse_one
    first = (unit_one * f_gain + f_bias).astype(BF)
    qkv = mm(first, qkv_full)
    queries = turn(qkv[:, :head_width] + q_bias, cosine, sine).astype(BF)
    keys = turn(qkv[:, head_width : 2 * head_width], cosine, sine).astype(BF)
    values = (qkv[:, 2 * head_width :] + v_bias).astype(BF)
    queries, keys, values = heads(queries), heads(keys), heads(values)
    keeps = jnp.broadcast_to(keep, (queries.shape[0], keep.shape[0]))
    items, logsum = lax.map(attend, (queries, keys, values, keeps))
    attended = unheads(items)
    sums = tensor_sum(jnp.stack([jnp.sum(attended, -1), jnp.sum(attended * attended, -1)]))
    mean = (sums[0] / width)[:, None]
    inverse_mix = lax.rsqrt((sums[1] / width)[:, None] - mean * mean + EPSILON)
    unit_mix = (attended - mean) * inverse_mix
    mixed = (unit_mix * m_gain + m_bias).astype(BF)
    hidden_state = x_own.astype(F32) + tensor_scatter(cut(mm(mixed, out_full).astype(BF))) + o_bias

    center, inverse_two = stats(hidden_state)
    unit_two = (hidden_state - center) * inverse_two
    second_own = (unit_two * s_gain + s_bias).astype(BF)
    second = jnp.concatenate([pad(b) for b in tensor_gather(second_own)])
    gate = mm(second, gate_full) + gate_b
    up = mm(second, up_full) + up_b
    sigmoid = jax.nn.sigmoid(gate)
    activated = gate * sigmoid * up
    grad_inner = mm_nt(cot_all, down_full)
    grad_hat = grad_inner * i_gain
    sums = tensor_sum(
        jnp.stack(
            [jnp.sum(activated, -1), jnp.sum(activated * activated, -1), jnp.sum(grad_hat, -1),
             jnp.sum(grad_hat * activated, -1)]
        )
    )
    hidden_all = hidden * ranks
    mean = (sums[0] / hidden_all)[:, None]
    inverse = lax.rsqrt((sums[1] / hidden_all)[:, None] - mean * mean + EPSILON)
    unit = (activated - mean) * inverse
    inner = (unit * i_gain + i_bias).astype(BF)
    grad_mean = (sums[2] / hidden_all)[:, None]
    cross = inverse * ((sums[3] / hidden_all)[:, None] - mean * grad_mean)
    grad_activated = inverse * (grad_hat - grad_mean - unit * cross)
    grad_gate = (grad_activated * up * sigmoid * (1.0 + gate * (1.0 - sigmoid))).astype(BF)
    grad_up = (grad_activated * gate * sigmoid).astype(BF)
    grad_second = tensor_scatter(cut((mm_nt(grad_gate, gate_full) + mm_nt(grad_up, up_full)).astype(BF)))
    layer_output = (hidden_state + tensor_scatter(cut(mm(inner, down_full).astype(BF))) + d_bias).astype(BF)

    def row_chunks(grad):
        return dp_order(grad.astype(BF).reshape(count_d, width // count_d, -1))

    def column_chunks(grad):
        return dp_order(grad.astype(BF).reshape(grad.shape[0], count_d, -1).transpose(1, 0, 2))

    down_grad = dp_scatter(column_chunks(mm_tn(inner, cot_all)))
    gate_grad = dp_scatter(row_chunks(mm_tn(second, grad_gate)))
    up_grad = dp_scatter(row_chunks(mm_tn(second, grad_up)))

    cot_f = cot_own.astype(F32)
    grad_hidden = cot_f + normalize_back(grad_second * s_gain, unit_two, inverse_two)
    branch_own = grad_hidden.astype(BF)
    branch = jnp.concatenate([pad(b) for b in tensor_gather(branch_own)])
    grad_mixed = mm_nt(branch, out_full)
    grad_hat = grad_mixed * m_gain
    sums = tensor_sum(jnp.stack([jnp.sum(grad_hat, -1), jnp.sum(grad_hat * unit_mix, -1)]))
    grad_attended = (
        inverse_mix * (grad_hat - (sums[0] / width)[:, None] - unit_mix * (sums[1] / width)[:, None])
    ).astype(BF)
    out_grad = dp_scatter(column_chunks(mm_tn(mixed, branch)))
    grad_q, grad_k, grad_v = lax.map(attend_back, (queries, keys, values, keeps, logsum, heads(grad_attended)))
    grad_q = turn(unheads(grad_q), cosine, -sine).astype(BF)
    grad_k = turn(unheads(grad_k), cosine, -sine).astype(BF)
    grad_v = unheads(grad_v).astype(BF)
    grad_qkv = jnp.concatenate([grad_q, grad_k, grad_v], axis=1)
    grad_first_part = mm_nt(grad_qkv, qkv_full)
    grad_first = tensor_scatter(cut(grad_first_part.astype(BF)))
    qkv_grad = dp_scatter(row_chunks(mm_tn(first, grad_qkv)))
    input_grad = grad_hidden + normalize_back(grad_first * f_gain, unit_one[:block], inverse_one[:block])

    def total(rows):
        return jnp.sum(rows.astype(F32), axis=0)

    def place_piece(piece):
        return lax.dynamic_update_slice_in_dim(jnp.zeros((width,), F32), piece, me_t * head_width, 0)

    model = jnp.stack(
        [total(grad_first_part * unit_one), total(grad_first_part), place_piece(total(grad_q)), place_piece(total(grad_v)),
         place_piece(total(grad_mixed * unit_mix)), place_piece(total(grad_mixed)), total(branch_own),
         total(grad_second * unit_two), total(grad_second), total(cot_f)]
    )
    ffn = jnp.stack([total(grad_gate), total(grad_up), total(grad_inner * unit), total(grad_inner)])
    model = lax.psum(model, ("dp", "tensor"))
    ffn = lax.psum(ffn, "dp")
    mine = lax.dynamic_slice_in_dim(model, me_d * (width // count_d), width // count_d, 1)
    return (
        layer_output[None], input_grad[None],
        qkv_grad[:, :head_width], qkv_grad[:, head_width : 2 * head_width], qkv_grad[:, 2 * head_width :],
        mine[2], mine[3], mine[0], mine[1], mine[4], mine[5], out_grad, mine[6], mine[7], mine[8],
        gate_grad, up_grad, ffn[0], ffn[1], ffn[2], ffn[3], down_grad, mine[9],
    )


def solution(mesh):
    rows, across, tokens = P("dp", "tensor"), P("tensor", "dp"), P("dp", "tensor", None)
    model, ffn, image = P("dp"), P("tensor"), P("dp", None)
    in_specs = (
        tokens, rows, rows, rows, model, model, model, model, model, model, across, model, model, model, rows, rows,
        ffn, ffn, ffn, ffn, across, model, tokens, image, image, image,
    )
    out_specs = (
        tokens, tokens, rows, rows, rows, model, model, model, model, model, model, across, model, model, model,
        rows, rows, ffn, ffn, ffn, ffn, across, model,
    )
    return jax.shard_map(local, mesh=mesh, in_specs=in_specs, out_specs=out_specs, check_vma=False)
```

```python
import functools
import math

import jax
import jax.numpy as jnp
from jax import lax
from jax.experimental import pallas as pl
from jax.experimental.pallas import tpu as pltpu
from jax.sharding import PartitionSpec as P

HD = 64
EPSILON = 1e-06
LOW = -1e30
BF = jnp.bfloat16
F32 = jnp.float32
HI = lax.Precision.HIGHEST
VM = pl.BlockSpec(memory_space=pltpu.VMEM)
SM = pl.BlockSpec(memory_space=pltpu.SMEM)
HB = pl.BlockSpec(memory_space=pl.ANY)
Q_BIAS, V_BIAS, F_GAIN, F_BIAS, M_GAIN, M_BIAS, O_BIAS, S_GAIN, S_BIAS, D_BIAS = range(10)


def nn(a, b, precision=None):
    return lax.dot_general(a, b, (((1,), (0,)), ((), ())), precision, F32)


def nt(a, b, precision=None):
    return lax.dot_general(a, b, (((1,), (1,)), ((), ())), precision, F32)


def tn(a, b, precision=None):
    return lax.dot_general(a, b, (((0,), (0,)), ((), ())), precision, F32)


def call(body, outs, *args, specs=None, mib=32, flops=0, name=None, **extra):
    shapes = [jax.ShapeDtypeStruct(shape, dtype) for shape, dtype in outs]
    moved = sum(a.size * a.dtype.itemsize for a in args) + sum(math.prod(s.shape) * s.dtype.itemsize for s in shapes)
    return pl.pallas_call(
        body,
        out_shape=shapes,
        in_specs=specs or [VM] * len(args),
        out_specs=[VM] * len(shapes),
        compiler_params=pltpu.CompilerParams(vmem_limit_bytes=mib << 20),
        cost_estimate=pl.CostEstimate(flops=int(flops), bytes_accessed=int(moved), transcendentals=0),
        name=name,
        **extra,
    )(*args)


def swap(value, axis, offset):
    count = lax.axis_size(axis)
    return lax.ppermute(value, axis, [(i, i ^ offset) for i in range(count)])


def tensor_gather(block):
    core = swap(block, "tensor", 1)
    far = swap(block, "tensor", 2)
    return [block, core, far, swap(far, "tensor", 1)]


def tensor_scatter(parts):
    third = swap(parts[3], "tensor", 1)
    first = swap(parts[1], "tensor", 1)
    to_far = (parts[2].astype(F32) + third.astype(F32)).astype(BF)
    return [parts[0], first, swap(to_far, "tensor", 2)]


def tensor_share(value):
    return [value] + [swap(value, "tensor", k) for k in (1, 2, 3)]


def dp_gather(block):
    count = lax.axis_size("dp")
    column = [block] + [swap(block, "dp", 2 * k) for k in range(1, count // 2)]
    across = [swap(one, "dp", 1) for one in column]
    return [one for pair in zip(column, across) for one in pair]


def tie(value, *others):
    def body(*refs):
        pass

    return pl.pallas_call(
        body,
        out_shape=jax.ShapeDtypeStruct(value.shape, value.dtype),
        in_specs=[HB] * (1 + len(others)),
        out_specs=HB,
        input_output_aliases={0: 0},
        name="tie",
    )(value, *others)


def center_scale(values):
    width = values.shape[-1]
    mean = jnp.sum(values, axis=-1, keepdims=True) / width
    spread = jnp.sum(values * values, axis=-1, keepdims=True) / width - mean * mean
    return mean, lax.rsqrt(spread + EPSILON)


def unit_back(grad_hat, unit, inverse):
    width = unit.shape[-1]
    mean = jnp.sum(grad_hat, axis=-1, keepdims=True) / width
    cross = jnp.sum(grad_hat * unit, axis=-1, keepdims=True) / width
    return inverse * (grad_hat - mean - unit * cross)


def columns_to_rows(columns):
    count = columns[0].shape[0]
    lanes = lax.broadcasted_iota(jnp.int32, (count, 128), 1)
    wide = jnp.zeros((count, 128), F32)
    for k, column in enumerate(columns):
        wide = jnp.where(lanes == k, column, wide)
    return wide.T[0:8]


def rows_to_columns(rows):
    return rows.T


def summed_stats(refs, r):
    return refs[0][r] + refs[1][r ^ 1] + refs[2][r ^ 2] + refs[3][r ^ 3]


def turn(values, cosine, sine):
    lanes = lax.broadcasted_iota(jnp.int32, values.shape, 1)
    other = jnp.where(lanes % 2 == 0, pltpu.roll(values, 127, 1), pltpu.roll(values, 1, 1))
    return values * cosine + other * sine


def half_mask(s):
    lane = lax.broadcasted_iota(jnp.int32, (1, 128), 1)
    return lane < HD if s == 0 else lane >= HD


def local(
    layer_input, query_weight, key_weight, value_weight, query_bias, value_bias, first_gain, first_bias,
    mixer_gain, mixer_bias, output_weight, output_bias, second_gain, second_bias, gate_weight, up_weight,
    gate_bias, up_bias, inner_gain, inner_bias, down_weight, down_bias, cotangent, key_valid, patch_row, patch_column,
):
    ranks = lax.axis_size("tensor")
    me_t, me_d, count_d = lax.axis_index("tensor"), lax.axis_index("dp"), lax.axis_size("dp")
    block, width = layer_input.shape[1:]
    pad = -(-block // 16) * 16
    length = ranks * pad
    heads = query_weight.shape[1]
    hidden = gate_weight.shape[1]
    hidden_pad = -(-hidden // 128) * 128
    own_rows = width // count_d
    direct = own_rows % 128 == 0 and count_d & (count_d - 1) == 0
    index = jnp.stack([me_d, me_t]).astype(jnp.int32)
    x_own, cot_own = layer_input[0], cotangent[0]
    blocks = range(ranks)

    def rows_of(r):
        return slice(r * pad, (r + 1) * pad)

    small = jnp.stack(
        [query_bias, value_bias, first_gain, first_bias, mixer_gain, mixer_bias, output_bias, second_gain,
         second_bias, down_bias] + [jnp.zeros_like(down_bias)] * 6
    )
    x_blocks = tensor_gather(x_own)
    if direct:
        tiles = heads // 128
        full_tiles = hidden // 128
        tail = hidden - full_tiles * 128
        pack_a = jnp.concatenate(
            [w[:, k * 128 : (k + 1) * 128] for w in (query_weight, key_weight, value_weight) for k in range(tiles)]
            + [small]
        )
        gates = [w[:, k * 128 : (k + 1) * 128] for w in (gate_weight, up_weight) for k in range(full_tiles)]
        gates += [jnp.pad(w[:, full_tiles * 128 :], ((0, 0), (0, 128 - tail))) for w in (gate_weight, up_weight)]
        pack_b = jnp.concatenate(gates)
        pack_c = jnp.concatenate([output_weight, jnp.pad(down_weight, ((0, hidden_pad - hidden), (0, 0)))])
        got_a = dp_gather(pack_a)
        pack_c = tie(pack_c, *got_a[2::2])
        got_c = dp_gather(pack_c)
        pack_b = tie(pack_b, *got_c[2::2])
        got_b = dp_gather(pack_b)

        def assemble_a(index_ref, *refs):
            chunks, (w_ref, v_ref) = refs[:-2], refs[-2:]
            for r, chunk in enumerate(chunks):
                at = pl.multiple_of((index_ref[0] ^ r) * own_rows, 128)
                for k in range(3 * tiles):
                    w_ref[pl.ds(at, own_rows), k * 128 : (k + 1) * 128] = chunk[k * own_rows : (k + 1) * own_rows]
                v_ref[:, pl.ds(at, own_rows)] = chunk[3 * tiles * own_rows :].astype(F32)

        def assemble_b(index_ref, *refs):
            chunks, outs = refs[:-2], refs[-2:]
            for r, chunk in enumerate(chunks):
                at = pl.multiple_of((index_ref[0] ^ r) * own_rows, 128)
                for j in range(2):
                    for k in range(full_tiles):
                        outs[j][pl.ds(at, own_rows), k * 128 : (k + 1) * 128] = chunk[
                            (j * full_tiles + k) * own_rows : (j * full_tiles + k + 1) * own_rows
                        ]
                    outs[j][pl.ds(at, own_rows), full_tiles * 128 :] = chunk[
                        (2 * full_tiles + j) * own_rows : (2 * full_tiles + j + 1) * own_rows
                    ]

        def assemble_c(index_ref, *refs):
            chunks, (o_ref, d_ref) = refs[:-2], refs[-2:]
            for r, chunk in enumerate(chunks):
                at = pl.multiple_of((index_ref[0] ^ r) * own_rows, 128)
                o_ref[:, pl.ds(at, own_rows)] = chunk[:heads]
                d_ref[:, pl.ds(at, own_rows)] = chunk[heads:]

        specs = [SM] + [VM] * count_d
        w_qkv, vec = call(
            assemble_a, [((width, 3 * heads), BF), ((16, width), F32)], index, *got_a, specs=specs, name="assemble_a"
        )
        w_out, w_down = call(
            assemble_c, [((heads, width), BF), ((hidden_pad, width), BF)], index, *got_c, specs=specs, name="assemble_c"
        )
        w_gate, w_up = call(
            assemble_b, [((width, hidden_pad), BF)] * 2, index, *got_b, specs=specs, name="assemble_b"
        )
    else:
        def whole(weight, axis):
            return lax.all_gather(weight, "dp", axis=axis, tiled=True)

        w_qkv = whole(jnp.concatenate([query_weight, key_weight, value_weight], axis=1), 0)
        vec = whole(small, 1).astype(F32)
        w_out = whole(output_weight, 1)
        w_down = jnp.pad(whole(down_weight, 1), ((0, hidden_pad - hidden), (0, 0)))
        w_gate, w_up = (
            jnp.pad(whole(w, 0), ((0, 0), (0, hidden_pad - hidden))) for w in (gate_weight, up_weight)
        )
    cot_blocks = tensor_gather(cot_own)
    ffn_vec = jnp.pad(
        jnp.stack([gate_bias, up_bias, inner_gain, inner_bias]).astype(F32), ((0, 4), (0, hidden_pad - hidden))
    )

    def tokens(vector):
        parts = vector.reshape(ranks, block)
        picked = [
            jnp.pad(lax.dynamic_index_in_dim(parts, me_t ^ r, 0, False), (0, pad - block)) for r in blocks
        ]
        return jnp.concatenate(picked)

    mask = jnp.where(tokens(key_valid[0]) == 1, 0.0, LOW).astype(F32)
    mask_row = jnp.broadcast_to(mask[None, :], (8, length))
    mask_column = jnp.broadcast_to(mask[:, None], (length, 128))
    quarter = HD // 4
    frequency = jnp.power(F32(10000.0), -jnp.arange(quarter).astype(F32) / quarter)
    place = tokens(jnp.arange(ranks * block))
    angles = 0.5 * jnp.concatenate(
        [tokens(p[0]).astype(F32)[:, None] * frequency for p in (patch_row, patch_column)], axis=-1
    )
    angles = jnp.where((place > 0)[:, None], angles, 0.0)
    cosine, sine = jnp.cos(angles), jnp.sin(angles)
    cosine = jnp.tile(jnp.repeat(cosine, 2, axis=1), (1, 128 // HD))
    sine = jnp.tile(jnp.stack([-sine, sine], axis=-1).reshape(length, HD), (1, 128 // HD))

    def own(ref, k, index_ref):
        return ref[k : k + 1, pl.ds(pl.multiple_of(index_ref[1] * heads, 128), heads)]

    def project_body(index_ref, x0, x1, x2, x3, w_ref, vec_ref, cos_ref, sin_ref, first_ref, q_ref, k_ref, v_ref):
        gain, bias = vec_ref[F_GAIN : F_GAIN + 1], vec_ref[F_BIAS : F_BIAS + 1]
        q_bias, v_bias = own(vec_ref, Q_BIAS, index_ref), own(vec_ref, V_BIAS, index_ref)
        for r, x_ref in enumerate((x0, x1, x2, x3)):
            x = x_ref[...].astype(F32)
            mean, inverse = center_scale(x)
            first_ref[(r + 1) * pad - 16 : (r + 1) * pad] = jnp.zeros((16, width), BF)
            first_ref[r * pad : r * pad + block] = ((x - mean) * inverse * gain + bias).astype(BF)
            rows = rows_of(r)
            qkv = nn(first_ref[rows], w_ref[...])
            v_ref[rows] = (qkv[:, 2 * heads :] + v_bias).astype(BF)
            c, s = cos_ref[rows], sin_ref[rows]
            for k in range(heads // 128):
                cols = slice(k * 128, (k + 1) * 128)
                q_ref[rows, cols] = turn(qkv[:, cols] + q_bias[:, cols], c, s).astype(BF)
                k_ref[rows, cols] = turn(qkv[:, heads + k * 128 : heads + (k + 1) * 128], c, s).astype(BF)

    first, queries, keys, values = call(
        project_body, [((length, width), BF)] + [((length, heads), BF)] * 3,
        index, *x_blocks, w_qkv, vec, cosine, sine, specs=[SM] + [VM] * 8, name="project",
        flops=2 * length * width * 3 * heads,
    )

    def attend_body(q_ref, k_ref, v_ref, mask_ref, o_ref, stat_ref):
        mask_line = mask_ref[0:1]
        k_half, v_half = [], []
        for h in range(heads // HD):
            cols = slice(h // 2 * 128, (h // 2 + 1) * 128)
            k_half.append(jnp.where(half_mask(h % 2), k_ref[:, cols], 0).astype(BF))
            v_half.append(jnp.where(half_mask(h % 2), v_ref[:, cols], 0).astype(BF))

        def step(b, _):
            rows = pl.ds(pl.multiple_of(b * pad, 16), pad)
            kept = []
            total = jnp.zeros((pad, 1), F32)
            square = jnp.zeros((pad, 1), F32)
            for pair in range(heads // 128):
                cols = slice(pair * 128, (pair + 1) * 128)
                q = q_ref[rows, cols]
                out = jnp.zeros((pad, 128), F32)
                for s in range(2):
                    h = 2 * pair + s
                    scores = nt(q, k_half[h]) * (1.0 / math.sqrt(HD)) + mask_line
                    top = jnp.max(scores, axis=-1, keepdims=True)
                    terms = jnp.exp(scores - top)
                    below = jnp.sum(terms, axis=-1, keepdims=True)
                    out += nn(terms.astype(BF), v_half[h]) * (1.0 / below)
                    kept.append(top + jnp.log(below))
                o_ref[rows, cols] = out
                total += jnp.sum(out, axis=-1, keepdims=True)
                square += jnp.sum(out * out, axis=-1, keepdims=True)
            stat_ref[b] = columns_to_rows(kept + [total, square])
            return 0

        lax.fori_loop(0, ranks, step, 0)

    n_heads = heads // HD
    attended, stat_mix = call(
        attend_body, [((length, heads), F32), ((ranks, 8, pad), F32)], queries, keys, values, mask_row, name="attend",
        flops=4 * length * length * heads,
    )
    shared_mix = tensor_share(stat_mix)

    def mix_body(index_ref, a_ref, s0, s1, s2, s3, w_ref, vec_ref, mixed_ref, norm_ref, *part_refs):
        gain, bias = own(vec_ref, M_GAIN, index_ref), own(vec_ref, M_BIAS, index_ref)
        for r in reversed(blocks):
            rows = rows_of(r)
            sums = summed_stats((s0, s1, s2, s3), r)
            mean = sums[n_heads : n_heads + 1] / width
            inverse = lax.rsqrt(sums[n_heads + 1 : n_heads + 2] / width - mean * mean + EPSILON)
            lines = jnp.concatenate([mean, inverse, jnp.zeros((6, pad), F32)], axis=0)
            norm_ref[r] = lines
            columns = rows_to_columns(lines)
            mixed = ((a_ref[rows] - columns[:, 0:1]) * columns[:, 1:2] * gain + bias).astype(BF)
            mixed_ref[rows] = mixed
            part_refs[r][...] = nn(mixed, w_ref[...])[:block].astype(BF)

    mixed, norm_mix, *parts = call(
        mix_body, [((length, heads), BF), ((ranks, 8, pad), F32)] + [((block, width), BF)] * ranks,
        index, attended, *shared_mix, w_out, vec, specs=[SM] + [VM] * 7, name="mix", flops=2 * length * heads * width,
    )
    arrived = tensor_scatter(parts)

    def second_body(x_ref, p0, p1, p2, vec_ref, hidden_ref, second_ref):
        out = p0[...].astype(F32) + p1[...].astype(F32) + p2[...].astype(F32)
        state = x_ref[...].astype(F32) + out + vec_ref[O_BIAS : O_BIAS + 1]
        hidden_ref[...] = state
        mean, inverse = center_scale(state)
        unit = (state - mean) * inverse
        second_ref[...] = (unit * vec_ref[S_GAIN : S_GAIN + 1] + vec_ref[S_BIAS : S_BIAS + 1]).astype(BF)

    hidden_state, second_own = call(
        second_body, [((block, width), F32), ((block, width), BF)], x_own, *arrived, vec, name="second"
    )
    second_blocks = tensor_gather(second_own)

    def inner_grad_body(c0, c1, c2, c3, w_ref, cot_ref, grad_ref):
        for r, c_ref in enumerate((c0, c1, c2, c3)):
            cot_ref[(r + 1) * pad - 16 : (r + 1) * pad] = jnp.zeros((16, width), BF)
            cot_ref[r * pad : r * pad + block] = c_ref[...]
            grad_ref[rows_of(r)] = nt(cot_ref[rows_of(r)], w_ref[...])

    cot_all, grad_inner = call(
        inner_grad_body, [((length, width), BF), ((length, hidden_pad), F32)], *cot_blocks, w_down, name="inner_grad",
        flops=2 * length * width * hidden_pad,
    )

    def expand_body(b0, b1, b2, b3, wg_ref, wu_ref, vec_ref, grad_ref, second_ref, gate_ref, up_ref, stat_ref):
        for r, b_ref in enumerate((b0, b1, b2, b3)):
            rows = rows_of(r)
            second_ref[(r + 1) * pad - 16 : (r + 1) * pad] = jnp.zeros((16, width), BF)
            second_ref[r * pad : r * pad + block] = b_ref[...]
            gate = nn(second_ref[rows], wg_ref[...]) + vec_ref[0:1]
            up = nn(second_ref[rows], wu_ref[...]) + vec_ref[1:2]
            gate_ref[rows] = gate
            up_ref[rows] = up
            activated = gate * jax.nn.sigmoid(gate) * up
            hat = grad_ref[rows] * vec_ref[2:3]
            stat_ref[r] = columns_to_rows(
                [jnp.sum(v, axis=-1, keepdims=True) for v in (activated, activated * activated, hat, hat * activated)]
            )

    second, gate, up, stat_ffn = call(
        expand_body,
        [((length, width), BF), ((length, hidden_pad), F32), ((length, hidden_pad), F32), ((ranks, 8, pad), F32)],
        *second_blocks, w_gate, w_up, ffn_vec, grad_inner, name="expand", mib=40,
        flops=4 * length * width * hidden_pad,
    )
    shared_ffn = tensor_share(stat_ffn)

    def ffn_back_body(
        g_ref, u_ref, grad_ref, s0, s1, s2, s3, vec_ref, wg_ref, wu_ref, dg_ref, du_ref, inner_ref, sum_ref, *part_refs
    ):
        wide = hidden * ranks
        sum_ref[...] = jnp.zeros_like(sum_ref)
        for r in reversed(blocks):
            rows = rows_of(r)
            sums = summed_stats((s0, s1, s2, s3), r)
            mean = sums[0:1] / wide
            inverse = lax.rsqrt(sums[1:2] / wide - mean * mean + EPSILON)
            grad_mean = sums[2:3] / wide
            cross = inverse * (sums[3:4] / wide - mean * grad_mean)
            columns = rows_to_columns(
                jnp.concatenate([mean, inverse, grad_mean, cross, jnp.zeros((4, pad), F32)], axis=0)
            )
            mean, inverse, grad_mean, cross = (columns[:, k : k + 1] for k in range(4))
            gate, up, grad = g_ref[rows], u_ref[rows], grad_ref[rows]
            sigmoid = jax.nn.sigmoid(gate)
            silu = gate * sigmoid
            unit = (silu * up - mean) * inverse
            inner_ref[rows] = (unit * vec_ref[2:3] + vec_ref[3:4]).astype(BF)
            grad_act = inverse * (grad * vec_ref[2:3] - grad_mean - unit * cross)
            d_gate = (grad_act * up * sigmoid * (1.0 + gate - silu)).astype(BF)
            d_up = (grad_act * silu).astype(BF)
            dg_ref[rows] = d_gate
            du_ref[rows] = d_up
            lines = [d_gate.astype(F32), d_up.astype(F32), grad * unit, grad]
            sum_ref[0:4] += jnp.concatenate([jnp.sum(v, axis=0, keepdims=True) for v in lines], axis=0)
            part_refs[r][...] = (nt(d_gate, wg_ref[...]) + nt(d_up, wu_ref[...]))[:block].astype(BF)

    d_gate, d_up, inner, sum_ffn, *parts = call(
        ffn_back_body, [((length, hidden_pad), BF)] * 3 + [((8, hidden_pad), F32)] + [((block, width), BF)] * ranks,
        gate, up, grad_inner, *shared_ffn, ffn_vec, w_gate, w_up, name="ffn_back", mib=44,
        flops=4 * length * width * hidden_pad,
    )
    arrived = tensor_scatter(parts)

    def down_body(i_ref, w_ref, *part_refs):
        for r in reversed(blocks):
            part_refs[r][...] = nn(i_ref[rows_of(r)], w_ref[...])[:block].astype(BF)

    parts = call(
        down_body, [((block, width), BF)] * ranks, inner, w_down, name="down", flops=2 * length * width * hidden_pad
    )
    arrived_out = tensor_scatter(parts)

    def finish_body(h_ref, p0, p1, p2, vec_ref, out_ref):
        out = p0[...].astype(F32) + p1[...].astype(F32) + p2[...].astype(F32)
        out_ref[...] = (h_ref[...] + out + vec_ref[D_BIAS : D_BIAS + 1]).astype(BF)

    (layer_output,) = call(finish_body, [((block, width), BF)], hidden_state, *arrived_out, vec, name="finish")

    def weight_grad(left, right):
        return tn(left, right).astype(BF)

    def dp_scatter(grads):
        if not direct:
            return lax.psum_scatter(grads, "dp", scatter_dimension=0, tiled=True).astype(F32)
        shaped = grads.reshape(count_d // 2, 2, own_rows, -1)
        side, far = me_d % 2, me_d // 2
        across = swap(lax.dynamic_index_in_dim(shaped, 1 - side, 1, False), "dp", 1)
        mine = lax.dynamic_index_in_dim(shaped, side, 1, False)

        def part(k):
            return sum(lax.dynamic_index_in_dim(v, far ^ k, 0, False).astype(F32) for v in (mine, across))

        total = part(0)
        for k in range(1, count_d // 2):
            total = total + swap(part(k).astype(BF), "dp", 2 * k).astype(F32)
        return total

    ffn_grads = jnp.concatenate(
        [weight_grad(cot_all, inner), weight_grad(second, d_gate), weight_grad(second, d_up)], axis=1
    )
    ffn_total = dp_scatter(ffn_grads)

    def hidden_back_body(p0, p1, p2, h_ref, cot_ref, vec_ref, grad_ref, branch_ref, sum_ref):
        grad_second = p0[...].astype(F32) + p1[...].astype(F32) + p2[...].astype(F32)
        mean, inverse = center_scale(h_ref[...])
        unit = (h_ref[...] - mean) * inverse
        cot = cot_ref[...].astype(F32)
        grad = cot + unit_back(grad_second * vec_ref[S_GAIN : S_GAIN + 1], unit, inverse)
        branch = grad.astype(BF)
        grad_ref[...] = grad
        branch_ref[...] = branch
        lines = [grad_second * unit, grad_second, branch.astype(F32), cot]
        lines = [jnp.sum(v, axis=0, keepdims=True) for v in lines]
        sum_ref[...] = jnp.concatenate(lines + [jnp.zeros((4, width), F32)], axis=0)

    grad_hidden, branch_own, sum_two = call(
        hidden_back_body, [((block, width), F32), ((block, width), BF), ((8, width), F32)],
        *arrived, hidden_state, cot_own, vec, name="hidden_back",
    )
    branch_blocks = tensor_gather(branch_own)

    def mix_back_body(index_ref, b0, b1, b2, b3, w_ref, a_ref, norm_ref, vec_ref, branch_ref, grad_ref, stat_ref, sum_ref):
        gain = own(vec_ref, M_GAIN, index_ref)
        sum_ref[...] = jnp.zeros_like(sum_ref)
        for r, b_ref in enumerate((b0, b1, b2, b3)):
            rows = rows_of(r)
            branch_ref[(r + 1) * pad - 16 : (r + 1) * pad] = jnp.zeros((16, width), BF)
            branch_ref[r * pad : r * pad + block] = b_ref[...]
            grad = nt(branch_ref[rows], w_ref[...])
            columns = rows_to_columns(norm_ref[r])
            unit = (a_ref[rows] - columns[:, 0:1]) * columns[:, 1:2]
            hat = grad * gain
            grad_ref[rows] = hat
            stat_ref[r] = columns_to_rows([jnp.sum(v, axis=-1, keepdims=True) for v in (hat, hat * unit)])
            lines = [jnp.sum(v, axis=0, keepdims=True) for v in (grad * unit, grad)]
            sum_ref[0:2] += jnp.concatenate(lines, axis=0)

    branch, hat_mix, stat_back, sum_mix = call(
        mix_back_body,
        [((length, width), BF), ((length, heads), F32), ((ranks, 8, pad), F32), ((8, heads), F32)],
        index, *branch_blocks, w_out, attended, norm_mix, vec, specs=[SM] + [VM] * 8, name="mix_back",
        flops=2 * length * width * heads,
    )
    shared_back = tensor_share(stat_back)

    def attend_back_body(
        q_ref, k_ref, v_ref, a_ref, hat_ref, norm_ref, s0, s1, s2, s3, log_ref, mask_ref, cos_ref, sin_ref,
        d_ref, sum_ref, go_ref, dq_ref, dk_ref, dv_ref,
    ):
        r8 = lax.broadcasted_iota(jnp.int32, (8, heads), 0)
        c8 = lax.broadcasted_iota(jnp.int32, (8, heads), 1)
        pick = (c8 // HD == r8).astype(F32)
        deltas = []
        for r in blocks:
            rows = rows_of(r)
            sums = summed_stats((s0, s1, s2, s3), r)
            columns = rows_to_columns(norm_ref[r])
            back = rows_to_columns(sums / width)
            unit = (a_ref[rows] - columns[:, 0:1]) * columns[:, 1:2]
            grad = (columns[:, 1:2] * (hat_ref[rows] - back[:, 0:1] - unit * back[:, 1:2])).astype(BF)
            go_ref[rows] = grad
            deltas.append(nt(pick, grad.astype(F32) * a_ref[rows], HI))
        delta = jnp.concatenate(deltas, axis=1)
        logs = jnp.concatenate([log_ref[r] for r in blocks], axis=1)
        scale = 1.0 / math.sqrt(HD)
        dq_ref[...] = jnp.zeros_like(dq_ref)
        for h in range(n_heads):
            cols = slice(h // 2 * 128, (h // 2 + 1) * 128)
            half = half_mask(h % 2)
            q, go = q_ref[:, cols], go_ref[:, cols]
            q_half, go_half = jnp.where(half, q, 0).astype(BF), jnp.where(half, go, 0).astype(BF)
            log_line, delta_line = logs[h : h + 1], delta[h : h + 1]

            def step(b, _):
                rows = pl.ds(pl.multiple_of(b * pad, 16), pad)
                k = jnp.where(half, k_ref[rows, cols], 0).astype(BF)
                v = jnp.where(half, v_ref[rows, cols], 0).astype(BF)
                probs = jnp.exp(nt(k, q) * scale - log_line + mask_ref[rows, 0:1])
                grad_scores = (probs * (nt(v, go) - delta_line)).astype(BF)
                dv = nn(probs.astype(BF), go_half)
                dk = nn(grad_scores, q_half) * scale
                if h % 2 == 0:
                    dv_ref[rows, cols] = dv
                    dk_ref[rows, cols] = dk
                else:
                    dv_ref[rows, cols] += dv
                    dk_ref[rows, cols] += dk
                dq_ref[:, cols] += tn(grad_scores, k) * scale
                return 0

            lax.fori_loop(0, ranks, step, 0)
        sum_ref[...] = jnp.zeros_like(sum_ref)
        for r in blocks:
            rows = rows_of(r)
            c, s = cos_ref[rows], -sin_ref[rows]
            for k in range(heads // 128):
                cols = slice(k * 128, (k + 1) * 128)
                dq = turn(dq_ref[rows, cols], c, s).astype(BF)
                dv = dv_ref[rows, cols].astype(BF)
                d_ref[rows, cols] = dq
                d_ref[rows, heads + k * 128 : heads + (k + 1) * 128] = turn(dk_ref[rows, cols], c, s).astype(BF)
                d_ref[rows, 2 * heads + k * 128 : 2 * heads + (k + 1) * 128] = dv
                lines = [jnp.sum(t.astype(F32), axis=0, keepdims=True) for t in (dq, dv)]
                sum_ref[0:2, cols] += jnp.concatenate(lines, axis=0)

    d_qkv, sum_qkv = call(
        attend_back_body, [((length, 3 * heads), BF), ((8, heads), F32)],
        queries, keys, values, attended, hat_mix, norm_mix, *shared_back, stat_mix, mask_column, cosine, sine,
        scratch_shapes=[pltpu.VMEM((length, heads), BF)] + [pltpu.VMEM((length, heads), F32)] * 3, name="attend_back",
        flops=10 * length * length * heads,
    )

    def project_back_body(d_ref, w_ref, x0, x1, x2, x3, sum_ref, *part_refs):
        sum_ref[...] = jnp.zeros_like(sum_ref)
        for r in reversed(blocks):
            x = (x0, x1, x2, x3)[r][...].astype(F32)
            mean, inverse = center_scale(x)
            grad = nt(d_ref[rows_of(r)], w_ref[...])[:block]
            part_refs[r][...] = grad.astype(BF)
            lines = [jnp.sum(v, axis=0, keepdims=True) for v in (grad * ((x - mean) * inverse), grad)]
            sum_ref[0:2] += jnp.concatenate(lines, axis=0)

    sum_one, *parts = call(
        project_back_body, [((8, width), F32)] + [((block, width), BF)] * ranks, d_qkv, w_qkv, *x_blocks,
        name="project_back", flops=6 * length * width * heads,
    )
    arrived = tensor_scatter(parts)

    def input_body(p0, p1, p2, x_ref, grad_ref, vec_ref, out_ref):
        grad_first = p0[...].astype(F32) + p1[...].astype(F32) + p2[...].astype(F32)
        x = x_ref[...].astype(F32)
        mean, inverse = center_scale(x)
        unit = (x - mean) * inverse
        out_ref[...] = grad_ref[...] + unit_back(grad_first * vec_ref[F_GAIN : F_GAIN + 1], unit, inverse)

    (input_grad,) = call(input_body, [((block, width), F32)], *arrived, x_own, grad_hidden, vec, name="input_grad")

    def place_piece(piece):
        return lax.dynamic_update_slice(jnp.zeros((piece.shape[0], width), F32), piece, (0, me_t * heads))

    vectors = jnp.concatenate(
        [sum_one[0:2], place_piece(jnp.concatenate([sum_qkv[0:2], sum_mix[0:2]])), sum_two[0:4], jnp.zeros((6, width), F32)]
    )
    vectors = sum(tensor_share(vectors))
    attn_grads = jnp.concatenate(
        [weight_grad(first, d_qkv), weight_grad(branch, mixed), vectors.T.astype(BF)], axis=1
    )
    attn_total = dp_scatter(attn_grads)
    model = attn_total[:, 4 * heads :].T
    sum_ffn = sum_ffn[0:4]
    if direct:
        k = 1
        while k < count_d:
            sum_ffn = sum_ffn + swap(sum_ffn, "dp", k)
            k *= 2
    else:
        sum_ffn = lax.psum(sum_ffn, "dp")
    ffn = sum_ffn[:, :hidden]
    return (
        layer_output[None], input_grad[None],
        attn_total[:, :heads], attn_total[:, heads : 2 * heads], attn_total[:, 2 * heads : 3 * heads],
        model[2], model[3], model[0], model[1], model[4], model[5],
        attn_total[:, 3 * heads : 4 * heads].T, model[8], model[6], model[7],
        ffn_total[:, hidden_pad : hidden_pad + hidden], ffn_total[:, 2 * hidden_pad : 2 * hidden_pad + hidden],
        ffn[0], ffn[1], ffn[2], ffn[3], ffn_total[:, :hidden].T, model[9],
    )


def solution(mesh):
    rows, across, tokens = P("dp", "tensor"), P("tensor", "dp"), P("dp", "tensor", None)
    model, ffn, image = P("dp"), P("tensor"), P("dp", None)
    in_specs = (
        tokens, rows, rows, rows, model, model, model, model, model, model, across, model, model, model, rows, rows,
        ffn, ffn, ffn, ffn, across, model, tokens, image, image, image,
    )
    out_specs = (
        tokens, tokens, rows, rows, rows, model, model, model, model, model, model, across, model, model, model,
        rows, rows, ffn, ffn, ffn, ffn, across, model,
    )
    return jax.shard_map(local, mesh=mesh, in_specs=in_specs, out_specs=out_specs, check_vma=False)
```

```python
import functools
import math

import jax
import jax.numpy as jnp
from jax import lax
from jax.experimental import pallas as pl
from jax.experimental.pallas import tpu as pltpu
from jax.sharding import PartitionSpec as P

HD = 64
EPSILON = 1e-06
LOW = -1e30
BF = jnp.bfloat16
F32 = jnp.float32
HI = lax.Precision.HIGHEST
VM = pl.BlockSpec(memory_space=pltpu.VMEM)
SM = pl.BlockSpec(memory_space=pltpu.SMEM)
ANY = pl.BlockSpec(memory_space=pl.ANY)
HB = pl.BlockSpec(memory_space=pltpu.HBM)
Q_BIAS, V_BIAS, F_GAIN, F_BIAS, M_GAIN, M_BIAS, O_BIAS, S_GAIN, S_BIAS, D_BIAS = range(10)


def nn(a, b, precision=None):
    return lax.dot_general(a, b, (((1,), (0,)), ((), ())), precision, F32)


def nt(a, b, precision=None):
    return lax.dot_general(a, b, (((1,), (1,)), ((), ())), precision, F32)


def tn(a, b, precision=None):
    return lax.dot_general(a, b, (((0,), (0,)), ((), ())), precision, F32)


def call(
    body, outs, *args, specs=None, load=(), store=(), mib=16, us=1.0, name=None, after=(), scratch=(), **extra
):
    shapes = [jax.ShapeDtypeStruct(shape, dtype) for shape, dtype in outs]
    n_in, n_out, n_after, moved = len(args), len(outs), len(after), len(load) + len(store)
    specs = list(specs or [VM] * n_in)
    out_specs = [VM] * n_out
    for i in load:
        specs[i] = HB
    for i in store:
        out_specs[i] = HB
        shapes[i] = pltpu.HBM(*outs[i])
    args = [pltpu.with_memory_space_constraint(a, pltpu.HBM) if s is HB else a for a, s in zip(args, specs)]
    held = [pltpu.VMEM(args[i].shape, args[i].dtype) for i in load] + [pltpu.VMEM(*outs[i]) for i in store]
    if moved:
        held.append(pltpu.SemaphoreType.DMA((moved,)))

    def run(*refs):
        ins, outs_ = list(refs[:n_in]), list(refs[n_in + n_after : n_in + n_after + n_out])
        rest = refs[n_in + n_after + n_out :]
        own, copies = rest[: len(scratch)], rest[len(scratch) :]
        reads = [pltpu.make_async_copy(ins[i], copies[j], copies[-1].at[j]) for j, i in enumerate(load)]
        for one in reads:
            one.start()
        for j, i in enumerate(load):
            ins[i] = copies[j]
        writes = []
        for j, i in enumerate(store, len(load)):
            writes.append(pltpu.make_async_copy(copies[j], outs_[i], copies[-1].at[j]))
            outs_[i] = copies[j]
        for one in reads:
            one.wait()
        body(*ins, *outs_, *own)
        for one in writes:
            one.start()
        for one in writes:
            one.wait()

    return pl.pallas_call(
        run,
        out_shape=shapes,
        in_specs=specs + [ANY] * n_after,
        out_specs=out_specs,
        scratch_shapes=list(scratch) + held,
        compiler_params=pltpu.CompilerParams(vmem_limit_bytes=mib << 20),
        cost_estimate=pl.CostEstimate(flops=int(us * 1.1e7), bytes_accessed=1 << 10, transcendentals=0),
        name=name,
        **extra,
    )(*args, *after)


def swap(value, axis, offset):
    count = lax.axis_size(axis)
    return lax.ppermute(value, axis, [(i, i ^ offset) for i in range(count)])


def tensor_gather(block):
    core = swap(block, "tensor", 1)
    far = swap(block, "tensor", 2)
    return [block, core, far, swap(far, "tensor", 1)]


def add_pair_body(a_ref, b_ref, out_ref):
    out_ref[...] = (a_ref[...].astype(F32) + b_ref[...].astype(F32)).astype(BF)


def tensor_scatter(parts, after=()):
    third = swap(parts[3], "tensor", 1)
    first = swap(parts[1], "tensor", 1)
    (to_far,) = call(add_pair_body, [(third.shape, BF)], parts[2], third, name="add_pair", after=after)
    return [parts[0], first, swap(to_far, "tensor", 2)], to_far


def tensor_share(value):
    return [value] + [swap(value, "tensor", k) for k in (1, 2, 3)]


def dp_column(block):
    return [block] + [swap(block, "dp", 2 * k) for k in range(1, lax.axis_size("dp") // 2)]


def dp_across(column):
    return [one for mine in column for one in (mine, swap(mine, "dp", 1))]


def tie(value, *others):
    def body(*refs):
        pass

    return pl.pallas_call(
        body,
        out_shape=jax.ShapeDtypeStruct(value.shape, value.dtype),
        in_specs=[ANY] * (1 + len(others)),
        out_specs=ANY,
        input_output_aliases={0: 0},
        cost_estimate=pl.CostEstimate(flops=1, bytes_accessed=1, transcendentals=0),
        name="tie",
    )(value, *others)


def hold(values, *others):
    count = len(values)

    def body(*refs):
        for source, target in zip(refs[:count], refs[count:]):
            target[...] = source[...]

    return call(body, [(v.shape, v.dtype) for v in values], *values, name="hold", after=others)


def center_scale(values):
    width = values.shape[-1]
    mean = jnp.sum(values, axis=-1, keepdims=True) / width
    spread = jnp.sum(values * values, axis=-1, keepdims=True) / width - mean * mean
    return mean, lax.rsqrt(spread + EPSILON)


def unit_back(grad_hat, unit, inverse):
    width = unit.shape[-1]
    mean = jnp.sum(grad_hat, axis=-1, keepdims=True) / width
    cross = jnp.sum(grad_hat * unit, axis=-1, keepdims=True) / width
    return inverse * (grad_hat - mean - unit * cross)


def columns_to_rows(columns):
    count = columns[0].shape[0]
    lanes = lax.broadcasted_iota(jnp.int32, (count, 128), 1)
    wide = jnp.zeros((count, 128), F32)
    for k, column in enumerate(columns):
        wide = jnp.where(lanes == k, column, wide)
    return wide.T[0:8]


def rows_to_columns(rows):
    return rows.T


def summed_stats(refs, r):
    return refs[0][r] + refs[1][r ^ 1] + refs[2][r ^ 2] + refs[3][r ^ 3]


def turn(values, cosine, sine):
    lanes = lax.broadcasted_iota(jnp.int32, values.shape, 1)
    other = jnp.where(lanes % 2 == 0, pltpu.roll(values, 127, 1), pltpu.roll(values, 1, 1))
    return values * cosine + other * sine


def half_mask(s):
    lane = lax.broadcasted_iota(jnp.int32, (1, 128), 1)
    return lane < HD if s == 0 else lane >= HD


def local(
    layer_input, query_weight, key_weight, value_weight, query_bias, value_bias, first_gain, first_bias,
    mixer_gain, mixer_bias, output_weight, output_bias, second_gain, second_bias, gate_weight, up_weight,
    gate_bias, up_bias, inner_gain, inner_bias, down_weight, down_bias, cotangent, key_valid, patch_row, patch_column,
):
    ranks = lax.axis_size("tensor")
    me_t, me_d, count_d = lax.axis_index("tensor"), lax.axis_index("dp"), lax.axis_size("dp")
    block, width = layer_input.shape[1:]
    pad = -(-block // 16) * 16
    length = ranks * pad
    heads = query_weight.shape[1]
    hidden = gate_weight.shape[1]
    hidden_pad = -(-hidden // 128) * 128
    own_rows = width // count_d
    direct = own_rows % 128 == 0 and count_d & (count_d - 1) == 0
    index = jnp.stack([me_d, me_t]).astype(jnp.int32)
    x_own, cot_own = layer_input[0], cotangent[0]
    blocks = range(ranks)

    def rows_of(r):
        return slice(r * pad, (r + 1) * pad)

    lines = jnp.stack([key_valid[0], patch_row[0], patch_column[0], jnp.arange(ranks * block, dtype=jnp.int32)])
    lines = jnp.pad(lines.reshape(4, ranks, block), ((0, 4), (0, 0), (0, pad - block))).astype(F32)
    lines = jnp.stack([lax.dynamic_index_in_dim(lines, me_t ^ r, 1, False) for r in blocks])
    lane = jnp.arange(128)
    frequency = jnp.power(F32(10000.0), -((lane % HD) // 2 % (HD // 4)).astype(F32) / (HD // 4))
    frequency = jnp.broadcast_to(frequency[None, :], (8, 128))

    def table_body(line_ref, frequency_ref, cos_ref, sin_ref):
        lanes = lax.broadcasted_iota(jnp.int32, (pad, 128), 1)
        for r in blocks:
            columns = rows_to_columns(line_ref[r])
            position = jnp.where(lanes % HD < HD // 2, columns[:, 1:2], columns[:, 2:3])
            angle = jnp.where(columns[:, 3:4] > 0.0, 0.5 * (position * frequency_ref[0:1]), 0.0)
            cos_ref[rows_of(r)] = jnp.cos(angle)
            sine = jnp.sin(angle)
            sin_ref[rows_of(r)] = jnp.where(lanes % 2 == 0, -sine, sine)

    cosine, sine = call(table_body, [((length, 128), F32)] * 2, lines, frequency, name="tables", us=4)

    small = [
        v[None, :]
        for v in (
            query_bias, value_bias, first_gain, first_bias, mixer_gain, mixer_bias, output_bias, second_gain,
            second_bias, down_bias,
        )
    ]
    tiles = heads // 128
    hidden_low = -(-hidden // 16) * 16
    starts = [(k % 3) * tiles + k // 3 for k in range(3 * tiles)]
    if direct:
        o_start = 3 * tiles * own_rows + 16

        def pack_a_body(q_ref, k_ref, v_ref, w_ref, *refs):
            *small_refs, out_ref = refs
            out_ref[o_start:] = w_ref[...]
            for k in range(3 * tiles):
                ref = (q_ref, k_ref, v_ref)[k % 3]
                out_ref[k * own_rows : (k + 1) * own_rows] = ref[:, k // 3 * 128 : (k // 3 + 1) * 128]
            lines = [ref[...].astype(F32) for ref in small_refs]
            lines.append(jnp.zeros((16 - len(lines), own_rows), F32))
            out_ref[3 * tiles * own_rows : o_start] = jnp.concatenate(lines, axis=0).astype(BF)

        (pack_a,) = call(
            pack_a_body, [((o_start + heads, 128), BF)], query_weight, key_weight, value_weight, output_weight,
            *small, name="pack_a", load=tuple(range(14)),
        )
        column_a = dp_column(pack_a)
        across_a = [swap(pack_a, "dp", 1)]
        x_far = swap(x_own, "tensor", 2)
        *tied, first_across, x_far = hold([*column_a[1:], *across_a, x_far], cosine)
        column_a[1:], across_a[:] = tied, [first_across]
        across_a += [swap(one, "dp", 1) for one in column_a[1:]]
        x_blocks = [x_own, swap(x_own, "tensor", 1), x_far, swap(x_far, "tensor", 1)]
        got_a = [one for pair in zip(column_a, across_a) for one in pair]

        def pack_f_body(g_ref, u_ref, d_ref, out_ref):
            for j, ref in enumerate((g_ref, u_ref, d_ref)):
                out_ref[(j + 1) * hidden_low - 16 : (j + 1) * hidden_low] = jnp.zeros((16, own_rows), BF)
                out_ref[j * hidden_low : j * hidden_low + hidden] = ref[...]

        (pack_f,) = call(
            pack_f_body, [((3 * hidden_low, own_rows), BF)], gate_weight.T, up_weight.T, down_weight, name="pack_f",
            load=(0, 1, 2),
        )
        got_f = lax.all_gather(tie(pack_f, column_a[1]), "dp")
        def copies(pairs, sems):
            started = [pltpu.make_async_copy(a, b, sems.at[i]) for i, (a, b) in enumerate(pairs)]
            for one in started:
                one.start()
            for one in started:
                one.wait()

        def chunk_at(index_ref, r):
            return pl.ds(pl.multiple_of((index_ref[0] ^ r) * own_rows, 128), own_rows)

        def assemble_a(index_ref, *refs):
            chunks, (w_ref, v_ref, o_ref, small_ref, sems) = refs[:-5], refs[-5:]
            pairs = []
            for r, chunk in enumerate(chunks):
                for k in range(3 * tiles):
                    pairs.append((
                        chunk.at[k * own_rows : (k + 1) * own_rows],
                        w_ref.at[chunk_at(index_ref, r), k * 128 : (k + 1) * 128],
                    ))
                pairs.append((chunk.at[3 * tiles * own_rows : o_start], small_ref.at[r]))
                pairs.append((chunk.at[o_start:], o_ref.at[:, chunk_at(index_ref, r)]))
            copies(pairs, sems)
            for r in range(count_d):
                v_ref[:, chunk_at(index_ref, r)] = small_ref[r].astype(F32)

        def assemble_f(chunks, g_ref, u_ref, d_ref, sems):
            pairs = []
            for a in range(count_d):
                for j, out in enumerate((g_ref, u_ref, d_ref)):
                    pairs.append((
                        chunks.at[a, j * hidden_low : (j + 1) * hidden_low],
                        out.at[0:hidden_low, a * own_rows : (a + 1) * own_rows],
                    ))
            for out in (g_ref, u_ref, d_ref):
                out[hidden_low:] = jnp.zeros((hidden_pad - hidden_low, width), BF)
            copies(pairs, sems)

        specs = [SM] + [VM, ANY] * (count_d // 2)

        def dma(count):
            return pltpu.SemaphoreType.DMA((count,))

        w_qkv, vec, w_out = call(
            assemble_a, [((width, 3 * heads), BF), ((16, width), F32), ((heads, width), BF)], index, *got_a, specs=specs, name="assemble_a",
            scratch=[pltpu.VMEM((count_d, 16, 128), BF), dma(count_d * (3 * tiles + 2))],
        )
    else:
        def whole(weight, axis):
            return lax.all_gather(weight, "dp", axis=axis, tiled=True)

        x_blocks = tensor_gather(x_own)
        cot_blocks = tensor_gather(cot_own)
        w_qkv = whole(jnp.concatenate(
            [(query_weight, key_weight, value_weight)[k % 3][:, k // 3 * 128 : (k // 3 + 1) * 128] for k in range(3 * tiles)],
            axis=1,
        ), 0)
        vec = jnp.pad(whole(jnp.concatenate(small), 1).astype(F32), ((0, 6), (0, 0)))
        w_out = whole(output_weight, 1)
        w_gate, w_up, w_down = (
            jnp.pad(whole(w, 1), ((0, hidden_pad - hidden), (0, 0))) for w in (gate_weight.T, up_weight.T, down_weight)
        )
    ffn_vec = jnp.pad(
        jnp.stack([gate_bias, up_bias, inner_gain, inner_bias]).astype(F32), ((0, 4), (0, hidden_pad - hidden))
    )

    def own(ref, k, index_ref):
        return ref[k : k + 1, pl.ds(pl.multiple_of(index_ref[1] * heads, 128), heads)]

    def project_body(index_ref, x0, x1, x2, x3, w_ref, vec_ref, cos_ref, sin_ref, first_ref, q_ref, k_ref, v_ref):
        gain, bias = vec_ref[F_GAIN : F_GAIN + 1], vec_ref[F_BIAS : F_BIAS + 1]
        q_bias, v_bias = own(vec_ref, Q_BIAS, index_ref), own(vec_ref, V_BIAS, index_ref)
        for r, x_ref in enumerate((x0, x1, x2, x3)):
            x = x_ref[...].astype(F32)
            mean, inverse = center_scale(x)
            first_ref[(r + 1) * pad - 16 : (r + 1) * pad] = jnp.zeros((16, width), BF)
            first_ref[r * pad : r * pad + block] = ((x - mean) * inverse * gain + bias).astype(BF)
            rows = rows_of(r)
            qkv = nn(first_ref[rows], w_ref[...])
            c, s = cos_ref[rows], sin_ref[rows]
            for k in range(tiles):
                cols = slice(k * 128, (k + 1) * 128)
                q, key, v = (qkv[:, (3 * k + j) * 128 : (3 * k + j + 1) * 128] for j in range(3))
                q_ref[rows, cols] = turn(q + q_bias[:, cols], c, s).astype(BF)
                k_ref[rows, cols] = turn(key, c, s).astype(BF)
                v_ref[rows, cols] = (v + v_bias[:, cols]).astype(BF)

    first, queries, keys, values = call(
        project_body, [((length, width), BF)] + [((length, heads), BF)] * 3,
        index, *x_blocks, w_qkv, vec, cosine, sine, specs=[SM] + [VM] * 8, name="project", us=4,
        store=(0, 1, 2, 3),
    )
    if direct:
        (cot_tied,) = hold([cot_own], values)
        cot_blocks = tensor_gather(cot_tied)
        w_gate, w_up, w_down = call(
            assemble_f, [((hidden_pad, width), BF)] * 3, got_f, specs=[HB], name="assemble_f",
            scratch=[dma(3 * count_d)],
        )

    def attend_body(q_ref, k_ref, v_ref, mask_ref, o_ref, stat_ref):
        mask_line = jnp.concatenate([jnp.where(mask_ref[r][0:1] == 1.0, 0.0, LOW) for r in blocks], axis=1)
        k_half, v_half = [], []
        for h in range(heads // HD):
            cols = slice(h // 2 * 128, (h // 2 + 1) * 128)
            k_half.append(jnp.where(half_mask(h % 2), k_ref[:, cols], 0).astype(BF))
            v_half.append(jnp.where(half_mask(h % 2), v_ref[:, cols], 0).astype(BF))

        def step(b, _):
            rows = pl.ds(pl.multiple_of(b * pad, 16), pad)
            kept = []
            total = jnp.zeros((pad, 1), F32)
            square = jnp.zeros((pad, 1), F32)
            for pair in range(heads // 128):
                cols = slice(pair * 128, (pair + 1) * 128)
                q = q_ref[rows, cols]
                out = jnp.zeros((pad, 128), F32)
                for s in range(2):
                    h = 2 * pair + s
                    scores = nt(q, k_half[h]) * (1.0 / math.sqrt(HD)) + mask_line
                    top = jnp.max(scores, axis=-1, keepdims=True)
                    terms = jnp.exp(scores - top)
                    below = jnp.sum(terms, axis=-1, keepdims=True)
                    out += nn(terms.astype(BF), v_half[h]) * (1.0 / below)
                    kept.append(top + jnp.log(below))
                o_ref[rows, cols] = out
                total += jnp.sum(out, axis=-1, keepdims=True)
                square += jnp.sum(out * out, axis=-1, keepdims=True)
            stat_ref[b] = columns_to_rows(kept + [total, square])
            return 0

        lax.fori_loop(0, ranks, step, 0)

    n_heads = heads // HD
    attended, stat_mix = call(
        attend_body, [((length, heads), F32), ((ranks, 8, pad), F32)], queries, keys, values, lines, name="attend", us=10,
        load=(0, 1, 2),
    )
    shared_mix = tensor_share(stat_mix)

    def mix_body(index_ref, a_ref, s0, s1, s2, s3, w_ref, vec_ref, mixed_ref, norm_ref, *part_refs):
        gain, bias = own(vec_ref, M_GAIN, index_ref), own(vec_ref, M_BIAS, index_ref)
        for r in reversed(blocks):
            rows = rows_of(r)
            sums = summed_stats((s0, s1, s2, s3), r)
            mean = sums[n_heads : n_heads + 1] / width
            inverse = lax.rsqrt(sums[n_heads + 1 : n_heads + 2] / width - mean * mean + EPSILON)
            lines = jnp.concatenate([mean, inverse, jnp.zeros((6, pad), F32)], axis=0)
            norm_ref[r] = lines
            columns = rows_to_columns(lines)
            mixed = ((a_ref[rows] - columns[:, 0:1]) * columns[:, 1:2] * gain + bias).astype(BF)
            mixed_ref[rows] = mixed
            part_refs[r][...] = nn(mixed, w_ref[...])[:block].astype(BF)

    mixed, norm_mix, *parts = call(
        mix_body, [((length, heads), BF), ((ranks, 8, pad), F32)] + [((block, width), BF)] * ranks,
        index, attended, *shared_mix, w_out, vec, specs=[SM] + [VM] * 7, name="mix", us=2.5,
        store=(0,), after=[cot_blocks[2]],
    )
    arrived, _ = tensor_scatter(parts)

    def second_body(x_ref, p0, p1, p2, vec_ref, hidden_ref, second_ref):
        out = p0[...].astype(F32) + p1[...].astype(F32) + p2[...].astype(F32)
        state = x_ref[...].astype(F32) + out + vec_ref[O_BIAS : O_BIAS + 1]
        hidden_ref[...] = state
        mean, inverse = center_scale(state)
        unit = (state - mean) * inverse
        second_ref[...] = (unit * vec_ref[S_GAIN : S_GAIN + 1] + vec_ref[S_BIAS : S_BIAS + 1]).astype(BF)

    hidden_state, second_own = call(
        second_body, [((block, width), F32), ((block, width), BF)], x_own, *arrived, vec, name="second"
    )
    half = 2 * pad

    def half_rows(r):
        return slice(r % 2 * pad, (r % 2 + 1) * pad)

    def pad_block(ref, r, value):
        start = r * pad
        ref[start + pad - 16 : start + pad] = jnp.zeros((16, width), BF)
        ref[start : start + block] = value

    def inner_grad_body(c0, c1, w_ref, cot_ref, grad_ref):
        for r, c_ref in enumerate((c0, c1)):
            pad_block(cot_ref, r, c_ref[...])
            grad_ref[half_rows(r)] = nt(cot_ref[half_rows(r)], w_ref[...])

    cot_halves, grad_inner = zip(*(
        call(
            inner_grad_body, [((half, width), BF), ((half, hidden_pad), F32)], *pair, w_down, name="inner_grad", us=2
        )
        for pair in (cot_blocks[:2], cot_blocks[2:])
    ))

    def expand_body(b0, b1, wg_ref, wu_ref, vec_ref, grad_ref, *refs):
        second_ref, gate_ref, up_ref, stat_ref = refs[-4:]
        base = 0
        if len(refs) == 5:
            base = 2
            stat_ref[0:2] = refs[0][...]
        for r, b_ref in enumerate((b0, b1)):
            rows = half_rows(r)
            pad_block(second_ref, r, b_ref[...])
            gate = nt(second_ref[rows], wg_ref[...]) + vec_ref[0:1]
            up = nt(second_ref[rows], wu_ref[...]) + vec_ref[1:2]
            gate_ref[rows] = gate
            up_ref[rows] = up
            activated = gate * jax.nn.sigmoid(gate) * up
            hat = grad_ref[rows] * vec_ref[2:3]
            stat_ref[base + r] = columns_to_rows(
                [jnp.sum(v, axis=-1, keepdims=True) for v in (activated, activated * activated, hat, hat * activated)]
            )

    second_far = swap(second_own, "tensor", 2)
    second_blocks = [second_own, swap(second_own, "tensor", 1), second_far]
    (second_far,) = hold([second_far], *grad_inner)
    second_blocks = [*second_blocks[:2], second_far, swap(second_far, "tensor", 1)]
    expanded = []
    for j in range(2):
        before = [expanded[0][3]] if j else []
        expanded.append(call(
            expand_body,
            [((half, width), BF), ((half, hidden_pad), F32), ((half, hidden_pad), F32), ((2 + 2 * j, 8, pad), F32)],
            *second_blocks[2 * j : 2 * j + 2], w_gate, w_up, ffn_vec, grad_inner[j], *before, name="expand", us=3.7,
        ))
    shared_ffn = tensor_share(expanded[1][3])

    def ffn_back_body(
        first_block, g_ref, u_ref, grad_ref, s0, s1, s2, s3, vec_ref, wg_ref, wu_ref, *refs
    ):
        dg_ref, du_ref, inner_ref, sum_ref, *part_refs = refs[-6:]
        wide = hidden * ranks
        sum_ref[...] = refs[0][...] if len(refs) == 7 else jnp.zeros_like(sum_ref)
        for r in (1, 0):
            rows = half_rows(r)
            sums = summed_stats((s0, s1, s2, s3), first_block + r)
            mean = sums[0:1] / wide
            inverse = lax.rsqrt(sums[1:2] / wide - mean * mean + EPSILON)
            grad_mean = sums[2:3] / wide
            cross = inverse * (sums[3:4] / wide - mean * grad_mean)
            columns = rows_to_columns(
                jnp.concatenate([mean, inverse, grad_mean, cross, jnp.zeros((4, pad), F32)], axis=0)
            )
            mean, inverse, grad_mean, cross = (columns[:, k : k + 1] for k in range(4))
            gate, up, grad = g_ref[rows], u_ref[rows], grad_ref[rows]
            sigmoid = jax.nn.sigmoid(gate)
            silu = gate * sigmoid
            unit = (silu * up - mean) * inverse
            inner_ref[rows] = (unit * vec_ref[2:3] + vec_ref[3:4]).astype(BF)
            grad_act = inverse * (grad * vec_ref[2:3] - grad_mean - unit * cross)
            d_gate = (grad_act * up * sigmoid * (1.0 + gate - silu)).astype(BF)
            d_up = (grad_act * silu).astype(BF)
            dg_ref[rows] = d_gate
            du_ref[rows] = d_up
            totals = [d_gate.astype(F32), d_up.astype(F32), grad * unit, grad]
            sum_ref[0:4] += jnp.concatenate([jnp.sum(v, axis=0, keepdims=True) for v in totals], axis=0)
            part_refs[r][...] = (nn(d_gate, wg_ref[...]) + nn(d_up, wu_ref[...]))[:block].astype(BF)

    backed = [None, None]
    for j in (1, 0):
        before = [backed[1][3]] if j == 0 else []
        backed[j] = call(
            functools.partial(ffn_back_body, 2 * j),
            [((half, hidden_pad), BF)] * 3 + [((8, hidden_pad), F32)] + [((block, width), BF)] * 2,
            *expanded[j][1:3], grad_inner[j], *shared_ffn, ffn_vec, w_gate, w_up, *before, name="ffn_back", us=5.5,
        )
    sum_ffn = backed[0][3]
    arrived, to_far = tensor_scatter([*backed[0][4:], *backed[1][4:]])

    def dp_sum_step(total, k):
        return total + swap(total, "dp", k)


    if direct:
        rows_f = 3 * hidden_low

        def ffn_grad_body(g0, g1, u0, u1, i0, i1, e0, e1, c0, c1, out_ref):
            for j, (rights, lefts) in enumerate((((g0, g1), (e0, e1)), ((u0, u1), (e0, e1)), ((i0, i1), (c0, c1)))):
                for at in range(0, hidden_low, 256):
                    stop = min(at + 256, hidden_low)
                    cols = slice(at, min(at + 256, hidden_pad))
                    total = sum(tn(a[:, cols], b[...]) for a, b in zip(rights, lefts)).astype(BF)
                    for d in range(count_d):
                        base = d * rows_f + j * hidden_low
                        out_ref[base + at : base + stop] = total[: stop - at, d * own_rows : (d + 1) * own_rows]

        (ffn_grads,) = call(
            ffn_grad_body, [((count_d * rows_f, own_rows), BF)], *(backed[j][k] for k in (0, 1, 2) for j in range(2)),
            expanded[0][0], expanded[1][0], *cot_halves, name="ffn_grad", us=8, store=(0,),
            after=[to_far],
        )
        ffn_grads = tie(ffn_grads, arrived[2])
        got_ffn = lax.psum_scatter(ffn_grads, "dp", scatter_dimension=0, tiled=True)

        def ffn_finish_body(p_ref, *out_refs):
            for j, ref in enumerate(out_refs):
                ref[...] = p_ref[j * hidden_low : j * hidden_low + hidden].astype(F32)

        gate_grad, up_grad, down_grad = call(
            ffn_finish_body, [((hidden, own_rows), F32)] * 3, got_ffn, store=(0, 1, 2), load=(0,), name="ffn_finish",
        )
        gate_grad, up_grad = gate_grad.T, up_grad.T
    else:
        def plain_grad(left, right):
            return lax.psum_scatter(tn(left, right).astype(BF), "dp", scatter_dimension=0, tiled=True).astype(F32)

        def joined(pair):
            return jnp.concatenate(pair)

        second_all = joined([expanded[j][0] for j in range(2)])
        down_grad = plain_grad(joined(cot_halves), joined([backed[j][2] for j in range(2)]))[:, :hidden].T
        gate_grad = plain_grad(second_all, joined([backed[j][0] for j in range(2)]))[:, :hidden]
        up_grad = plain_grad(second_all, joined([backed[j][1] for j in range(2)]))[:, :hidden]

    def hidden_back_body(p0, p1, p2, h_ref, cot_ref, vec_ref, grad_ref, branch_ref, sum_ref):
        grad_second = p0[...].astype(F32) + p1[...].astype(F32) + p2[...].astype(F32)
        mean, inverse = center_scale(h_ref[...])
        unit = (h_ref[...] - mean) * inverse
        cot = cot_ref[...].astype(F32)
        grad = cot + unit_back(grad_second * vec_ref[S_GAIN : S_GAIN + 1], unit, inverse)
        branch = grad.astype(BF)
        grad_ref[...] = grad
        branch_ref[...] = branch
        lines = [grad_second * unit, grad_second, branch.astype(F32), cot]
        lines = [jnp.sum(v, axis=0, keepdims=True) for v in lines]
        sum_ref[...] = jnp.concatenate(lines + [jnp.zeros((4, width), F32)], axis=0)

    grad_hidden, branch_own, sum_two = call(
        hidden_back_body, [((block, width), F32), ((block, width), BF), ((8, width), F32)],
        *arrived, hidden_state, cot_own, vec, name="hidden_back", after=[ffn_grads] if direct else [],
        store=(0,),
    )
    branch_blocks = tensor_gather(branch_own)
    if direct:
        sum_ffn = dp_sum_step(sum_ffn, 1)

    def down_body(i0, i1, w_ref, *part_refs):
        for r in reversed(blocks):
            part_refs[r][...] = nn((i0, i1)[r // 2][half_rows(r)], w_ref[...])[:block].astype(BF)

    parts = call(
        down_body, [((block, width), BF)] * ranks, backed[0][2], backed[1][2], w_down, name="down", us=2.5,
    )
    down_parts = parts

    def mix_back_body(index_ref, b0, b1, b2, b3, w_ref, a_ref, norm_ref, vec_ref, branch_ref, grad_ref, stat_ref, sum_ref):
        gain = own(vec_ref, M_GAIN, index_ref)
        sum_ref[...] = jnp.zeros_like(sum_ref)
        for r, b_ref in enumerate((b0, b1, b2, b3)):
            rows = rows_of(r)
            branch_ref[(r + 1) * pad - 16 : (r + 1) * pad] = jnp.zeros((16, width), BF)
            branch_ref[r * pad : r * pad + block] = b_ref[...]
            grad = nt(branch_ref[rows], w_ref[...])
            columns = rows_to_columns(norm_ref[r])
            unit = (a_ref[rows] - columns[:, 0:1]) * columns[:, 1:2]
            hat = grad * gain
            grad_ref[rows] = hat
            stat_ref[r] = columns_to_rows([jnp.sum(v, axis=-1, keepdims=True) for v in (hat, hat * unit)])
            lines = [jnp.sum(v, axis=0, keepdims=True) for v in (grad * unit, grad)]
            sum_ref[0:2] += jnp.concatenate(lines, axis=0)

    branch, hat_mix, stat_back, sum_mix = call(
        mix_back_body,
        [((length, width), BF), ((length, heads), F32), ((ranks, 8, pad), F32), ((8, heads), F32)],
        index, *branch_blocks, w_out, attended, norm_mix, vec, specs=[SM] + [VM] * 8, name="mix_back", us=3,
        after=down_parts, store=(0,),
    )

    shared_back = tensor_share(stat_back)
    arrived_out, _ = tensor_scatter(down_parts, after=shared_back[1:])

    def finish_body(h_ref, p0, p1, p2, vec_ref, out_ref):
        out = p0[...].astype(F32) + p1[...].astype(F32) + p2[...].astype(F32)
        out_ref[...] = (h_ref[...] + out + vec_ref[D_BIAS : D_BIAS + 1]).astype(BF)

    (layer_output,) = call(finish_body, [((block, width), BF)], hidden_state, *arrived_out, vec, name="finish")


    def attend_back_body(
        pair, q_ref, k_ref, v_ref, a_ref, hat_ref, norm_ref, s0, s1, s2, s3, log_ref, line_ref, cos_ref, sin_ref,
        d_ref, sum_ref, go_ref, dq_ref, dk_ref, dv_ref, mask_ref,
    ):
        cols = slice(pair * 128, (pair + 1) * 128)
        r8 = lax.broadcasted_iota(jnp.int32, (8, 128), 0)
        c8 = lax.broadcasted_iota(jnp.int32, (8, 128), 1)
        pick = (c8 // HD == r8).astype(F32)
        deltas = []
        for r in blocks:
            rows = rows_of(r)
            sums = summed_stats((s0, s1, s2, s3), r)
            columns = rows_to_columns(norm_ref[r])
            back = rows_to_columns(sums / width)
            unit = (a_ref[rows, cols] - columns[:, 0:1]) * columns[:, 1:2]
            grad = (columns[:, 1:2] * (hat_ref[rows, cols] - back[:, 0:1] - unit * back[:, 1:2])).astype(BF)
            go_ref[rows] = grad
            valid = rows_to_columns(line_ref[r])[:, 0:1]
            mask_ref[rows] = jnp.broadcast_to(jnp.where(valid == 1.0, 0.0, LOW), (pad, 128))
            deltas.append(nt(pick, grad.astype(F32) * a_ref[rows, cols], HI))
        delta = jnp.concatenate(deltas, axis=1)
        logs = jnp.concatenate([log_ref[r] for r in blocks], axis=1)
        scale = 1.0 / math.sqrt(HD)
        dq_ref[...] = jnp.zeros_like(dq_ref)
        q, go = q_ref[:, cols], go_ref[...]
        for s in range(2):
            half_of = half_mask(s)
            q_half, go_half = jnp.where(half_of, q, 0).astype(BF), jnp.where(half_of, go, 0).astype(BF)
            h = 2 * pair + s
            log_line, delta_line = logs[h : h + 1], delta[s : s + 1]

            def step(b, _):
                rows = pl.ds(pl.multiple_of(b * pad, 16), pad)
                k = jnp.where(half_of, k_ref[rows, cols], 0).astype(BF)
                v = jnp.where(half_of, v_ref[rows, cols], 0).astype(BF)
                probs = jnp.exp(nt(k, q) * scale - log_line + mask_ref[rows, 0:1])
                grad_scores = (probs * (nt(v, go) - delta_line)).astype(BF)
                dv = nn(probs.astype(BF), go_half)
                dk = nn(grad_scores, q_half) * scale
                if s == 0:
                    dv_ref[rows] = dv
                    dk_ref[rows] = dk
                else:
                    dv_ref[rows] += dv
                    dk_ref[rows] += dk
                dq_ref[...] += tn(grad_scores, k) * scale
                return 0

            lax.fori_loop(0, ranks, step, 0)
        sum_ref[...] = jnp.zeros_like(sum_ref)
        for r in blocks:
            rows = rows_of(r)
            c, s = cos_ref[rows], -sin_ref[rows]
            dq = turn(dq_ref[rows], c, s).astype(BF)
            dv = dv_ref[rows].astype(BF)
            d_ref[rows, 0:128] = dq
            d_ref[rows, 128:256] = turn(dk_ref[rows], c, s).astype(BF)
            d_ref[rows, 256:384] = dv
            totals = [jnp.sum(t.astype(F32), axis=0, keepdims=True) for t in (dq, dv)]
            sum_ref[0:2] += jnp.concatenate(totals, axis=0)

    def attend_back(pair, after):
        return call(
            functools.partial(attend_back_body, pair), [((length, 384), BF), ((8, 128), F32)],
            queries, keys, values, attended, hat_mix, norm_mix, *shared_back, stat_mix, lines, cosine, sine,
            scratch=[pltpu.VMEM((length, 128), BF)] + [pltpu.VMEM((length, 128), F32)] * 4, name="attend_back", us=11,
            after=after,
        )

    zs = count_d // 2

    def weight_grad(index_ref, left, rights, keep_ref, send_ref, at):
        odd = index_ref[0] % 2
        for k in range(zs):
            cols = pl.ds(pl.multiple_of(((index_ref[0] // 2) ^ k) * 2 * own_rows, 128), 2 * own_rows)
            turned = left[:, cols].T
            start = at
            for right in rights:
                both = nn(turned, right[...])
                upper, lower = both[:own_rows].astype(BF), both[own_rows:].astype(BF)
                stop = start + both.shape[1]
                keep_ref[k, :own_rows, start:stop] = jnp.where(odd == 0, upper, lower)
                send_ref[k, :own_rows, start:stop] = jnp.where(odd == 0, lower, upper)
                start = stop

    def add_body(keep_ref, across_ref, own_ref, *send_refs):
        own_ref[...] = keep_ref[0].astype(F32) + across_ref[0].astype(F32)
        for k, ref in enumerate(send_refs):
            ref[...] = (keep_ref[k + 1].astype(F32) + across_ref[k + 1].astype(F32)).astype(BF)

    def dp_reduce(keep, send, name, after=()):
        across = swap(send, "dp", 1)
        mine, *sends = call(
            add_body, [(keep.shape[1:], F32)] + [(keep.shape[1:], BF)] * (zs - 1), keep, across, name=name, us=1,
            after=after,
        )
        return [mine] + [swap(one, "dp", 2 * (k + 1)) for k, one in enumerate(sends)]

    d_first, sum_first = attend_back(0, [])
    if direct:
        def first_grad_body(index_ref, f_ref, d_ref, b_ref, m_ref, keep_ref, send_ref):
            weight_grad(index_ref, f_ref, [d_ref], keep_ref, send_ref, 0)
            weight_grad(index_ref, b_ref, [m_ref], keep_ref, send_ref, 384)

        sum_ffn = dp_sum_step(sum_ffn, 2)
        keep_first, send_first = call(
            first_grad_body, [((zs, own_rows, 384 + heads), BF)] * 2, index, first, d_first, branch, mixed,
            specs=[SM] + [VM] * 4, name="first_grad", us=3,
            after=[sum_ffn],
        )
    d_last, sum_last = attend_back(1, [send_first] if direct else [])
    if direct:
        sum_ffn = dp_sum_step(sum_ffn, 4)
        got_first = dp_reduce(keep_first, send_first, "first_add", after=[d_last])

    def project_back_body(first_block, d0_ref, d1_ref, w_ref, x0, x1, *refs):
        sum_ref, *part_refs = refs[-3:]
        sum_ref[...] = refs[0][...] if len(refs) == 4 else jnp.zeros_like(sum_ref)
        for r in (1, 0):
            x = (x0, x1)[r][...].astype(F32)
            mean, inverse = center_scale(x)
            rows = rows_of(first_block + r)
            grad = (nt(d0_ref[rows], w_ref[:, :384]) + nt(d1_ref[rows], w_ref[:, 384:]))[:block]
            part_refs[r][...] = grad.astype(BF)
            totals = [jnp.sum(v, axis=0, keepdims=True) for v in (grad * ((x - mean) * inverse), grad)]
            sum_ref[0:2] += jnp.concatenate(totals, axis=0)

    projected = [None, None]
    for j in (1, 0):
        before = [projected[1][0]] if j == 0 else []
        projected[j] = call(
            functools.partial(project_back_body, 2 * j), [((8, width), F32)] + [((block, width), BF)] * 2,
            d_first, d_last, w_qkv, *x_blocks[2 * j : 2 * j + 2], *before, name="project_back", us=2,
            after=[layer_output] if j else [],
        )
    sum_one = projected[0][0]
    arrived, _ = tensor_scatter([*projected[0][1:], *projected[1][1:]])

    def input_body(p0, p1, p2, x_ref, grad_ref, vec_ref, out_ref):
        grad_first = p0[...].astype(F32) + p1[...].astype(F32) + p2[...].astype(F32)
        x = x_ref[...].astype(F32)
        mean, inverse = center_scale(x)
        unit = (x - mean) * inverse
        out_ref[:, 0, :] = grad_ref[...] + unit_back(grad_first * vec_ref[F_GAIN : F_GAIN + 1], unit, inverse)

    (input_grad,) = call(
        input_body, [((block, 1, width), F32)], *arrived, x_own, grad_hidden, vec, name="input_grad", store=(0,),
    )

    def vector_body(index_ref, one_ref, first_ref, last_ref, mix_ref, two_ref, out_ref):
        out_ref[...] = jnp.zeros_like(out_ref)
        out_ref[0:2] = one_ref[0:2]
        cols = pl.ds(pl.multiple_of(index_ref[1] * heads, 128), heads)
        out_ref[2:4, cols] = jnp.concatenate([first_ref[0:2], last_ref[0:2]], axis=1)
        out_ref[4:6, cols] = mix_ref[0:2]
        out_ref[6:10] = two_ref[0:4]

    (vectors,) = call(
        vector_body, [((16, width), F32)], index, sum_one, sum_first, sum_last, sum_mix, sum_two, specs=[SM] + [VM] * 5,
        name="vectors",
    )
    shared_vectors = tensor_share(vectors)
    if direct:
        def last_grad_body(index_ref, f_ref, d_ref, v0, v1, v2, v3, keep_ref, send_ref):
            weight_grad(index_ref, f_ref, [d_ref], keep_ref, send_ref, 0)
            for k in range(zs):
                for ref, side in ((keep_ref, index_ref[0] % 2), (send_ref, 1 - index_ref[0] % 2)):
                    cols = pl.ds(pl.multiple_of((((index_ref[0] // 2) ^ k) * 2 + side) * own_rows, 128), own_rows)
                    total = v0[:, cols] + v1[:, cols] + v2[:, cols] + v3[:, cols]
                    ref[k, own_rows:] = jnp.zeros((16, 384), BF)
                    ref[k, own_rows:, :own_rows] = total.astype(BF)

        keep, send = call(
            last_grad_body, [((zs, own_rows + 16, 384), BF)] * 2, index, first, d_last,
            *shared_vectors, specs=[SM] + [VM] * 6, name="last_grad", us=2, after=[sum_ffn],
        )
        got_last = dp_reduce(keep, send, "last_add", after=got_first[1:])

        def attn_finish_body(p0, p1, p2, p3, t0, t1, t2, t3, q_ref, k_ref, v_ref, o_ref, model_ref):
            early = p0[...] + p1[...].astype(F32) + p2[...].astype(F32) + p3[...].astype(F32)
            late = t0[...] + t1[...].astype(F32) + t2[...].astype(F32) + t3[...].astype(F32)
            for k, ref in enumerate((q_ref, k_ref, v_ref)):
                cols = slice(k * 128, (k + 1) * 128)
                ref[:, 0:128] = early[:, cols]
                ref[:, 128:256] = late[:own_rows, cols]
            o_ref[...] = early[:, 384:].T
            model_ref[...] = late[own_rows:, :own_rows]

        shapes = [(own_rows, heads)] * 3 + [(heads, own_rows), (16, own_rows)]
        q_grad, k_grad, v_grad, out_grad, model = call(
            attn_finish_body, [(shape, F32) for shape in shapes], *got_first, *got_last, store=(0, 1, 2, 3),
            name="attn_finish",
        )
    else:
        pairs = [plain_grad(first, d).T.reshape(3, 128, own_rows) for d in (d_first, d_last)]
        q_grad, k_grad, v_grad = (joined([p[k] for p in pairs]).T for k in range(3))
        out_grad = plain_grad(branch, mixed).T
        model = lax.psum_scatter(sum(shared_vectors), "dp", scatter_dimension=1, tiled=True)
        sum_ffn = lax.psum(sum_ffn, "dp")
    ffn = sum_ffn[:, :hidden]
    return (
        layer_output[None], input_grad.transpose(1, 0, 2), q_grad, k_grad, v_grad,
        model[2], model[3], model[0], model[1], model[4], model[5], out_grad, model[8], model[6], model[7],
        gate_grad, up_grad, ffn[0], ffn[1], ffn[2], ffn[3], down_grad, model[9],
    )


def solution(mesh):
    rows, across, tokens = P("dp", "tensor"), P("tensor", "dp"), P("dp", "tensor", None)
    model, ffn, image = P("dp"), P("tensor"), P("dp", None)
    in_specs = (
        tokens, rows, rows, rows, model, model, model, model, model, model, across, model, model, model, rows, rows,
        ffn, ffn, ffn, ffn, across, model, tokens, image, image, image,
    )
    out_specs = (
        tokens, tokens, rows, rows, rows, model, model, model, model, model, model, across, model, model, model,
        rows, rows, ffn, ffn, ffn, ffn, across, model,
    )
    return jax.shard_map(local, mesh=mesh, in_specs=in_specs, out_specs=out_specs, check_vma=False)
```

```python
import functools
import math

import jax
import jax.numpy as jnp
from jax import lax
from jax.experimental import pallas as pl
from jax.experimental.pallas import tpu as pltpu
from jax.sharding import PartitionSpec as P

HD = 64
EPSILON = 1e-06
LOW = -1e30
BF = jnp.bfloat16
F32 = jnp.float32
HI = lax.Precision.HIGHEST
VM = pl.BlockSpec(memory_space=pltpu.VMEM)
SM = pl.BlockSpec(memory_space=pltpu.SMEM)
ANY = pl.BlockSpec(memory_space=pl.ANY)
HB = pl.BlockSpec(memory_space=pltpu.HBM)
Q_BIAS, V_BIAS, F_GAIN, F_BIAS, M_GAIN, M_BIAS, O_BIAS, S_GAIN, S_BIAS, D_BIAS = range(10)


def nn(a, b, precision=None):
    return lax.dot_general(a, b, (((1,), (0,)), ((), ())), precision, F32)


def nt(a, b, precision=None):
    return lax.dot_general(a, b, (((1,), (1,)), ((), ())), precision, F32)


def tn(a, b, precision=None):
    return lax.dot_general(a, b, (((0,), (0,)), ((), ())), precision, F32)


def call(
    body, outs, *args, specs=None, load=(), store=(), mib=8, us=1.0, name=None, after=(), scratch=(), token=False, **extra
):
    if token:
        outs = [*outs, ((8, 128), F32)]
    shapes = [jax.ShapeDtypeStruct(shape, dtype) for shape, dtype in outs]
    n_in, n_out, n_after, moved = len(args), len(outs), len(after), len(load) + len(store)
    specs = list(specs or [VM] * n_in)
    out_specs = [VM] * n_out
    for i in load:
        specs[i] = HB
    for i in store:
        out_specs[i] = HB
        shapes[i] = pltpu.HBM(*outs[i])
    args = [hbm(a) if s is HB else a for a, s in zip(args, specs)]
    held = [pltpu.VMEM(args[i].shape, args[i].dtype) for i in load] + [pltpu.VMEM(*outs[i]) for i in store]
    if moved:
        held.append(pltpu.SemaphoreType.DMA((moved,)))

    def run(*refs):
        ins, outs_ = list(refs[:n_in]), list(refs[n_in + n_after : n_in + n_after + n_out])
        rest = refs[n_in + n_after + n_out :]
        own, copies = rest[: len(scratch)], rest[len(scratch) :]
        reads = [pltpu.make_async_copy(ins[i], copies[j], copies[-1].at[j]) for j, i in enumerate(load)]
        for one in reads:
            one.start()
        for j, i in enumerate(load):
            ins[i] = copies[j]
        writes = []
        for j, i in enumerate(store, len(load)):
            writes.append(pltpu.make_async_copy(copies[j], outs_[i], copies[-1].at[j]))
            outs_[i] = copies[j]
        for one in reads:
            one.wait()
        body(*ins, *(outs_[:-1] if token else outs_), *own)
        for one in writes:
            one.start()
        for one in writes:
            one.wait()

    return pl.pallas_call(
        run,
        out_shape=shapes,
        in_specs=specs + [ANY] * n_after,
        out_specs=out_specs,
        scratch_shapes=list(scratch) + held,
        compiler_params=pltpu.CompilerParams(vmem_limit_bytes=mib << 20),
        cost_estimate=pl.CostEstimate(flops=int(us * 1.1e7), bytes_accessed=1 << 10, transcendentals=0),
        name=name,
        **extra,
    )(*args, *after)


def swap(value, axis, offset):
    count = lax.axis_size(axis)
    return lax.ppermute(value, axis, [(i, i ^ offset) for i in range(count)])


def tensor_gather(block):
    core = swap(block, "tensor", 1)
    far = swap(block, "tensor", 2)
    return [block, core, far, swap(far, "tensor", 1)]


def add_pair_body(a_ref, b_ref, out_ref):
    out_ref[...] = (a_ref[...].astype(F32) + b_ref[...].astype(F32)).astype(BF)


def tensor_scatter(parts, after=()):
    third = swap(parts[3], "tensor", 1)
    first = swap(parts[1], "tensor", 1)
    (to_far,) = call(add_pair_body, [(third.shape, BF)], parts[2], third, name="add_pair", after=after)
    return [parts[0], first, swap(to_far, "tensor", 2)], to_far


def tensor_share(value):
    return [value] + [swap(value, "tensor", k) for k in (1, 2, 3)]


def dp_column(block):
    return [block] + [swap(block, "dp", 2 * k) for k in range(1, lax.axis_size("dp") // 2)]


def dp_across(column):
    return [one for mine in column for one in (mine, swap(mine, "dp", 1))]


def hbm(value):
    return pltpu.with_memory_space_constraint(value, pltpu.HBM)


def tie(value, *others):
    def body(*refs):
        pass

    return pl.pallas_call(
        body,
        out_shape=pltpu.HBM(value.shape, value.dtype),
        in_specs=[HB] + [ANY] * len(others),
        out_specs=HB,
        input_output_aliases={0: 0},
        cost_estimate=pl.CostEstimate(flops=1, bytes_accessed=1, transcendentals=0),
        compiler_params=pltpu.CompilerParams(vmem_limit_bytes=1 << 20),
        name="tie",
    )(hbm(value), *others)


def hold(values, *others):
    count = len(values)

    def body(*refs):
        refs, held, sems = refs[: -count - 1], refs[-count - 1 : -1], refs[-1]
        reads = [pltpu.make_async_copy(refs[i], held[i], sems.at[0, i]) for i in range(count)]
        writes = [pltpu.make_async_copy(held[i], refs[i - count], sems.at[1, i]) for i in range(count)]
        for one in reads:
            one.start()
        for read, write in zip(reads, writes):
            read.wait()
            write.start()
        for one in writes:
            one.wait()

    return pl.pallas_call(
        body,
        out_shape=[pltpu.HBM(v.shape, v.dtype) for v in values],
        in_specs=[ANY] * (count + len(others)),
        out_specs=[HB] * count,
        scratch_shapes=[pltpu.VMEM(v.shape, v.dtype) for v in values] + [pltpu.SemaphoreType.DMA((2, count))],
        cost_estimate=pl.CostEstimate(flops=1, bytes_accessed=1, transcendentals=0),
        compiler_params=pltpu.CompilerParams(vmem_limit_bytes=4 << 20),
        name="hold",
    )(*values, *others)


def center_scale(values):
    width = values.shape[-1]
    mean = jnp.sum(values, axis=-1, keepdims=True) / width
    spread = jnp.sum(values * values, axis=-1, keepdims=True) / width - mean * mean
    return mean, lax.rsqrt(spread + EPSILON)


def unit_back(grad_hat, unit, inverse):
    width = unit.shape[-1]
    mean = jnp.sum(grad_hat, axis=-1, keepdims=True) / width
    cross = jnp.sum(grad_hat * unit, axis=-1, keepdims=True) / width
    return inverse * (grad_hat - mean - unit * cross)


def columns_to_rows(columns):
    count = columns[0].shape[0]
    lanes = lax.broadcasted_iota(jnp.int32, (count, 128), 1)
    wide = jnp.zeros((count, 128), F32)
    for k, column in enumerate(columns):
        wide = jnp.where(lanes == k, column, wide)
    return wide.T[0:8]


def rows_to_columns(rows):
    return rows.T


def summed_stats(refs, r):
    return refs[0][r] + refs[1][r ^ 1] + refs[2][r ^ 2] + refs[3][r ^ 3]


def turn(values, cosine, sine):
    lanes = lax.broadcasted_iota(jnp.int32, values.shape, 1)
    other = jnp.where(lanes % 2 == 0, pltpu.roll(values, 127, 1), pltpu.roll(values, 1, 1))
    return values * cosine + other * sine


def half_mask(s):
    lane = lax.broadcasted_iota(jnp.int32, (1, 128), 1)
    return lane < HD if s == 0 else lane >= HD


def local(
    layer_input, query_weight, key_weight, value_weight, query_bias, value_bias, first_gain, first_bias,
    mixer_gain, mixer_bias, output_weight, output_bias, second_gain, second_bias, gate_weight, up_weight,
    gate_bias, up_bias, inner_gain, inner_bias, down_weight, down_bias, cotangent, key_valid, patch_row, patch_column,
):
    ranks = lax.axis_size("tensor")
    me_t, me_d, count_d = lax.axis_index("tensor"), lax.axis_index("dp"), lax.axis_size("dp")
    block, width = layer_input.shape[1:]
    pad = -(-block // 16) * 16
    length = ranks * pad
    heads = query_weight.shape[1]
    hidden = gate_weight.shape[1]
    hidden_pad = -(-hidden // 128) * 128
    own_rows = width // count_d
    direct = own_rows % 128 == 0 and count_d & (count_d - 1) == 0
    index = jnp.stack([me_d, me_t]).astype(jnp.int32)
    x_own, cot_own = layer_input[0], cotangent[0]
    blocks = range(ranks)

    def rows_of(r):
        return slice(r * pad, (r + 1) * pad)

    lines = jnp.stack([key_valid[0], patch_row[0], patch_column[0], jnp.arange(ranks * block, dtype=jnp.int32)])
    lines = jnp.pad(lines.reshape(4, ranks, block), ((0, 4), (0, 0), (0, pad - block))).astype(F32)
    lines = jnp.stack([lax.dynamic_index_in_dim(lines, me_t ^ r, 1, False) for r in blocks])
    lane = jnp.arange(128)
    frequency = jnp.power(F32(10000.0), -((lane % HD) // 2 % (HD // 4)).astype(F32) / (HD // 4))
    frequency = jnp.broadcast_to(frequency[None, :], (8, 128))

    def table_body(line_ref, frequency_ref, cos_ref, sin_ref):
        lanes = lax.broadcasted_iota(jnp.int32, (pad, 128), 1)
        for r in blocks:
            columns = rows_to_columns(line_ref[r])
            position = jnp.where(lanes % HD < HD // 2, columns[:, 1:2], columns[:, 2:3])
            angle = jnp.where(columns[:, 3:4] > 0.0, 0.5 * (position * frequency_ref[0:1]), 0.0)
            cos_ref[rows_of(r)] = jnp.cos(angle)
            sine = jnp.sin(angle)
            sin_ref[rows_of(r)] = jnp.where(lanes % 2 == 0, -sine, sine)

    cosine, sine = call(table_body, [((length, 128), F32)] * 2, lines, frequency, name="tables", us=4)

    small = [
        v[None, :]
        for v in (
            query_bias, value_bias, first_gain, first_bias, mixer_gain, mixer_bias, output_bias, second_gain,
            second_bias, down_bias,
        )
    ]
    tiles = heads // 128
    hidden_low = -(-hidden // 16) * 16
    starts = [(k % 3) * tiles + k // 3 for k in range(3 * tiles)]
    if direct:
        o_start = 3 * tiles * own_rows + 16

        def pack_a_body(q_ref, k_ref, v_ref, w_ref, *refs):
            *small_refs, out_ref = refs
            out_ref[o_start:] = w_ref[...]
            for k in range(3 * tiles):
                ref = (q_ref, k_ref, v_ref)[k % 3]
                out_ref[k * own_rows : (k + 1) * own_rows] = ref[:, k // 3 * 128 : (k // 3 + 1) * 128]
            lines = [ref[...].astype(F32) for ref in small_refs]
            lines.append(jnp.zeros((16 - len(lines), own_rows), F32))
            out_ref[3 * tiles * own_rows : o_start] = jnp.concatenate(lines, axis=0).astype(BF)

        (pack_a,) = call(
            pack_a_body, [((o_start + heads, 128), BF)], query_weight, key_weight, value_weight, output_weight,
            *small, name="pack_a", load=tuple(range(14)),
        )
        column_a = dp_column(pack_a)
        across_a = [swap(pack_a, "dp", 1)]
        x_far = swap(x_own, "tensor", 2)
        *column_a[1:], across_a[0], x_held, x_far = hold([*column_a[1:], *across_a, x_own, x_far], cosine)
        across_a += [swap(one, "dp", 1) for one in column_a[1:]]
        x_blocks = [x_own, swap(x_held, "tensor", 1), x_far, swap(x_far, "tensor", 1)]
        got_a = [one for pair in zip(column_a, across_a) for one in pair]

        def pack_f_body(g_ref, u_ref, d_ref, out_ref):
            for j, ref in enumerate((g_ref, u_ref, d_ref)):
                out_ref[(j + 1) * hidden_low - 16 : (j + 1) * hidden_low] = jnp.zeros((16, own_rows), BF)
                out_ref[j * hidden_low : j * hidden_low + hidden] = ref[...]

        (pack_f,) = call(
            pack_f_body, [((3 * hidden_low, own_rows), BF)], gate_weight.T, up_weight.T, down_weight, name="pack_f",
            load=(0, 1, 2),
        )
        got_f = lax.all_gather(tie(pack_f, column_a[3]), "dp")
        def copies(pairs, sems):
            started = [pltpu.make_async_copy(a, b, sems.at[i]) for i, (a, b) in enumerate(pairs)]
            for one in started:
                one.start()
            for one in started:
                one.wait()

        def chunk_at(index_ref, r):
            return pl.ds(pl.multiple_of((index_ref[0] ^ r) * own_rows, 128), own_rows)

        def assemble_a(index_ref, *refs):
            *chunks, cot_ref = refs[: count_d + 1]
            w_ref, v_ref, o_ref, cot_out, small_ref, held_ref, sems, cot_sems = refs[count_d + 1 :]
            cot_read = pltpu.make_async_copy(cot_ref, held_ref, cot_sems.at[0])
            cot_write = pltpu.make_async_copy(held_ref, cot_out, cot_sems.at[1])
            cot_read.start()
            pairs = []
            for r, chunk in enumerate(chunks):
                for k in range(3 * tiles):
                    pairs.append((
                        chunk.at[k * own_rows : (k + 1) * own_rows],
                        w_ref.at[chunk_at(index_ref, r), k * 128 : (k + 1) * 128],
                    ))
                pairs.append((chunk.at[3 * tiles * own_rows : o_start], small_ref.at[r]))
                pairs.append((chunk.at[o_start:], o_ref.at[:, chunk_at(index_ref, r)]))
            started = [pltpu.make_async_copy(a, b, sems.at[i]) for i, (a, b) in enumerate(pairs)]
            for one in started:
                one.start()
            cot_read.wait()
            cot_write.start()
            for one in started:
                one.wait()
            for r in range(count_d):
                v_ref[:, chunk_at(index_ref, r)] = small_ref[r].astype(F32)
            cot_write.wait()

        specs = [SM] + [HB] * count_d

        def dma(count):
            return pltpu.SemaphoreType.DMA((count,))

        shapes = [((width, 3 * heads), BF), ((16, width), F32), ((heads, width), BF), (cot_own.shape, BF)]
        w_qkv, vec, w_out, cot_held = pl.pallas_call(
            assemble_a,
            out_shape=[jax.ShapeDtypeStruct(*shape) for shape in shapes[:3]] + [pltpu.HBM(*shapes[3])],
            in_specs=specs + [HB],
            out_specs=[VM] * 3 + [HB],
            scratch_shapes=[
                pltpu.VMEM((count_d, 16, 128), BF), pltpu.VMEM(*shapes[3]), dma(count_d * (3 * tiles + 2)), dma(2)
            ],
            compiler_params=pltpu.CompilerParams(vmem_limit_bytes=4 << 20),
            cost_estimate=pl.CostEstimate(flops=1 << 10, bytes_accessed=1 << 10, transcendentals=0),
            name="assemble_a",
        )(index, *[hbm(v) for v in got_a], hbm(cot_own))
        cot_blocks = tensor_gather(cot_held)
    else:
        def whole(weight, axis):
            return lax.all_gather(weight, "dp", axis=axis, tiled=True)

        x_blocks = tensor_gather(x_own)
        cot_blocks = tensor_gather(cot_own)
        w_qkv = whole(jnp.concatenate(
            [(query_weight, key_weight, value_weight)[k % 3][:, k // 3 * 128 : (k // 3 + 1) * 128] for k in range(3 * tiles)],
            axis=1,
        ), 0)
        vec = jnp.pad(whole(jnp.concatenate(small), 1).astype(F32), ((0, 6), (0, 0)))
        w_out = whole(output_weight, 1)
        w_gate, w_up, w_down = (
            jnp.pad(whole(w, 1), ((0, hidden_pad - hidden), (0, 0))) for w in (gate_weight.T, up_weight.T, down_weight)
        )
    ffn_vec = jnp.pad(
        jnp.stack([gate_bias, up_bias, inner_gain, inner_bias]).astype(F32), ((0, 4), (0, hidden_pad - hidden))
    )

    def own(ref, k, index_ref):
        return ref[k : k + 1, pl.ds(pl.multiple_of(index_ref[1] * heads, 128), heads)]

    n_heads = heads // HD

    def attend_body(
        index_ref, x0, x1, x2, x3, w_ref, vec_ref, cos_ref, sin_ref, line_ref,
        unit_out, q_out, k_out, v_out, o_ref, stat_ref, unit_ref, q_ref, k_ref, v_ref, first_ref, x_ref, cos_held,
        sin_held, sems, load_sems,
    ):
        reads = [pltpu.make_async_copy(ref, x_ref.at[r], load_sems.at[r]) for r, ref in enumerate((x0, x1, x2, x3))]
        reads.append(pltpu.make_async_copy(cos_ref, cos_held, load_sems.at[4]))
        reads.append(pltpu.make_async_copy(sin_ref, sin_held, load_sems.at[5]))
        for one in reads:
            one.start()
        gain, bias = vec_ref[F_GAIN : F_GAIN + 1], vec_ref[F_BIAS : F_BIAS + 1]
        q_bias, v_bias = own(vec_ref, Q_BIAS, index_ref), own(vec_ref, V_BIAS, index_ref)
        moves = []
        for r in blocks:
            reads[r].wait()
            x = x_ref[r].astype(F32)
            mean, inverse = center_scale(x)
            unit = (x - mean) * inverse
            unit_ref[(r + 1) * pad - 16 : (r + 1) * pad] = jnp.zeros((16, width), BF)
            unit_ref[r * pad : r * pad + block] = unit.astype(BF)
            first_ref[pad - 16 :] = jnp.zeros((16, width), BF)
            first_ref[:block] = (unit * gain + bias).astype(BF)
            rows = rows_of(r)
            qkv = nn(first_ref[...], w_ref[...])
            if r == 0:
                reads[4].wait()
                reads[5].wait()
            c, s = cos_held[rows], sin_held[rows]
            for k in range(tiles):
                cols = slice(k * 128, (k + 1) * 128)
                q, key, v = (qkv[:, (3 * k + j) * 128 : (3 * k + j + 1) * 128] for j in range(3))
                q_ref[rows, cols] = turn(q + q_bias[:, cols], c, s).astype(BF)
                k_ref[rows, cols] = turn(key, c, s).astype(BF)
                v_ref[rows, cols] = (v + v_bias[:, cols]).astype(BF)
            for j, (held, out) in enumerate(
                ((unit_ref, unit_out), (q_ref, q_out), (k_ref, k_out), (v_ref, v_out))
            ):
                moves.append(pltpu.make_async_copy(held.at[rows], out.at[rows], sems.at[4 * r + j]))
                moves[-1].start()
        mask_line = jnp.concatenate([jnp.where(line_ref[r][0:1] == 1.0, 0.0, LOW) for r in blocks], axis=1)
        k_half, v_half = [], []
        for h in range(n_heads):
            cols = slice(h // 2 * 128, (h // 2 + 1) * 128)
            k_half.append(jnp.where(half_mask(h % 2), k_ref[:, cols], 0).astype(BF))
            v_half.append(jnp.where(half_mask(h % 2), v_ref[:, cols], 0).astype(BF))

        def step(b, _):
            rows = pl.ds(pl.multiple_of(b * pad, 16), pad)
            kept = []
            total = jnp.zeros((pad, 1), F32)
            square = jnp.zeros((pad, 1), F32)
            for pair in range(tiles):
                cols = slice(pair * 128, (pair + 1) * 128)
                q = q_ref[rows, cols]
                out = jnp.zeros((pad, 128), F32)
                for s in range(2):
                    h = 2 * pair + s
                    scores = nt(q, k_half[h]) * (1.0 / math.sqrt(HD)) + mask_line
                    top = jnp.max(scores, axis=-1, keepdims=True)
                    terms = jnp.exp(scores - top)
                    below = jnp.sum(terms, axis=-1, keepdims=True)
                    out += nn(terms.astype(BF), v_half[h]) * (1.0 / below)
                    kept.append(top + jnp.log(below))
                o_ref[rows, cols] = out
                total += jnp.sum(out, axis=-1, keepdims=True)
                square += jnp.sum(out * out, axis=-1, keepdims=True)
            stat_ref[b] = columns_to_rows(kept + [total, square])
            return 0

        lax.fori_loop(0, ranks, step, 0)
        for one in moves:
            one.wait()

    shapes = [((length, width), BF)] + [((length, heads), BF)] * 3
    unit_one, queries, keys, values, attended, stat_mix = pl.pallas_call(
        attend_body,
        out_shape=[pltpu.HBM(*shape) for shape in shapes]
        + [jax.ShapeDtypeStruct((length, heads), F32), jax.ShapeDtypeStruct((ranks, 8, pad), F32)],
        in_specs=[SM] + [HB] * 4 + [VM] * 2 + [HB] * 2 + [VM],
        out_specs=[HB] * 4 + [VM] * 2,
        scratch_shapes=[pltpu.VMEM(*shape) for shape in shapes]
        + [pltpu.VMEM((pad, width), BF), pltpu.VMEM((ranks, block, width), BF)]
        + [pltpu.VMEM((length, 128), F32)] * 2
        + [pltpu.SemaphoreType.DMA((4 * ranks,)), pltpu.SemaphoreType.DMA((6,))],
        compiler_params=pltpu.CompilerParams(vmem_limit_bytes=22 << 20),
        cost_estimate=pl.CostEstimate(flops=1 << 17, bytes_accessed=1 << 10, transcendentals=0),
        name="attend",
    )(index, *[hbm(v) for v in x_blocks], w_qkv, vec, hbm(cosine), hbm(sine), lines)
    shared_mix = tensor_share(stat_mix)

    def mix_body(index_ref, a_ref, s0, s1, s2, s3, w_ref, vec_ref, mixed_ref, norm_ref, *part_refs):
        gain, bias = own(vec_ref, M_GAIN, index_ref), own(vec_ref, M_BIAS, index_ref)
        for r in reversed(blocks):
            rows = rows_of(r)
            sums = summed_stats((s0, s1, s2, s3), r)
            mean = sums[n_heads : n_heads + 1] / width
            inverse = lax.rsqrt(sums[n_heads + 1 : n_heads + 2] / width - mean * mean + EPSILON)
            lines = jnp.concatenate([mean, inverse, jnp.zeros((6, pad), F32)], axis=0)
            norm_ref[r] = lines
            columns = rows_to_columns(lines)
            mixed = ((a_ref[rows] - columns[:, 0:1]) * columns[:, 1:2] * gain + bias).astype(BF)
            mixed_ref[rows] = mixed
            part_refs[r][...] = nn(mixed, w_ref[...])[:block].astype(BF)

    mixed, norm_mix, *parts = call(
        mix_body, [((length, heads), BF), ((ranks, 8, pad), F32)] + [((block, width), BF)] * ranks,
        index, attended, *shared_mix, w_out, vec, specs=[SM] + [VM] * 7, name="mix", us=2.5,
        store=(0,), after=[cot_blocks[2]],
    )
    arrived, _ = tensor_scatter(parts)

    def second_body(x_ref, p0, p1, p2, vec_ref, hidden_ref, second_ref):
        out = p0[...].astype(F32) + p1[...].astype(F32) + p2[...].astype(F32)
        state = x_ref[...].astype(F32) + out + vec_ref[O_BIAS : O_BIAS + 1]
        hidden_ref[...] = state
        mean, inverse = center_scale(state)
        unit = (state - mean) * inverse
        second_ref[...] = (unit * vec_ref[S_GAIN : S_GAIN + 1] + vec_ref[S_BIAS : S_BIAS + 1]).astype(BF)

    hidden_state, second_own = call(
        second_body, [((block, width), F32), ((block, width), BF)], x_own, *arrived, vec, name="second", store=(0, 1),
    )
    half = 2 * pad

    def half_rows(r):
        return slice(r % 2 * pad, (r % 2 + 1) * pad)

    def pad_block(ref, r, value):
        start = r * pad
        ref[start + pad - 16 : start + pad] = jnp.zeros((16, width), BF)
        ref[start : start + block] = value

    def expand(b_refs, wg_ref, wu_ref, vec_ref, grad_ref, second_ref, gate_ref, up_ref, stat_ref, base):
        for r, b_ref in enumerate(b_refs):
            rows = half_rows(r)
            pad_block(second_ref, r, b_ref[...])
            gate = nt(second_ref[rows], wg_ref[...]) + vec_ref[0:1]
            up = nt(second_ref[rows], wu_ref[...]) + vec_ref[1:2]
            gate_ref[rows] = gate
            up_ref[rows] = up
            activated = gate * jax.nn.sigmoid(gate) * up
            hat = grad_ref[rows] * vec_ref[2:3]
            stat_ref[base + r] = columns_to_rows(
                [jnp.sum(v, axis=-1, keepdims=True) for v in (activated, activated * activated, hat, hat * activated)]
            )

    def expand_first_body(c0, c1, c2, c3, b0, b1, vec_ref, *refs):
        if direct:
            chunks, *refs, down_sems, gate_sems = refs
            wg_ref, wu_ref, wd_ref = refs[:3]
            outs = refs[3:]
            moves = []
            for j, (out, sems) in enumerate(((wd_ref, down_sems), (wg_ref, gate_sems), (wu_ref, gate_sems))):
                for a in range(count_d):
                    start = (2, 0, 1)[j] * hidden_low
                    moves.append(pltpu.make_async_copy(
                        chunks.at[a, start : start + hidden_low],
                        out.at[0:hidden_low, a * own_rows : (a + 1) * own_rows],
                        sems.at[a if j < 2 else count_d + a],
                    ))
                    moves[-1].start()
            for out in (wg_ref, wu_ref, wd_ref):
                out[hidden_low:] = jnp.zeros((hidden_pad - hidden_low, width), BF)
            for one in moves[:count_d]:
                one.wait()
        else:
            wg_ref, wu_ref, wd_ref = refs[:3]
            outs = refs[3:]
        cot0, cot1, grad0, grad1, second_ref, gate_ref, up_ref, stat_ref = outs
        for r, c_ref in enumerate((c0, c1, c2, c3)):
            cot_ref, grad_ref = ((cot0, grad0), (cot1, grad1))[r // 2]
            pad_block(cot_ref, r % 2, c_ref[...])
            grad_ref[half_rows(r)] = nt(cot_ref[half_rows(r)], wd_ref[...])
        if direct:
            for one in moves[count_d:]:
                one.wait()
        expand((b0, b1), wg_ref, wu_ref, vec_ref, grad0, second_ref, gate_ref, up_ref, stat_ref, 0)

    half_outs = [((half, width), BF)] + [((half, hidden_pad), F32)] * 2
    second_far = swap(second_own, "tensor", 2)
    blocks_in = [*cot_blocks, second_own, swap(second_own, "tensor", 1), ffn_vec]
    outs = [((half, width), BF)] * 2 + [((half, hidden_pad), F32)] * 2 + half_outs + [((2, 8, pad), F32)]
    weights = [((hidden_pad, width), BF)] * 3
    if direct:
        w_gate, w_up, w_down, *made = call(
            expand_first_body, weights + outs, *blocks_in, got_f, specs=[VM] * 7 + [HB], name="expand_first",
            scratch=[dma(count_d), dma(2 * count_d)], us=10, load=tuple(range(6)),
        )
    else:
        made = call(expand_first_body, outs, *blocks_in, w_gate, w_up, w_down, name="expand_first", us=10)
    cot_halves, grad_inner, first_half = made[:2], made[2:4], made[4:]

    def expand_body(b0, b1, wg_ref, wu_ref, vec_ref, grad_ref, before_ref, second_ref, gate_ref, up_ref, stat_ref):
        stat_ref[0:2] = before_ref[...]
        expand((b0, b1), wg_ref, wu_ref, vec_ref, grad_ref, second_ref, gate_ref, up_ref, stat_ref, 2)

    second_far = tie(second_far, first_half[3])
    expanded = [first_half, call(
        expand_body, half_outs + [((4, 8, pad), F32)], second_far, swap(second_far, "tensor", 1), w_gate, w_up, ffn_vec,
        grad_inner[1], first_half[3], name="expand", us=3.7, load=(0, 1),
    )]
    shared_ffn = tensor_share(expanded[1][3])

    def ffn_back_body(
        first_block, g_ref, u_ref, grad_ref, s0, s1, s2, s3, vec_ref, wg_ref, wu_ref, *refs
    ):
        dg_ref, du_ref, inner_ref, sum_ref, *part_refs = refs[-6:]
        wide = hidden * ranks
        sum_ref[...] = refs[0][...] if len(refs) == 7 else jnp.zeros_like(sum_ref)
        for r in (1, 0):
            rows = half_rows(r)
            sums = summed_stats((s0, s1, s2, s3), first_block + r)
            mean = sums[0:1] / wide
            inverse = lax.rsqrt(sums[1:2] / wide - mean * mean + EPSILON)
            grad_mean = sums[2:3] / wide
            cross = inverse * (sums[3:4] / wide - mean * grad_mean)
            columns = rows_to_columns(
                jnp.concatenate([mean, inverse, grad_mean, cross, jnp.zeros((4, pad), F32)], axis=0)
            )
            mean, inverse, grad_mean, cross = (columns[:, k : k + 1] for k in range(4))
            gate, up, grad = g_ref[rows], u_ref[rows], grad_ref[rows]
            sigmoid = jax.nn.sigmoid(gate)
            silu = gate * sigmoid
            unit = (silu * up - mean) * inverse
            inner_ref[rows] = (unit * vec_ref[2:3] + vec_ref[3:4]).astype(BF)
            grad_act = inverse * (grad * vec_ref[2:3] - grad_mean - unit * cross)
            d_gate = (grad_act * up * sigmoid * (1.0 + gate - silu)).astype(BF)
            d_up = (grad_act * silu).astype(BF)
            dg_ref[rows] = d_gate
            du_ref[rows] = d_up
            totals = [d_gate.astype(F32), d_up.astype(F32), grad * unit, grad]
            sum_ref[0:4] += jnp.concatenate([jnp.sum(v, axis=0, keepdims=True) for v in totals], axis=0)
            part_refs[r][...] = (nn(d_gate, wg_ref[...]) + nn(d_up, wu_ref[...]))[:block].astype(BF)

    backed = [None, None]
    for j in (1, 0):
        before = [backed[1][3]] if j == 0 else []
        backed[j] = call(
            functools.partial(ffn_back_body, 2 * j),
            [((half, hidden_pad), BF)] * 3 + [((8, hidden_pad), F32)] + [((block, width), BF)] * 2,
            *expanded[j][1:3], grad_inner[j], *shared_ffn, ffn_vec, w_gate, w_up, *before, name="ffn_back", us=5.5,
            store=() if j else (4, 5),
        )
    sum_ffn = backed[0][3]
    arrived, to_far = tensor_scatter([*backed[0][4:], *backed[1][4:]])

    def dp_sum_step(total, k, after):
        def body(a_ref, b_ref, out_ref):
            out_ref[...] = a_ref[...] + b_ref[...]

        return call(body, [(total.shape, F32)], total, swap(total, "dp", k), name="dp_sum", after=after)[0]

    if direct:
        rows_f = 3 * hidden_low

        def ffn_grad_body(g0, g1, u0, u1, i0, i1, e0, e1, c0, c1, out_ref):
            for j, (rights, lefts) in enumerate((((g0, g1), (e0, e1)), ((u0, u1), (e0, e1)), ((i0, i1), (c0, c1)))):
                for at in range(0, hidden_low, 256):
                    stop = min(at + 256, hidden_low)
                    cols = slice(at, min(at + 256, hidden_pad))
                    total = sum(tn(a[:, cols], b[...]) for a, b in zip(rights, lefts)).astype(BF)
                    for d in range(count_d):
                        base = d * rows_f + j * hidden_low
                        out_ref[base + at : base + stop] = total[: stop - at, d * own_rows : (d + 1) * own_rows]

        ffn_grads, ffn_token = call(
            ffn_grad_body, [((count_d * rows_f, own_rows), BF)], *(backed[j][k] for k in (0, 1, 2) for j in range(2)),
            expanded[0][0], expanded[1][0], *cot_halves, name="ffn_grad", us=8, store=(0,),
            after=[to_far], token=True,
        )
        ffn_grads = tie(ffn_grads, arrived[2])
        got_ffn = lax.psum_scatter(ffn_grads, "dp", scatter_dimension=0, tiled=True)

        def ffn_finish_body(p_ref, *out_refs):
            for j, ref in enumerate(out_refs):
                ref[...] = p_ref[j * hidden_low : j * hidden_low + hidden].astype(F32)

        gate_grad, up_grad, down_grad = call(
            ffn_finish_body, [((hidden, own_rows), F32)] * 3, got_ffn, store=(0, 1, 2), load=(0,), name="ffn_finish",
        )
        gate_grad, up_grad = gate_grad.T, up_grad.T
    else:
        def plain_grad(left, right):
            return lax.psum_scatter(tn(left, right).astype(BF), "dp", scatter_dimension=0, tiled=True).astype(F32)

        def joined(pair):
            return jnp.concatenate(pair)

        second_all = joined([expanded[j][0] for j in range(2)])
        down_grad = plain_grad(joined(cot_halves), joined([backed[j][2] for j in range(2)]))[:, :hidden].T
        gate_grad = plain_grad(second_all, joined([backed[j][0] for j in range(2)]))[:, :hidden]
        up_grad = plain_grad(second_all, joined([backed[j][1] for j in range(2)]))[:, :hidden]

    def hidden_back_body(p0, p1, p2, h_ref, cot_ref, vec_ref, grad_ref, branch_ref, sum_ref):
        grad_second = p0[...].astype(F32) + p1[...].astype(F32) + p2[...].astype(F32)
        mean, inverse = center_scale(h_ref[...])
        unit = (h_ref[...] - mean) * inverse
        cot = cot_ref[...].astype(F32)
        grad = cot + unit_back(grad_second * vec_ref[S_GAIN : S_GAIN + 1], unit, inverse)
        branch = grad.astype(BF)
        grad_ref[...] = grad
        branch_ref[...] = branch
        lines = [grad_second * unit, grad_second, branch.astype(F32), cot]
        lines = [jnp.sum(v, axis=0, keepdims=True) for v in lines]
        sum_ref[...] = jnp.concatenate(lines + [jnp.zeros((4, width), F32)], axis=0)

    grad_hidden, branch_own, sum_two = call(
        hidden_back_body, [((block, width), F32), ((block, width), BF), ((8, width), F32)],
        *arrived, hidden_state, cot_own, vec, name="hidden_back", after=[ffn_token] if direct else [],
        store=(0,), load=(0, 1, 2, 3, 4),
    )

    def down_body(i0, i1, w_ref, *part_refs):
        for r in reversed(blocks):
            part_refs[r][...] = nn((i0, i1)[r // 2][half_rows(r)], w_ref[...])[:block].astype(BF)

    if direct:
        sum_ffn = dp_sum_step(sum_ffn, 1, [branch_own])
    *down_parts, down_token = call(
        down_body, [((block, width), BF)] * ranks, backed[0][2], backed[1][2], w_down, name="down", us=2.5, token=True,
        after=[sum_ffn],
    )
    branch_far = swap(branch_own, "tensor", 2)
    branch_core = swap(branch_own, "tensor", 1)
    if direct:
        sum_ffn = dp_sum_step(sum_ffn, 2, [down_token])
    branch_far = tie(branch_far, sum_ffn)
    branch_blocks = [branch_own, branch_core, branch_far, swap(branch_far, "tensor", 1)]

    def mix_back_body(index_ref, b0, b1, b2, b3, w_ref, a_ref, norm_ref, vec_ref, branch_ref, grad_ref, stat_ref, sum_ref):
        gain = own(vec_ref, M_GAIN, index_ref)
        sum_ref[...] = jnp.zeros_like(sum_ref)
        for r, b_ref in enumerate((b0, b1, b2, b3)):
            rows = rows_of(r)
            branch_ref[(r + 1) * pad - 16 : (r + 1) * pad] = jnp.zeros((16, width), BF)
            branch_ref[r * pad : r * pad + block] = b_ref[...]
            grad = nt(branch_ref[rows], w_ref[...])
            columns = rows_to_columns(norm_ref[r])
            unit = (a_ref[rows] - columns[:, 0:1]) * columns[:, 1:2]
            hat = grad * gain
            grad_ref[rows] = hat
            stat_ref[r] = columns_to_rows([jnp.sum(v, axis=-1, keepdims=True) for v in (hat, hat * unit)])
            lines = [jnp.sum(v, axis=0, keepdims=True) for v in (grad * unit, grad)]
            sum_ref[0:2] += jnp.concatenate(lines, axis=0)

    branch, hat_mix, stat_back, sum_mix = call(
        mix_back_body,
        [((length, width), BF), ((length, heads), F32), ((ranks, 8, pad), F32), ((8, heads), F32)],
        index, *branch_blocks, w_out, attended, norm_mix, vec, specs=[SM] + [VM] * 8, name="mix_back", us=3,
        load=(3, 4),
    )

    zs = count_d // 2

    def weight_grad(index_ref, left, rights, keep_ref, send_ref, at):
        odd = index_ref[0] % 2
        for k in range(zs):
            cols = pl.ds(pl.multiple_of(((index_ref[0] // 2) ^ k) * 2 * own_rows, 128), 2 * own_rows)
            turned = left[:, cols].T
            start = at
            for right in rights:
                both = nn(turned, right[...])
                upper, lower = both[:own_rows].astype(BF), both[own_rows:].astype(BF)
                stop = start + both.shape[1]
                keep_ref[k, :own_rows, start:stop] = jnp.where(odd == 0, upper, lower)
                send_ref[k, :own_rows, start:stop] = jnp.where(odd == 0, lower, upper)
                start = stop

    def qkv_grad_body(pair, index_ref, unit_ref, d_ref, w_ref, vec_ref, *refs):
        keep_ref, send_ref, sum_ref = refs[-3:]
        odd = index_ref[0] % 2
        d_sum = jnp.sum(d_ref[...].astype(F32), axis=0, keepdims=True)
        w_cols = slice(pair * 384, (pair + 1) * 384)
        for k in range(zs):
            cols = pl.ds(pl.multiple_of(((index_ref[0] // 2) ^ k) * 2 * own_rows, 128), 2 * own_rows)
            both = nn(unit_ref[:, cols].T, d_ref[...])
            weight = w_ref[cols, w_cols].astype(F32)
            sums = [jnp.sum(weight * both, axis=-1, keepdims=True), jnp.sum(weight * d_sum, axis=-1, keepdims=True)]
            lines = columns_to_rows(sums)
            sum_ref[:, cols] = lines + refs[0][:, cols] if len(refs) == 4 else lines
            columns = vec_ref[0:8, cols].T
            both = columns[:, F_GAIN : F_GAIN + 1] * both + columns[:, F_BIAS : F_BIAS + 1] * d_sum
            upper, lower = both[:own_rows].astype(BF), both[own_rows:].astype(BF)
            keep_ref[k] = jnp.where(odd == 0, upper, lower)
            send_ref[k] = jnp.where(odd == 0, lower, upper)

    def qkv_grad(pair, d, after, *before):
        return call(
            functools.partial(qkv_grad_body, pair), [((zs, own_rows, 384), BF)] * 2 + [((8, width), F32)],
            index, unit_one, d, w_qkv, vec, *before, specs=[SM] + [VM] * (4 + len(before)), name="qkv_grad", us=2,
            after=after, token=True,
        )

    def add_body(keep_ref, across_ref, own_ref, *send_refs):
        own_ref[...] = keep_ref[0].astype(F32) + across_ref[0].astype(F32)
        for k, ref in enumerate(send_refs):
            ref[...] = (keep_ref[k + 1].astype(F32) + across_ref[k + 1].astype(F32)).astype(BF)

    def dp_add(keep, across, name, after=()):
        return call(
            add_body, [(keep.shape[1:], F32)] + [(keep.shape[1:], BF)] * (zs - 1), keep, across, name=name, us=1,
            after=after,
        )

    def dp_column_sums(added):
        return [added[0]] + [swap(one, "dp", 2 * (k + 1)) for k, one in enumerate(added[1:])]

    shared_back = tensor_share(stat_back)
    if direct:
        def out_grad_body(index_ref, b_ref, m_ref, keep_ref, send_ref):
            weight_grad(index_ref, b_ref, [m_ref], keep_ref, send_ref, 0)

        keep_out, send_out, out_token = call(
            out_grad_body, [((zs, own_rows, heads), BF)] * 2, index, branch, mixed, specs=[SM] + [VM] * 2,
            name="out_grad", token=True,
        )
        across_out = swap(send_out, "dp", 1)
    arrived_out, _ = tensor_scatter(down_parts, after=shared_back[1:])

    def finish_body(h_ref, p0, p1, p2, vec_ref, out_ref):
        out = p0[...].astype(F32) + p1[...].astype(F32) + p2[...].astype(F32)
        out_ref[...] = (h_ref[...] + out + vec_ref[D_BIAS : D_BIAS + 1]).astype(BF)

    (layer_output,) = call(finish_body, [((block, width), BF)], hidden_state, *arrived_out, vec, name="finish")


    def three(column):
        upper = column.astype(BF).astype(F32)
        middle = (column - upper).astype(BF).astype(F32)
        return [upper, middle, column - upper - middle]

    def with_lanes(value, s, columns):
        lane = lax.broadcasted_iota(jnp.int32, (1, 128), 1)
        out = jnp.where(half_mask(s), value, 0.0)
        for j, column in enumerate(columns):
            out = jnp.where(lane == HD * (1 - s) + j, column, out)
        return out.astype(BF)

    def attend_back_body(
        pair, q_ref, k_ref, v_ref, a_ref, hat_ref, norm_ref, s0, s1, s2, s3, log_ref, line_ref, cos_ref, sin_ref,
        d_ref, sum_ref, kx_ref, qx_ref, vx_ref, gx_ref, dq_ref, dk_ref, dv_ref,
    ):
        cols = slice(pair * 128, (pair + 1) * 128)
        scale = 1.0 / math.sqrt(HD)
        for r in blocks:
            rows = rows_of(r)
            columns = rows_to_columns(norm_ref[r])
            back = rows_to_columns(summed_stats((s0, s1, s2, s3), r) / width)
            attended = a_ref[rows, cols]
            unit = (attended - columns[:, 0:1]) * columns[:, 1:2]
            grad = columns[:, 1:2] * (hat_ref[rows, cols] - back[:, 0:1] - unit * back[:, 1:2])
            grad = grad.astype(BF).astype(F32)
            mask = jnp.where(rows_to_columns(line_ref[r])[:, 0:1] == 1.0, 0.0, LOW)
            logs = rows_to_columns(log_ref[r])
            q, k, v = (ref[rows, cols].astype(F32) for ref in (q_ref, k_ref, v_ref))
            for s in range(2):
                h = 2 * pair + s
                log = three(logs[:, h : h + 1])
                delta = three(jnp.sum(jnp.where(half_mask(s), grad * attended, 0.0), axis=-1, keepdims=True))
                kx_ref[s, rows] = with_lanes(k * scale, s, [1.0, 1.0, 1.0, mask])
                qx_ref[s, rows] = with_lanes(q, s, [-log[0], -log[1], -log[2], 1.0])
                vx_ref[s, rows] = with_lanes(v, s, [1.0, 1.0, 1.0])
                gx_ref[s, rows] = with_lanes(grad, s, [-delta[0], -delta[1], -delta[2]])
        for s in range(2):
            dq_ref[s] = jnp.zeros((length, 128), F32)

            def step(b, _):
                rows = pl.ds(pl.multiple_of(b * 2 * pad, 16), 2 * pad)
                k = kx_ref[s, rows]
                probs = jnp.exp(nt(k, qx_ref[s]))
                grad_scores = (probs * nt(vx_ref[s, rows], gx_ref[s])).astype(BF)
                dv = nn(probs.astype(BF), gx_ref[s])
                dk = nn(grad_scores, qx_ref[s]) * scale
                if s == 0:
                    dv_ref[rows] = dv
                    dk_ref[rows] = dk
                else:
                    dv_ref[rows] = jnp.where(half_mask(s), dv, dv_ref[rows])
                    dk_ref[rows] = jnp.where(half_mask(s), dk, dk_ref[rows])
                dq_ref[s] += tn(grad_scores, k)
                return 0

            lax.fori_loop(0, ranks // 2, step, 0)
        sum_ref[...] = jnp.zeros_like(sum_ref)
        for r in blocks:
            rows = rows_of(r)
            c, s = cos_ref[rows], -sin_ref[rows]
            dq = turn(jnp.where(half_mask(0), dq_ref[0, rows], dq_ref[1, rows]), c, s).astype(BF)
            dv = dv_ref[rows].astype(BF)
            d_ref[rows, 0:128] = dq
            d_ref[rows, 128:256] = turn(dk_ref[rows], c, s).astype(BF)
            d_ref[rows, 256:384] = dv
            totals = [jnp.sum(t.astype(F32), axis=0, keepdims=True) for t in (dq, dv)]
            sum_ref[0:2] += jnp.concatenate(totals, axis=0)

    def attend_back(pair, after):
        return call(
            functools.partial(attend_back_body, pair), [((length, 384), BF), ((8, 128), F32)],
            queries, keys, values, attended, hat_mix, norm_mix, *shared_back, stat_mix, lines, cosine, sine,
            scratch=[pltpu.VMEM((2, length, 128), BF)] * 4
            + [pltpu.VMEM((2, length, 128), F32)] + [pltpu.VMEM((length, 128), F32)] * 2,
            name="attend_back", us=11, after=after, mib=14,
        )

    d_first, sum_first = attend_back(0, [out_token] if direct else [])
    if direct:
        sum_ffn = dp_sum_step(sum_ffn, 4, [d_first])
        added_out = dp_add(keep_out, across_out, "out_add", [d_first])
        got_out = dp_column_sums(added_out)
        keep_first, send_first, sum_one, first_token = qkv_grad(0, d_first, [added_out[1]])
    d_last, sum_last = attend_back(1, [first_token, added_out[1], layer_output, sum_ffn] if direct else [])
    if direct:
        added_first = dp_add(keep_first, swap(send_first, "dp", 1), "first_add", [d_last])
        got_first = dp_column_sums(added_first)
        keep_last, send_last, sum_one, last_token = qkv_grad(1, d_last, [added_first[1], *got_out[1:]], sum_one)
        across_last = swap(send_last, "dp", 1)

    def vector_body(index_ref, one_ref, first_ref, last_ref, mix_ref, two_ref, out_ref):
        out_ref[...] = jnp.zeros_like(out_ref)
        out_ref[0:2] = one_ref[0:2]
        cols = pl.ds(pl.multiple_of(index_ref[1] * heads, 128), heads)
        out_ref[2:4, cols] = jnp.concatenate([first_ref[0:2], last_ref[0:2]], axis=1)
        out_ref[4:6, cols] = mix_ref[0:2]
        out_ref[6:10] = two_ref[0:4]

    if not direct:
        d_all = joined([d.astype(F32) for d in (d_first.T, d_last.T)]).T
        unit_d = joined([tn(unit_one, d).T for d in (d_first, d_last)]).T
        d_sum = jnp.sum(d_all, axis=0, keepdims=True)
        sum_one = jnp.stack([jnp.sum(w_qkv * v, axis=1) for v in (unit_d, jnp.broadcast_to(d_sum, unit_d.shape))])
        sum_one = jnp.pad(sum_one, ((0, 6), (0, 0)))
    (vectors,) = call(
        vector_body, [((16, width), F32)], index, sum_one, sum_first, sum_last, sum_mix, sum_two, specs=[SM] + [VM] * 5,
        name="vectors",
    )
    shared_vectors = tensor_share(vectors)
    if direct:
        def vector_chunk_body(index_ref, v0, v1, v2, v3, keep_ref, send_ref):
            for k in range(zs):
                for ref, side in ((keep_ref, index_ref[0] % 2), (send_ref, 1 - index_ref[0] % 2)):
                    cols = pl.ds(pl.multiple_of((((index_ref[0] // 2) ^ k) * 2 + side) * own_rows, 128), own_rows)
                    ref[k] = v0[:, cols] + v1[:, cols] + v2[:, cols] + v3[:, cols]

        keep_vec, send_vec = call(
            vector_chunk_body, [((zs, 16, own_rows), F32)] * 2, index, *shared_vectors, specs=[SM] + [VM] * 4,
            name="vector_chunks",
        )

    def project_back_body(first_block, d0_ref, d1_ref, w_ref, *part_refs):
        for r in (1, 0):
            rows = rows_of(first_block + r)
            grad = nt(d0_ref[rows], w_ref[:, :384]) + nt(d1_ref[rows], w_ref[:, 384:])
            part_refs[r][...] = grad[:block].astype(BF)

    projected = [None, None]
    for j in (1, 0):
        after = [send_vec, across_last, *got_first[1:]] if j and direct else []
        projected[j] = call(
            functools.partial(project_back_body, 2 * j), [((block, width), BF)] * 2, d_first, d_last, w_qkv,
            name="project_back", us=2, after=after,
        )
    arrived, _ = tensor_scatter([*projected[0], *projected[1]])

    def input_body(p0, p1, p2, x_ref, grad_ref, vec_ref, out_ref):
        grad_first = p0[...].astype(F32) + p1[...].astype(F32) + p2[...].astype(F32)
        x = x_ref[...].astype(F32)
        mean, inverse = center_scale(x)
        unit = (x - mean) * inverse
        out_ref[:, 0, :] = grad_ref[...] + unit_back(grad_first * vec_ref[F_GAIN : F_GAIN + 1], unit, inverse)

    (input_grad,) = call(
        input_body, [((block, 1, width), F32)], *arrived, x_own, grad_hidden, vec, name="input_grad", store=(0,),
    )

    if direct:
        def last_add_body(keep_ref, across_ref, keep_vec_ref, across_vec_ref, own_ref, *send_refs):
            for k, ref in enumerate((own_ref, *send_refs)):
                ref[:own_rows] = (keep_ref[k].astype(F32) + across_ref[k].astype(F32)).astype(ref.dtype)
                ref[own_rows:] = jnp.zeros((16, 384), ref.dtype)
                ref[own_rows:, :own_rows] = (keep_vec_ref[k] + across_vec_ref[k]).astype(ref.dtype)

        got_last = dp_column_sums(call(
            last_add_body, [((own_rows + 16, 384), F32)] + [((own_rows + 16, 384), BF)] * (zs - 1),
            keep_last, across_last, keep_vec, swap(send_vec, "dp", 1), name="last_add", after=got_first[1:],
        ))

        def attn_finish_body(*refs):
            def total(parts):
                return sum(ref[...].astype(F32) for ref in parts)

            early, late = total(refs[:zs]), total(refs[zs : 2 * zs])
            q_ref, k_ref, v_ref, o_ref, model_ref = refs[3 * zs :]
            for k, ref in enumerate((q_ref, k_ref, v_ref)):
                cols = slice(k * 128, (k + 1) * 128)
                ref[:, 0:128] = early[:, cols]
                ref[:, 128:256] = late[:own_rows, cols]
            o_ref[...] = total(refs[2 * zs : 3 * zs]).T
            model_ref[...] = late[own_rows:, :own_rows]

        shapes = [(own_rows, heads)] * 3 + [(heads, own_rows), (16, own_rows)]
        q_grad, k_grad, v_grad, out_grad, model = call(
            attn_finish_body, [(shape, F32) for shape in shapes], *got_first, *got_last, *got_out, store=(0, 1, 2, 3),
            name="attn_finish",
        )
    else:
        qkv_all = vec[F_GAIN][:, None] * unit_d + vec[F_BIAS][:, None] * d_sum
        qkv_all = lax.psum_scatter(qkv_all.astype(BF), "dp", scatter_dimension=0, tiled=True).astype(F32).T
        qkv_all = qkv_all.reshape(2, 3, 128, own_rows)
        q_grad, k_grad, v_grad = (joined(list(qkv_all[:, k])).T for k in range(3))
        out_grad = plain_grad(branch, mixed).T
        model = lax.psum_scatter(sum(shared_vectors), "dp", scatter_dimension=1, tiled=True)
        sum_ffn = lax.psum(sum_ffn, "dp")
    ffn = sum_ffn[:, :hidden]
    return (
        layer_output[None], input_grad.transpose(1, 0, 2), q_grad, k_grad, v_grad,
        model[2], model[3], model[0], model[1], model[4], model[5], out_grad, model[8], model[6], model[7],
        gate_grad, up_grad, ffn[0], ffn[1], ffn[2], ffn[3], down_grad, model[9],
    )


def solution(mesh):
    rows, across, tokens = P("dp", "tensor"), P("tensor", "dp"), P("dp", "tensor", None)
    model, ffn, image = P("dp"), P("tensor"), P("dp", None)
    in_specs = (
        tokens, rows, rows, rows, model, model, model, model, model, model, across, model, model, model, rows, rows,
        ffn, ffn, ffn, ffn, across, model, tokens, image, image, image,
    )
    out_specs = (
        tokens, tokens, rows, rows, rows, model, model, model, model, model, model, across, model, model, model,
        rows, rows, ffn, ffn, ffn, ffn, across, model,
    )
    return jax.shard_map(local, mesh=mesh, in_specs=in_specs, out_specs=out_specs, check_vma=False)
```

```python
import functools
import math

import jax
import jax.numpy as jnp
from jax import lax
from jax.experimental import pallas as pl
from jax.experimental.pallas import tpu as pltpu
from jax.sharding import PartitionSpec as P

HD = 64
EPSILON = 1e-06
LOW = -1e30
BF = jnp.bfloat16
F32 = jnp.float32
HI = lax.Precision.HIGHEST
VM = pl.BlockSpec(memory_space=pltpu.VMEM)
SM = pl.BlockSpec(memory_space=pltpu.SMEM)
ANY = pl.BlockSpec(memory_space=pl.ANY)
HB = pl.BlockSpec(memory_space=pltpu.HBM)
Q_BIAS, V_BIAS, F_GAIN, F_BIAS, M_GAIN, M_BIAS, O_BIAS, S_GAIN, S_BIAS, D_BIAS = range(10)


def nn(a, b, precision=None):
    return lax.dot_general(a, b, (((1,), (0,)), ((), ())), precision, F32)


def nt(a, b, precision=None):
    return lax.dot_general(a, b, (((1,), (1,)), ((), ())), precision, F32)


def tn(a, b, precision=None):
    return lax.dot_general(a, b, (((0,), (0,)), ((), ())), precision, F32)


def call(
    body, outs, *args, specs=None, load=(), store=(), mib=8, us=1.0, name=None, after=(), scratch=(), token=False, **extra
):
    if token:
        outs = [*outs, ((8, 128), F32)]
    shapes = [jax.ShapeDtypeStruct(shape, dtype) for shape, dtype in outs]
    n_in, n_out, n_after, moved = len(args), len(outs), len(after), len(load) + len(store)
    specs = list(specs or [VM] * n_in)
    out_specs = [VM] * n_out
    for i in load:
        specs[i] = HB
    for i in store:
        out_specs[i] = HB
        shapes[i] = pltpu.HBM(*outs[i])
    args = [hbm(a) if s is HB else a for a, s in zip(args, specs)]
    held = [pltpu.VMEM(args[i].shape, args[i].dtype) for i in load] + [pltpu.VMEM(*outs[i]) for i in store]
    if moved:
        held.append(pltpu.SemaphoreType.DMA((moved,)))

    def run(*refs):
        ins, outs_ = list(refs[:n_in]), list(refs[n_in + n_after : n_in + n_after + n_out])
        rest = refs[n_in + n_after + n_out :]
        own, copies = rest[: len(scratch)], rest[len(scratch) :]
        reads = [pltpu.make_async_copy(ins[i], copies[j], copies[-1].at[j]) for j, i in enumerate(load)]
        for one in reads:
            one.start()
        for j, i in enumerate(load):
            ins[i] = copies[j]
        writes = []
        for j, i in enumerate(store, len(load)):
            writes.append(pltpu.make_async_copy(copies[j], outs_[i], copies[-1].at[j]))
            outs_[i] = copies[j]
        for one in reads:
            one.wait()
        body(*ins, *(outs_[:-1] if token else outs_), *own)
        for one in writes:
            one.start()
        for one in writes:
            one.wait()

    return pl.pallas_call(
        run,
        out_shape=shapes,
        in_specs=specs + [ANY] * n_after,
        out_specs=out_specs,
        scratch_shapes=list(scratch) + held,
        compiler_params=pltpu.CompilerParams(vmem_limit_bytes=mib << 20),
        cost_estimate=pl.CostEstimate(flops=int(us * 1.1e7), bytes_accessed=1 << 10, transcendentals=0),
        name=name,
        **extra,
    )(*args, *after)


def swap(value, axis, offset):
    count = lax.axis_size(axis)
    return lax.ppermute(value, axis, [(i, i ^ offset) for i in range(count)])


def tensor_gather(block):
    core = swap(block, "tensor", 1)
    far = swap(block, "tensor", 2)
    return [block, core, far, swap(far, "tensor", 1)]


def add_pair_body(a_ref, b_ref, out_ref):
    out_ref[...] = (a_ref[...].astype(F32) + b_ref[...].astype(F32)).astype(BF)


def tensor_scatter(parts, after=()):
    third = swap(parts[3], "tensor", 1)
    first = swap(parts[1], "tensor", 1)
    (to_far,) = call(add_pair_body, [(third.shape, BF)], parts[2], third, name="add_pair", after=after)
    return [parts[0], first, swap(to_far, "tensor", 2)], to_far


def tensor_share(value):
    return [value] + [swap(value, "tensor", k) for k in (1, 2, 3)]


def dp_column(block):
    return [block] + [swap(block, "dp", 2 * k) for k in range(1, lax.axis_size("dp") // 2)]


def dp_across(column):
    return [one for mine in column for one in (mine, swap(mine, "dp", 1))]


def hbm(value):
    return pltpu.with_memory_space_constraint(value, pltpu.HBM)


def tie(value, *others, held=False):
    def body(*refs):
        pass

    return pl.pallas_call(
        body,
        out_shape=pltpu.HBM(value.shape, value.dtype),
        in_specs=[HB] + [HB if held else ANY] * len(others),
        out_specs=HB,
        input_output_aliases={0: 0},
        cost_estimate=pl.CostEstimate(flops=1, bytes_accessed=1, transcendentals=0),
        compiler_params=pltpu.CompilerParams(vmem_limit_bytes=1 << 20),
        name="tie",
    )(hbm(value), *[hbm(v) if held else v for v in others])


def hold(values, *others):
    count = len(values)

    def body(*refs):
        refs, held, sems = refs[: -count - 1], refs[-count - 1 : -1], refs[-1]
        reads = [pltpu.make_async_copy(refs[i], held[i], sems.at[0, i]) for i in range(count)]
        writes = [pltpu.make_async_copy(held[i], refs[i - count], sems.at[1, i]) for i in range(count)]
        for one in reads:
            one.start()
        for read, write in zip(reads, writes):
            read.wait()
            write.start()
        for one in writes:
            one.wait()

    return pl.pallas_call(
        body,
        out_shape=[pltpu.HBM(v.shape, v.dtype) for v in values],
        in_specs=[ANY] * (count + len(others)),
        out_specs=[HB] * count,
        scratch_shapes=[pltpu.VMEM(v.shape, v.dtype) for v in values] + [pltpu.SemaphoreType.DMA((2, count))],
        cost_estimate=pl.CostEstimate(flops=1, bytes_accessed=1, transcendentals=0),
        compiler_params=pltpu.CompilerParams(vmem_limit_bytes=4 << 20),
        name="hold",
    )(*values, *others)


def center_scale(values):
    width = values.shape[-1]
    mean = jnp.sum(values, axis=-1, keepdims=True) / width
    spread = jnp.sum(values * values, axis=-1, keepdims=True) / width - mean * mean
    return mean, lax.rsqrt(spread + EPSILON)


def unit_back(grad_hat, unit, inverse):
    width = unit.shape[-1]
    mean = jnp.sum(grad_hat, axis=-1, keepdims=True) / width
    cross = jnp.sum(grad_hat * unit, axis=-1, keepdims=True) / width
    return inverse * (grad_hat - mean - unit * cross)


def columns_to_rows(columns):
    count = columns[0].shape[0]
    lanes = lax.broadcasted_iota(jnp.int32, (count, 128), 1)
    wide = jnp.zeros((count, 128), F32)
    for k, column in enumerate(columns):
        wide = jnp.where(lanes == k, column, wide)
    return wide.T[0:8]


def rows_to_columns(rows):
    return rows.T


def summed_stats(refs, r):
    return refs[0][r] + refs[1][r ^ 1] + refs[2][r ^ 2] + refs[3][r ^ 3]


def turn(values, cosine, sine):
    lanes = lax.broadcasted_iota(jnp.int32, values.shape, 1)
    other = jnp.where(lanes % 2 == 0, pltpu.roll(values, 127, 1), pltpu.roll(values, 1, 1))
    return values * cosine + other * sine


def half_mask(s):
    lane = lax.broadcasted_iota(jnp.int32, (1, 128), 1)
    return lane < HD if s == 0 else lane >= HD


def local(
    layer_input, query_weight, key_weight, value_weight, query_bias, value_bias, first_gain, first_bias,
    mixer_gain, mixer_bias, output_weight, output_bias, second_gain, second_bias, gate_weight, up_weight,
    gate_bias, up_bias, inner_gain, inner_bias, down_weight, down_bias, cotangent, key_valid, patch_row, patch_column,
):
    ranks = lax.axis_size("tensor")
    me_t, me_d, count_d = lax.axis_index("tensor"), lax.axis_index("dp"), lax.axis_size("dp")
    block, width = layer_input.shape[1:]
    pad = -(-block // 16) * 16
    length = ranks * pad
    heads = query_weight.shape[1]
    hidden = gate_weight.shape[1]
    hidden_pad = -(-hidden // 128) * 128
    own_rows = width // count_d
    direct = own_rows % 128 == 0 and count_d & (count_d - 1) == 0
    index = jnp.stack([me_d, me_t]).astype(jnp.int32)
    x_own, cot_own = layer_input[0], cotangent[0]
    blocks = range(ranks)

    def rows_of(r):
        return slice(r * pad, (r + 1) * pad)

    lines = jnp.stack([key_valid[0], patch_row[0], patch_column[0], jnp.arange(ranks * block, dtype=jnp.int32)])
    lines = jnp.pad(lines.reshape(4, ranks, block), ((0, 4), (0, 0), (0, pad - block))).astype(F32)
    lines = jnp.stack([lax.dynamic_index_in_dim(lines, me_t ^ r, 1, False) for r in blocks])
    lane = jnp.arange(128)
    frequency = jnp.power(F32(10000.0), -((lane % HD) // 2 % (HD // 4)).astype(F32) / (HD // 4))
    frequency = jnp.broadcast_to(frequency[None, :], (8, 128))

    def table_body(line_ref, frequency_ref, cos_ref, sin_ref):
        lanes = lax.broadcasted_iota(jnp.int32, (pad, 128), 1)
        for r in blocks:
            columns = rows_to_columns(line_ref[r])
            position = jnp.where(lanes % HD < HD // 2, columns[:, 1:2], columns[:, 2:3])
            angle = jnp.where(columns[:, 3:4] > 0.0, 0.5 * (position * frequency_ref[0:1]), 0.0)
            cos_ref[rows_of(r)] = jnp.cos(angle)
            sine = jnp.sin(angle)
            sin_ref[rows_of(r)] = jnp.where(lanes % 2 == 0, -sine, sine)

    cosine, sine = call(table_body, [((length, 128), F32)] * 2, lines, frequency, name="tables", us=4)

    small = [
        v[None, :]
        for v in (
            query_bias, value_bias, first_gain, first_bias, mixer_gain, mixer_bias, output_bias, second_gain,
            second_bias, down_bias,
        )
    ]
    tiles = heads // 128
    hidden_low = -(-hidden // 16) * 16
    starts = [(k % 3) * tiles + k // 3 for k in range(3 * tiles)]
    if direct:
        o_start = 3 * tiles * own_rows + 16

        def pack_a_body(q_ref, k_ref, v_ref, w_ref, *refs):
            *small_refs, out_ref = refs
            out_ref[o_start:] = w_ref[...]
            for k in range(3 * tiles):
                ref = (q_ref, k_ref, v_ref)[k % 3]
                out_ref[k * own_rows : (k + 1) * own_rows] = ref[:, k // 3 * 128 : (k // 3 + 1) * 128]
            lines = [ref[...].astype(F32) for ref in small_refs]
            lines.append(jnp.zeros((16 - len(lines), own_rows), F32))
            out_ref[3 * tiles * own_rows : o_start] = jnp.concatenate(lines, axis=0).astype(BF)

        (pack_a,) = call(
            pack_a_body, [((o_start + heads, 128), BF)], query_weight, key_weight, value_weight, output_weight,
            *small, name="pack_a", load=tuple(range(14)),
        )
        column_a = dp_column(pack_a)
        across_a = [swap(pack_a, "dp", 1)]
        x_far = swap(x_own, "tensor", 2)
        *column_a[1:], across_a[0], x_held, x_far = hold([*column_a[1:], *across_a, x_own, x_far], cosine)
        across_a += [swap(one, "dp", 1) for one in column_a[1:]]
        x_blocks = [x_own, swap(x_held, "tensor", 1), x_far, swap(x_far, "tensor", 1)]
        got_a = [one for pair in zip(column_a, across_a) for one in pair]

        def pack_f_body(g_ref, u_ref, d_ref, out_ref):
            for j, ref in enumerate((g_ref, u_ref, d_ref)):
                out_ref[(j + 1) * hidden_low - 16 : (j + 1) * hidden_low] = jnp.zeros((16, own_rows), BF)
                out_ref[j * hidden_low : j * hidden_low + hidden] = ref[...]

        (pack_f,) = call(
            pack_f_body, [((3 * hidden_low, own_rows), BF)], gate_weight.T, up_weight.T, down_weight, name="pack_f",
            load=(0, 1, 2),
        )
        got_f = lax.all_gather(tie(pack_f, column_a[3], held=True), "dp")
        def copies(pairs, sems):
            started = [pltpu.make_async_copy(a, b, sems.at[i]) for i, (a, b) in enumerate(pairs)]
            for one in started:
                one.start()
            for one in started:
                one.wait()

        def chunk_at(index_ref, r):
            return pl.ds(pl.multiple_of((index_ref[0] ^ r) * own_rows, 128), own_rows)

        def assemble_a(index_ref, *refs):
            *chunks, cot_ref = refs[: count_d + 1]
            w_ref, v_ref, o_ref, cot_out, small_ref, held_ref, sems, cot_sems = refs[count_d + 1 :]
            cot_read = pltpu.make_async_copy(cot_ref, held_ref, cot_sems.at[0])
            cot_write = pltpu.make_async_copy(held_ref, cot_out, cot_sems.at[1])
            cot_read.start()
            pairs = []
            for r, chunk in enumerate(chunks):
                for k in range(3 * tiles):
                    pairs.append((
                        chunk.at[k * own_rows : (k + 1) * own_rows],
                        w_ref.at[chunk_at(index_ref, r), k * 128 : (k + 1) * 128],
                    ))
                pairs.append((chunk.at[3 * tiles * own_rows : o_start], small_ref.at[r]))
                pairs.append((chunk.at[o_start:], o_ref.at[:, chunk_at(index_ref, r)]))
            started = [pltpu.make_async_copy(a, b, sems.at[i]) for i, (a, b) in enumerate(pairs)]
            for one in started:
                one.start()
            cot_read.wait()
            cot_write.start()
            for one in started:
                one.wait()
            for r in range(count_d):
                v_ref[:, chunk_at(index_ref, r)] = small_ref[r].astype(F32)
            cot_write.wait()

        specs = [SM] + [HB] * count_d

        def dma(count):
            return pltpu.SemaphoreType.DMA((count,))

        shapes = [((width, 3 * heads), BF), ((16, width), F32), ((heads, width), BF), (cot_own.shape, BF)]
        w_qkv, vec, w_out, cot_held = pl.pallas_call(
            assemble_a,
            out_shape=[jax.ShapeDtypeStruct(*shape) for shape in shapes[:3]] + [pltpu.HBM(*shapes[3])],
            in_specs=specs + [HB],
            out_specs=[VM] * 3 + [HB],
            scratch_shapes=[
                pltpu.VMEM((count_d, 16, 128), BF), pltpu.VMEM(*shapes[3]), dma(count_d * (3 * tiles + 2)), dma(2)
            ],
            compiler_params=pltpu.CompilerParams(vmem_limit_bytes=4 << 20),
            cost_estimate=pl.CostEstimate(flops=1 << 10, bytes_accessed=1 << 10, transcendentals=0),
            name="assemble_a",
        )(index, *[hbm(v) for v in got_a], hbm(cot_own))
        cot_blocks = tensor_gather(cot_held)
    else:
        def whole(weight, axis):
            return lax.all_gather(weight, "dp", axis=axis, tiled=True)

        x_blocks = tensor_gather(x_own)
        cot_blocks = tensor_gather(cot_own)
        w_qkv = whole(jnp.concatenate(
            [(query_weight, key_weight, value_weight)[k % 3][:, k // 3 * 128 : (k // 3 + 1) * 128] for k in range(3 * tiles)],
            axis=1,
        ), 0)
        vec = jnp.pad(whole(jnp.concatenate(small), 1).astype(F32), ((0, 6), (0, 0)))
        w_out = whole(output_weight, 1)
        w_gate, w_up, w_down = (
            jnp.pad(whole(w, 1), ((0, hidden_pad - hidden), (0, 0))) for w in (gate_weight.T, up_weight.T, down_weight)
        )
    ffn_vec = jnp.pad(
        jnp.stack([gate_bias, up_bias, inner_gain, inner_bias]).astype(F32), ((0, 4), (0, hidden_pad - hidden))
    )

    def own(ref, k, index_ref):
        return ref[k : k + 1, pl.ds(pl.multiple_of(index_ref[1] * heads, 128), heads)]

    n_heads = heads // HD

    def attend_body(
        index_ref, x0, x1, x2, x3, w_ref, vec_ref, cos_ref, sin_ref, line_ref,
        unit_out, q_out, k_out, v_out, o_ref, stat_ref, unit_ref, q_ref, k_ref, v_ref, first_ref, x_ref, cos_held,
        sin_held, sems, load_sems,
    ):
        pairs = [(x0, x_ref.at[0]), (x2, x_ref.at[1]), (cos_ref, cos_held), (sin_ref, sin_held)]
        reads = [pltpu.make_async_copy(a, b, load_sems.at[i]) for i, (a, b) in enumerate(pairs)]
        for one in reads:
            one.start()
        gain, bias = vec_ref[F_GAIN : F_GAIN + 1], vec_ref[F_BIAS : F_BIAS + 1]
        q_bias, v_bias = own(vec_ref, Q_BIAS, index_ref), own(vec_ref, V_BIAS, index_ref)
        moves = []
        for r in blocks:
            if r % 2 == 0:
                reads[r // 2].wait()
            x = (x_ref[0] if r == 0 else x1[...] if r == 1 else x_ref[1] if r == 2 else x3[...]).astype(F32)
            mean, inverse = center_scale(x)
            unit = (x - mean) * inverse
            unit_ref[(r + 1) * pad - 16 : (r + 1) * pad] = jnp.zeros((16, width), BF)
            unit_ref[r * pad : r * pad + block] = unit.astype(BF)
            first_ref[pad - 16 :] = jnp.zeros((16, width), BF)
            first_ref[:block] = (unit * gain + bias).astype(BF)
            rows = rows_of(r)
            qkv = nn(first_ref[...], w_ref[...])
            if r == 0:
                reads[2].wait()
                reads[3].wait()
            c, s = cos_held[rows], sin_held[rows]
            for k in range(tiles):
                cols = slice(k * 128, (k + 1) * 128)
                q, key, v = (qkv[:, (3 * k + j) * 128 : (3 * k + j + 1) * 128] for j in range(3))
                q_ref[rows, cols] = turn(q + q_bias[:, cols], c, s).astype(BF)
                k_ref[rows, cols] = turn(key, c, s).astype(BF)
                v_ref[rows, cols] = (v + v_bias[:, cols]).astype(BF)
            for j, (held, out) in enumerate(
                ((unit_ref, unit_out), (q_ref, q_out), (k_ref, k_out), (v_ref, v_out))
            ):
                moves.append(pltpu.make_async_copy(held.at[rows], out.at[rows], sems.at[4 * r + j]))
                moves[-1].start()
        mask_line = jnp.concatenate([jnp.where(line_ref[r][0:1] == 1.0, 0.0, LOW) for r in blocks], axis=1)
        k_half, v_half = [], []
        for h in range(n_heads):
            cols = slice(h // 2 * 128, (h // 2 + 1) * 128)
            k_half.append(jnp.where(half_mask(h % 2), k_ref[:, cols], 0).astype(BF))
            v_half.append(jnp.where(half_mask(h % 2), v_ref[:, cols], 0).astype(BF))

        def step(b, _):
            rows = pl.ds(pl.multiple_of(b * pad, 16), pad)
            kept = []
            total = jnp.zeros((pad, 1), F32)
            square = jnp.zeros((pad, 1), F32)
            for pair in range(tiles):
                cols = slice(pair * 128, (pair + 1) * 128)
                q = q_ref[rows, cols]
                out = jnp.zeros((pad, 128), F32)
                for s in range(2):
                    h = 2 * pair + s
                    scores = nt(q, k_half[h]) * (1.0 / math.sqrt(HD)) + mask_line
                    top = jnp.max(scores, axis=-1, keepdims=True)
                    terms = jnp.exp(scores - top)
                    below = jnp.sum(terms, axis=-1, keepdims=True)
                    out += nn(terms.astype(BF), v_half[h]) * (1.0 / below)
                    kept.append(top + jnp.log(below))
                o_ref[rows, cols] = out
                total += jnp.sum(out, axis=-1, keepdims=True)
                square += jnp.sum(out * out, axis=-1, keepdims=True)
            stat_ref[b] = columns_to_rows(kept + [total, square])
            return 0

        lax.fori_loop(0, ranks, step, 0)
        for one in moves:
            one.wait()

    shapes = [((length, width), BF)] + [((length, heads), BF)] * 3
    unit_one, queries, keys, values, attended, stat_mix = pl.pallas_call(
        attend_body,
        out_shape=[pltpu.HBM(*shape) for shape in shapes]
        + [jax.ShapeDtypeStruct((length, heads), F32), jax.ShapeDtypeStruct((ranks, 8, pad), F32)],
        in_specs=[SM] + [HB, VM] * 2 + [VM] * 2 + [HB] * 2 + [VM],
        out_specs=[HB] * 4 + [VM] * 2,
        scratch_shapes=[pltpu.VMEM(*shape) for shape in shapes]
        + [pltpu.VMEM((pad, width), BF), pltpu.VMEM((2, block, width), BF)]
        + [pltpu.VMEM((length, 128), F32)] * 2
        + [pltpu.SemaphoreType.DMA((4 * ranks,)), pltpu.SemaphoreType.DMA((4,))],
        compiler_params=pltpu.CompilerParams(vmem_limit_bytes=22 << 20),
        cost_estimate=pl.CostEstimate(flops=1 << 17, bytes_accessed=1 << 10, transcendentals=0),
        name="attend",
    )(index, hbm(x_blocks[0]), x_blocks[1], hbm(x_blocks[2]), x_blocks[3], w_qkv, vec, hbm(cosine), hbm(sine), lines)
    shared_mix = tensor_share(stat_mix)

    def mix_body(index_ref, a_ref, s0, s1, s2, s3, w_ref, vec_ref, mixed_ref, norm_ref, *part_refs):
        gain, bias = own(vec_ref, M_GAIN, index_ref), own(vec_ref, M_BIAS, index_ref)
        for r in reversed(blocks):
            rows = rows_of(r)
            sums = summed_stats((s0, s1, s2, s3), r)
            mean = sums[n_heads : n_heads + 1] / width
            inverse = lax.rsqrt(sums[n_heads + 1 : n_heads + 2] / width - mean * mean + EPSILON)
            lines = jnp.concatenate([mean, inverse, jnp.zeros((6, pad), F32)], axis=0)
            norm_ref[r] = lines
            columns = rows_to_columns(lines)
            mixed = ((a_ref[rows] - columns[:, 0:1]) * columns[:, 1:2] * gain + bias).astype(BF)
            mixed_ref[rows] = mixed
            part_refs[r][...] = nn(mixed, w_ref[...])[:block].astype(BF)

    mixed, norm_mix, *parts = call(
        mix_body, [((length, heads), BF), ((ranks, 8, pad), F32)] + [((block, width), BF)] * ranks,
        index, attended, *shared_mix, w_out, vec, specs=[SM] + [VM] * 7, name="mix", us=2.5,
        store=(0,), after=[cot_blocks[2]],
    )
    arrived, _ = tensor_scatter(parts)

    def second_body(x_ref, p0, p1, p2, vec_ref, hidden_ref, second_ref):
        out = p0[...].astype(F32) + p1[...].astype(F32) + p2[...].astype(F32)
        state = x_ref[...].astype(F32) + out + vec_ref[O_BIAS : O_BIAS + 1]
        hidden_ref[...] = state
        mean, inverse = center_scale(state)
        unit = (state - mean) * inverse
        second_ref[...] = (unit * vec_ref[S_GAIN : S_GAIN + 1] + vec_ref[S_BIAS : S_BIAS + 1]).astype(BF)

    hidden_state, second_own = call(
        second_body, [((block, width), F32), ((block, width), BF)], x_own, *arrived, vec, name="second", store=(0, 1),
    )
    half = 2 * pad

    def half_rows(r):
        return slice(r % 2 * pad, (r % 2 + 1) * pad)

    def pad_block(ref, r, value):
        start = r * pad
        ref[start + pad - 16 : start + pad] = jnp.zeros((16, width), BF)
        ref[start : start + block] = value

    def expand(b_refs, wg_ref, wu_ref, vec_ref, grad_ref, second_ref, gate_ref, up_ref, stat_ref, base):
        for r, b_ref in enumerate(b_refs):
            rows = half_rows(r)
            pad_block(second_ref, r, b_ref[...])
            gate = nt(second_ref[rows], wg_ref[...]) + vec_ref[0:1]
            up = nt(second_ref[rows], wu_ref[...]) + vec_ref[1:2]
            gate_ref[rows] = gate
            up_ref[rows] = up
            activated = gate * jax.nn.sigmoid(gate) * up
            hat = grad_ref[rows] * vec_ref[2:3]
            stat_ref[base + r] = columns_to_rows(
                [jnp.sum(v, axis=-1, keepdims=True) for v in (activated, activated * activated, hat, hat * activated)]
            )

    def expand_first_body(c0, c1, c2, c3, b0, b1, vec_ref, *refs):
        if direct:
            chunks, *refs, down_sems, gate_sems = refs
            wg_ref, wu_ref, wd_ref = refs[:3]
            outs = refs[3:]
            moves = []
            for j, (out, sems) in enumerate(((wd_ref, down_sems), (wg_ref, gate_sems), (wu_ref, gate_sems))):
                for a in range(count_d):
                    start = (2, 0, 1)[j] * hidden_low
                    moves.append(pltpu.make_async_copy(
                        chunks.at[a, start : start + hidden_low],
                        out.at[0:hidden_low, a * own_rows : (a + 1) * own_rows],
                        sems.at[a if j < 2 else count_d + a],
                    ))
                    moves[-1].start()
            for out in (wg_ref, wu_ref, wd_ref):
                out[hidden_low:] = jnp.zeros((hidden_pad - hidden_low, width), BF)
            for one in moves[:count_d]:
                one.wait()
        else:
            wg_ref, wu_ref, wd_ref = refs[:3]
            outs = refs[3:]
        cot0, cot1, grad0, grad1, second_ref, gate_ref, up_ref, stat_ref = outs
        for r, c_ref in enumerate((c0, c1, c2, c3)):
            cot_ref, grad_ref = ((cot0, grad0), (cot1, grad1))[r // 2]
            pad_block(cot_ref, r % 2, c_ref[...])
            grad_ref[half_rows(r)] = nt(cot_ref[half_rows(r)], wd_ref[...])
        if direct:
            for one in moves[count_d:]:
                one.wait()
        expand((b0, b1), wg_ref, wu_ref, vec_ref, grad0, second_ref, gate_ref, up_ref, stat_ref, 0)

    half_outs = [((half, width), BF)] + [((half, hidden_pad), F32)] * 2
    second_far = swap(second_own, "tensor", 2)
    blocks_in = [*cot_blocks, second_own, swap(second_own, "tensor", 1), ffn_vec]
    outs = [((half, width), BF)] * 2 + [((half, hidden_pad), F32)] * 2 + half_outs + [((2, 8, pad), F32)]
    weights = [((hidden_pad, width), BF)] * 3
    if direct:
        w_gate, w_up, w_down, *made = call(
            expand_first_body, weights + outs, *blocks_in, got_f, specs=[VM] * 7 + [HB], name="expand_first",
            scratch=[dma(count_d), dma(2 * count_d)], us=10, load=tuple(range(6)),
        )
    else:
        made = call(expand_first_body, outs, *blocks_in, w_gate, w_up, w_down, name="expand_first", us=10)
    cot_halves, grad_inner, first_half = made[:2], made[2:4], made[4:]

    def expand_body(b0, b1, wg_ref, wu_ref, vec_ref, grad_ref, before_ref, second_ref, gate_ref, up_ref, stat_ref):
        stat_ref[0:2] = before_ref[...]
        expand((b0, b1), wg_ref, wu_ref, vec_ref, grad_ref, second_ref, gate_ref, up_ref, stat_ref, 2)

    second_far = tie(second_far, first_half[3])
    expanded = [first_half, call(
        expand_body, half_outs + [((4, 8, pad), F32)], second_far, swap(second_far, "tensor", 1), w_gate, w_up, ffn_vec,
        grad_inner[1], first_half[3], name="expand", us=3.7, load=(0,),
    )]
    shared_ffn = tensor_share(expanded[1][3])

    def ffn_back_body(
        first_block, g_ref, u_ref, grad_ref, s0, s1, s2, s3, vec_ref, wg_ref, wu_ref, *refs
    ):
        dg_ref, du_ref, inner_ref, sum_ref, *part_refs = refs[-6:]
        wide = hidden * ranks
        sum_ref[...] = refs[0][...] if len(refs) == 7 else jnp.zeros_like(sum_ref)
        for r in (1, 0):
            rows = half_rows(r)
            sums = summed_stats((s0, s1, s2, s3), first_block + r)
            mean = sums[0:1] / wide
            inverse = lax.rsqrt(sums[1:2] / wide - mean * mean + EPSILON)
            grad_mean = sums[2:3] / wide
            cross = inverse * (sums[3:4] / wide - mean * grad_mean)
            columns = rows_to_columns(
                jnp.concatenate([mean, inverse, grad_mean, cross, jnp.zeros((4, pad), F32)], axis=0)
            )
            mean, inverse, grad_mean, cross = (columns[:, k : k + 1] for k in range(4))
            gate, up, grad = g_ref[rows], u_ref[rows], grad_ref[rows]
            sigmoid = jax.nn.sigmoid(gate)
            silu = gate * sigmoid
            unit = (silu * up - mean) * inverse
            inner_ref[rows] = (unit * vec_ref[2:3] + vec_ref[3:4]).astype(BF)
            grad_act = inverse * (grad * vec_ref[2:3] - grad_mean - unit * cross)
            d_gate = (grad_act * up * sigmoid * (1.0 + gate - silu)).astype(BF)
            d_up = (grad_act * silu).astype(BF)
            dg_ref[rows] = d_gate
            du_ref[rows] = d_up
            totals = [d_gate.astype(F32), d_up.astype(F32), grad * unit, grad]
            sum_ref[0:4] += jnp.concatenate([jnp.sum(v, axis=0, keepdims=True) for v in totals], axis=0)
            part_refs[r][...] = (nn(d_gate, wg_ref[...]) + nn(d_up, wu_ref[...]))[:block].astype(BF)

    backed = [None, None]
    for j in (1, 0):
        before = [backed[1][3]] if j == 0 else []
        backed[j] = call(
            functools.partial(ffn_back_body, 2 * j),
            [((half, hidden_pad), BF)] * 3 + [((8, hidden_pad), F32)] + [((block, width), BF)] * 2,
            *expanded[j][1:3], grad_inner[j], *shared_ffn, ffn_vec, w_gate, w_up, *before, name="ffn_back", us=5.5,
            store=() if j else (4, 5),
        )
    sum_ffn = backed[0][3]
    arrived, to_far = tensor_scatter([*backed[0][4:], *backed[1][4:]])

    def dp_sum_step(total, k, after):
        def body(a_ref, b_ref, out_ref):
            out_ref[...] = a_ref[...] + b_ref[...]

        return call(body, [(total.shape, F32)], total, swap(total, "dp", k), name="dp_sum", after=after)[0]

    if direct:
        rows_f = 3 * hidden_low

        def ffn_grad_body(g0, g1, u0, u1, i0, i1, e0, e1, c0, c1, after_ref, out_ref, token_ref, made_ref, sems):
            moves = []
            for j, (rights, lefts) in enumerate((((g0, g1), (e0, e1)), ((u0, u1), (e0, e1)), ((i0, i1), (c0, c1)))):
                for at in range(0, hidden_low, 256):
                    stop = min(at + 256, hidden_low)
                    cols = slice(at, min(at + 256, hidden_pad))
                    total = sum(tn(a[:, cols], b[...]) for a, b in zip(rights, lefts)).astype(BF)
                    for d in range(count_d):
                        made_ref[d, j * hidden_low + at : j * hidden_low + stop] = (
                            total[: stop - at, d * own_rows : (d + 1) * own_rows]
                        )
                    rows = slice(j * hidden_low + at, j * hidden_low + stop)
                    moves.append(pltpu.make_async_copy(made_ref.at[:, rows], out_ref.at[:, rows], sems.at[len(moves)]))
                    moves[-1].start()
            for one in moves:
                one.wait()

        shape = ((count_d, rows_f, own_rows), BF)
        pieces = 3 * -(-hidden_low // 256)
        ffn_grads, ffn_token = pl.pallas_call(
            ffn_grad_body,
            out_shape=[pltpu.HBM(*shape), jax.ShapeDtypeStruct((8, 128), F32)],
            in_specs=[VM] * 10 + [ANY],
            out_specs=[HB, VM],
            scratch_shapes=[pltpu.VMEM(*shape), pltpu.SemaphoreType.DMA((pieces,))],
            compiler_params=pltpu.CompilerParams(vmem_limit_bytes=10 << 20),
            cost_estimate=pl.CostEstimate(flops=1 << 17, bytes_accessed=1 << 10, transcendentals=0),
            name="ffn_grad",
        )(
            *(backed[j][k] for k in (0, 1, 2) for j in range(2)), expanded[0][0], expanded[1][0], *cot_halves, to_far
        )
        ffn_grads = ffn_grads.reshape(count_d * rows_f, own_rows)
        ffn_grads = tie(ffn_grads, arrived[2])
        got_ffn = lax.psum_scatter(ffn_grads, "dp", scatter_dimension=0, tiled=True)

        def ffn_finish_body(p_ref, *out_refs):
            for j, ref in enumerate(out_refs):
                ref[...] = p_ref[j * hidden_low : j * hidden_low + hidden].astype(F32)

        gate_grad, up_grad, down_grad, finished_token = call(
            ffn_finish_body, [((hidden, own_rows), F32)] * 3, got_ffn, store=(0, 1, 2), load=(0,), name="ffn_finish",
            token=True,
        )
        gate_grad, up_grad = gate_grad.T, up_grad.T
    else:
        def plain_grad(left, right):
            return lax.psum_scatter(tn(left, right).astype(BF), "dp", scatter_dimension=0, tiled=True).astype(F32)

        def joined(pair):
            return jnp.concatenate(pair)

        second_all = joined([expanded[j][0] for j in range(2)])
        down_grad = plain_grad(joined(cot_halves), joined([backed[j][2] for j in range(2)]))[:, :hidden].T
        gate_grad = plain_grad(second_all, joined([backed[j][0] for j in range(2)]))[:, :hidden]
        up_grad = plain_grad(second_all, joined([backed[j][1] for j in range(2)]))[:, :hidden]

    def hidden_back_body(p0, p1, p2, h_ref, cot_ref, vec_ref, grad_ref, branch_ref, sum_ref):
        grad_second = p0[...].astype(F32) + p1[...].astype(F32) + p2[...].astype(F32)
        mean, inverse = center_scale(h_ref[...])
        unit = (h_ref[...] - mean) * inverse
        cot = cot_ref[...].astype(F32)
        grad = cot + unit_back(grad_second * vec_ref[S_GAIN : S_GAIN + 1], unit, inverse)
        branch = grad.astype(BF)
        grad_ref[...] = grad
        branch_ref[...] = branch
        lines = [grad_second * unit, grad_second, branch.astype(F32), cot]
        lines = [jnp.sum(v, axis=0, keepdims=True) for v in lines]
        sum_ref[...] = jnp.concatenate(lines + [jnp.zeros((4, width), F32)], axis=0)

    grad_hidden, branch_own, sum_two = call(
        hidden_back_body, [((block, width), F32), ((block, width), BF), ((8, width), F32)],
        *arrived, hidden_state, cot_own, vec, name="hidden_back", after=[ffn_token] if direct else [],
        store=(0,), load=(0, 2, 3, 4),
    )

    def down_body(i0, i1, w_ref, *part_refs):
        for r in reversed(blocks):
            part_refs[r][...] = nn((i0, i1)[r // 2][half_rows(r)], w_ref[...])[:block].astype(BF)

    if direct:
        sum_ffn = dp_sum_step(sum_ffn, 1, [branch_own])
    *down_parts, down_token = call(
        down_body, [((block, width), BF)] * ranks, backed[0][2], backed[1][2], w_down, name="down", us=2.5, token=True,
        after=[sum_ffn],
    )
    branch_far = swap(branch_own, "tensor", 2)
    branch_core = swap(branch_own, "tensor", 1)
    if direct:
        sum_ffn = dp_sum_step(sum_ffn, 2, [down_token])
    branch_far = tie(branch_far, sum_ffn)
    branch_blocks = [branch_own, branch_core, branch_far, swap(branch_far, "tensor", 1)]

    def mix_back_body(index_ref, b0, b1, b2, b3, w_ref, a_ref, norm_ref, vec_ref, branch_ref, grad_ref, stat_ref, sum_ref):
        gain = own(vec_ref, M_GAIN, index_ref)
        sum_ref[...] = jnp.zeros_like(sum_ref)
        for r, b_ref in enumerate((b0, b1, b2, b3)):
            rows = rows_of(r)
            branch_ref[(r + 1) * pad - 16 : (r + 1) * pad] = jnp.zeros((16, width), BF)
            branch_ref[r * pad : r * pad + block] = b_ref[...]
            grad = nt(branch_ref[rows], w_ref[...])
            columns = rows_to_columns(norm_ref[r])
            unit = (a_ref[rows] - columns[:, 0:1]) * columns[:, 1:2]
            hat = grad * gain
            grad_ref[rows] = hat
            stat_ref[r] = columns_to_rows([jnp.sum(v, axis=-1, keepdims=True) for v in (hat, hat * unit)])
            lines = [jnp.sum(v, axis=0, keepdims=True) for v in (grad * unit, grad)]
            sum_ref[0:2] += jnp.concatenate(lines, axis=0)

    branch, hat_mix, stat_back, sum_mix = call(
        mix_back_body,
        [((length, width), BF), ((length, heads), F32), ((ranks, 8, pad), F32), ((8, heads), F32)],
        index, *branch_blocks, w_out, attended, norm_mix, vec, specs=[SM] + [VM] * 8, name="mix_back", us=3,
        load=(3,),
    )

    zs = count_d // 2

    def weight_grad(index_ref, left, rights, keep_ref, send_ref, at):
        odd = index_ref[0] % 2
        for k in range(zs):
            cols = pl.ds(pl.multiple_of(((index_ref[0] // 2) ^ k) * 2 * own_rows, 128), 2 * own_rows)
            turned = left[:, cols].T
            start = at
            for right in rights:
                both = nn(turned, right[...])
                upper, lower = both[:own_rows].astype(BF), both[own_rows:].astype(BF)
                stop = start + both.shape[1]
                keep_ref[k, :own_rows, start:stop] = jnp.where(odd == 0, upper, lower)
                send_ref[k, :own_rows, start:stop] = jnp.where(odd == 0, lower, upper)
                start = stop

    def qkv_grad_body(pair, index_ref, unit_ref, d_ref, w_ref, vec_ref, *refs):
        keep_ref, send_ref, sum_ref = refs[-3:]
        odd = index_ref[0] % 2
        d_sum = jnp.sum(d_ref[...].astype(F32), axis=0, keepdims=True)
        w_cols = slice(pair * 384, (pair + 1) * 384)
        for k in range(zs):
            cols = pl.ds(pl.multiple_of(((index_ref[0] // 2) ^ k) * 2 * own_rows, 128), 2 * own_rows)
            both = nn(unit_ref[:, cols].T, d_ref[...])
            weight = w_ref[cols, w_cols].astype(F32)
            sums = [jnp.sum(weight * both, axis=-1, keepdims=True), jnp.sum(weight * d_sum, axis=-1, keepdims=True)]
            lines = columns_to_rows(sums)
            sum_ref[:, cols] = lines + refs[0][:, cols] if len(refs) == 4 else lines
            columns = vec_ref[0:8, cols].T
            both = columns[:, F_GAIN : F_GAIN + 1] * both + columns[:, F_BIAS : F_BIAS + 1] * d_sum
            upper, lower = both[:own_rows].astype(BF), both[own_rows:].astype(BF)
            keep_ref[k] = jnp.where(odd == 0, upper, lower)
            send_ref[k] = jnp.where(odd == 0, lower, upper)

    def qkv_grad(pair, d, after, *before):
        return call(
            functools.partial(qkv_grad_body, pair), [((zs, own_rows, 384), BF)] * 2 + [((8, width), F32)],
            index, unit_one, d, w_qkv, vec, *before, specs=[SM] + [VM] * (4 + len(before)), name="qkv_grad", us=2,
            after=after, token=True,
        )

    def add_body(keep_ref, across_ref, own_ref, *send_refs):
        own_ref[...] = keep_ref[0].astype(F32) + across_ref[0].astype(F32)
        for k, ref in enumerate(send_refs):
            ref[...] = (keep_ref[k + 1].astype(F32) + across_ref[k + 1].astype(F32)).astype(BF)

    def dp_add(keep, across, name, after=()):
        return call(
            add_body, [(keep.shape[1:], F32)] + [(keep.shape[1:], BF)] * (zs - 1), keep, across, name=name, us=1,
            after=after,
        )

    def dp_column_sums(added):
        return [added[0]] + [swap(one, "dp", 2 * (k + 1)) for k, one in enumerate(added[1:])]

    shared_back = tensor_share(stat_back)
    if direct:
        def out_grad_body(index_ref, b_ref, m_ref, keep_ref, send_ref):
            weight_grad(index_ref, b_ref, [m_ref], keep_ref, send_ref, 0)

        keep_out, send_out, out_token = call(
            out_grad_body, [((zs, own_rows, heads), BF)] * 2, index, branch, mixed, specs=[SM] + [VM] * 2,
            name="out_grad", token=True,
        )
        across_out = swap(send_out, "dp", 1)
    arrived_out, _ = tensor_scatter(down_parts, after=shared_back[1:])

    def finish_body(h_ref, p0, p1, p2, vec_ref, out_ref):
        out = p0[...].astype(F32) + p1[...].astype(F32) + p2[...].astype(F32)
        out_ref[...] = (h_ref[...] + out + vec_ref[D_BIAS : D_BIAS + 1]).astype(BF)

    layer_output, finish_token = call(
        finish_body, [((block, width), BF)], hidden_state, *arrived_out, vec, name="finish", store=(0,), token=True
    )


    def three(column):
        upper = column.astype(BF).astype(F32)
        middle = (column - upper).astype(BF).astype(F32)
        return [upper, middle, column - upper - middle]

    def with_lanes(value, s, columns):
        lane = lax.broadcasted_iota(jnp.int32, (1, 128), 1)
        out = jnp.where(half_mask(s), value, 0.0)
        for j, column in enumerate(columns):
            out = jnp.where(lane == HD * (1 - s) + j, column, out)
        return out.astype(BF)

    def attend_back_body(
        pair, q_ref, k_ref, v_ref, a_ref, hat_ref, norm_ref, s0, s1, s2, s3, log_ref, line_ref, cos_ref, sin_ref,
        d_ref, sum_ref, kx_ref, qx_ref, vx_ref, gx_ref, dq_ref, dk_ref, dv_ref,
    ):
        cols = slice(pair * 128, (pair + 1) * 128)
        scale = 1.0 / math.sqrt(HD)
        for r in blocks:
            rows = rows_of(r)
            columns = rows_to_columns(norm_ref[r])
            back = rows_to_columns(summed_stats((s0, s1, s2, s3), r) / width)
            attended = a_ref[rows, cols]
            unit = (attended - columns[:, 0:1]) * columns[:, 1:2]
            grad = columns[:, 1:2] * (hat_ref[rows, cols] - back[:, 0:1] - unit * back[:, 1:2])
            grad = grad.astype(BF).astype(F32)
            mask = jnp.where(rows_to_columns(line_ref[r])[:, 0:1] == 1.0, 0.0, LOW)
            logs = rows_to_columns(log_ref[r])
            q, k, v = (ref[rows, cols].astype(F32) for ref in (q_ref, k_ref, v_ref))
            for s in range(2):
                h = 2 * pair + s
                log = three(logs[:, h : h + 1])
                delta = three(jnp.sum(jnp.where(half_mask(s), grad * attended, 0.0), axis=-1, keepdims=True))
                kx_ref[s, rows] = with_lanes(k * scale, s, [1.0, 1.0, 1.0, mask])
                qx_ref[s, rows] = with_lanes(q, s, [-log[0], -log[1], -log[2], 1.0])
                vx_ref[s, rows] = with_lanes(v, s, [1.0, 1.0, 1.0])
                gx_ref[s, rows] = with_lanes(grad, s, [-delta[0], -delta[1], -delta[2]])
        for s in range(2):
            dq_ref[s] = jnp.zeros((length, 128), F32)

            def step(b, _):
                rows = pl.ds(pl.multiple_of(b * 2 * pad, 16), 2 * pad)
                k = kx_ref[s, rows]
                probs = jnp.exp(nt(k, qx_ref[s]))
                grad_scores = (probs * nt(vx_ref[s, rows], gx_ref[s])).astype(BF)
                dv = nn(probs.astype(BF), gx_ref[s])
                dk = nn(grad_scores, qx_ref[s]) * scale
                if s == 0:
                    dv_ref[rows] = dv
                    dk_ref[rows] = dk
                else:
                    dv_ref[rows] = jnp.where(half_mask(s), dv, dv_ref[rows])
                    dk_ref[rows] = jnp.where(half_mask(s), dk, dk_ref[rows])
                dq_ref[s] += tn(grad_scores, k)
                return 0

            lax.fori_loop(0, ranks // 2, step, 0)
        sum_ref[...] = jnp.zeros_like(sum_ref)
        for r in blocks:
            rows = rows_of(r)
            c, s = cos_ref[rows], -sin_ref[rows]
            dq = turn(jnp.where(half_mask(0), dq_ref[0, rows], dq_ref[1, rows]), c, s).astype(BF)
            dv = dv_ref[rows].astype(BF)
            d_ref[rows, 0:128] = dq
            d_ref[rows, 128:256] = turn(dk_ref[rows], c, s).astype(BF)
            d_ref[rows, 256:384] = dv
            totals = [jnp.sum(t.astype(F32), axis=0, keepdims=True) for t in (dq, dv)]
            sum_ref[0:2] += jnp.concatenate(totals, axis=0)

    def attend_back(pair, after):
        return call(
            functools.partial(attend_back_body, pair), [((length, 384), BF), ((8, 128), F32)],
            queries, keys, values, attended, hat_mix, norm_mix, *shared_back, stat_mix, lines, cosine, sine,
            scratch=[pltpu.VMEM((2, length, 128), BF)] * 4
            + [pltpu.VMEM((2, length, 128), F32)] + [pltpu.VMEM((length, 128), F32)] * 2,
            name="attend_back", us=11, after=after, mib=14,
        )

    d_first, sum_first = attend_back(0, [out_token] if direct else [])
    if direct:
        added_out = dp_add(keep_out, across_out, "out_add", [d_first])
        got_out = dp_column_sums(added_out)
        keep_first, send_first, sum_one, first_token = qkv_grad(0, d_first, [added_out[1]])
    d_last, sum_last = attend_back(1, [first_token, added_out[1], finish_token] if direct else [])
    if direct:
        added_first = dp_add(keep_first, swap(send_first, "dp", 1), "first_add", [d_last])
        got_first = dp_column_sums(added_first)
        sum_ffn = dp_sum_step(sum_ffn, 4, [d_last])
        keep_last, send_last, sum_one, last_token = qkv_grad(
            1, d_last, [added_first[1], *got_out[1:], sum_ffn], sum_one
        )
        across_last = swap(send_last, "dp", 1)

    def vector_body(index_ref, one_ref, first_ref, last_ref, mix_ref, two_ref, out_ref):
        out_ref[...] = jnp.zeros_like(out_ref)
        out_ref[0:2] = one_ref[0:2]
        cols = pl.ds(pl.multiple_of(index_ref[1] * heads, 128), heads)
        out_ref[2:4, cols] = jnp.concatenate([first_ref[0:2], last_ref[0:2]], axis=1)
        out_ref[4:6, cols] = mix_ref[0:2]
        out_ref[6:10] = two_ref[0:4]

    if not direct:
        d_all = joined([d.astype(F32) for d in (d_first.T, d_last.T)]).T
        unit_d = joined([tn(unit_one, d).T for d in (d_first, d_last)]).T
        d_sum = jnp.sum(d_all, axis=0, keepdims=True)
        sum_one = jnp.stack([jnp.sum(w_qkv * v, axis=1) for v in (unit_d, jnp.broadcast_to(d_sum, unit_d.shape))])
        sum_one = jnp.pad(sum_one, ((0, 6), (0, 0)))
    (vectors,) = call(
        vector_body, [((16, width), F32)], index, sum_one, sum_first, sum_last, sum_mix, sum_two, specs=[SM] + [VM] * 5,
        name="vectors",
    )
    shared_vectors = tensor_share(vectors)
    if direct:
        def vector_chunk_body(index_ref, v0, v1, v2, v3, keep_ref, send_ref):
            for k in range(zs):
                for ref, side in ((keep_ref, index_ref[0] % 2), (send_ref, 1 - index_ref[0] % 2)):
                    cols = pl.ds(pl.multiple_of((((index_ref[0] // 2) ^ k) * 2 + side) * own_rows, 128), own_rows)
                    ref[k] = v0[:, cols] + v1[:, cols] + v2[:, cols] + v3[:, cols]

        keep_vec, send_vec = call(
            vector_chunk_body, [((zs, 16, own_rows), F32)] * 2, index, *shared_vectors, specs=[SM] + [VM] * 4,
            name="vector_chunks",
        )
        across_vec = swap(send_vec, "dp", 1)

    def project_back_body(first_block, d0_ref, d1_ref, w_ref, *part_refs):
        for r in (1, 0):
            rows = rows_of(first_block + r)
            grad = nt(d0_ref[rows], w_ref[:, :384]) + nt(d1_ref[rows], w_ref[:, 384:])
            part_refs[r][...] = grad[:block].astype(BF)

    projected = [None, None]
    for j in (1, 0):
        after = [across_vec, across_last, got_first[2]] if j and direct else []
        projected[j] = call(
            functools.partial(project_back_body, 2 * j), [((block, width), BF)] * 2, d_first, d_last, w_qkv,
            name="project_back", us=2, after=after,
        )
    arrived, _ = tensor_scatter([*projected[0], *projected[1]])

    def input_body(p0, p1, p2, x_ref, grad_ref, vec_ref, out_ref):
        grad_first = p0[...].astype(F32) + p1[...].astype(F32) + p2[...].astype(F32)
        x = x_ref[...].astype(F32)
        mean, inverse = center_scale(x)
        unit = (x - mean) * inverse
        out_ref[:, 0, :] = grad_ref[...] + unit_back(grad_first * vec_ref[F_GAIN : F_GAIN + 1], unit, inverse)

    input_grad, input_token = call(
        input_body, [((block, 1, width), F32)], *arrived, x_own, grad_hidden, vec, name="input_grad", store=(0,),
        token=True,
    )

    if direct:
        def last_add_body(keep_ref, across_ref, keep_vec_ref, across_vec_ref, own_ref, *send_refs):
            for k, ref in enumerate((own_ref, *send_refs)):
                ref[:own_rows] = (keep_ref[k].astype(F32) + across_ref[k].astype(F32)).astype(ref.dtype)
                ref[own_rows:] = jnp.zeros((16, 384), ref.dtype)
                ref[own_rows:, :own_rows] = (keep_vec_ref[k] + across_vec_ref[k]).astype(ref.dtype)

        got_last = dp_column_sums(call(
            last_add_body, [((own_rows + 16, 384), F32)] + [((own_rows + 16, 384), BF)] * (zs - 1),
            keep_last, across_last, keep_vec, across_vec, name="last_add", after=got_first[1:],
        ))

        def attn_finish_body(*refs):
            def total(parts):
                return sum(ref[...].astype(F32) for ref in parts)

            early, late = total(refs[:zs]), total(refs[zs : 2 * zs])
            q_ref, k_ref, v_ref, o_ref, model_ref = refs[3 * zs :]
            for k, ref in enumerate((q_ref, k_ref, v_ref)):
                cols = slice(k * 128, (k + 1) * 128)
                ref[:, 0:128] = early[:, cols]
                ref[:, 128:256] = late[:own_rows, cols]
            o_ref[...] = total(refs[2 * zs : 3 * zs]).T
            model_ref[...] = late[own_rows:, :own_rows]

        shapes = [(own_rows, heads)] * 3 + [(heads, own_rows), (16, own_rows)]
        q_grad, k_grad, v_grad, out_grad, model = call(
            attn_finish_body, [(shape, F32) for shape in shapes], *got_first, *got_last, *got_out, store=(0, 1, 2, 3),
            name="attn_finish", after=[input_token, finished_token],
        )
    else:
        qkv_all = vec[F_GAIN][:, None] * unit_d + vec[F_BIAS][:, None] * d_sum
        qkv_all = lax.psum_scatter(qkv_all.astype(BF), "dp", scatter_dimension=0, tiled=True).astype(F32).T
        qkv_all = qkv_all.reshape(2, 3, 128, own_rows)
        q_grad, k_grad, v_grad = (joined(list(qkv_all[:, k])).T for k in range(3))
        out_grad = plain_grad(branch, mixed).T
        model = lax.psum_scatter(sum(shared_vectors), "dp", scatter_dimension=1, tiled=True)
        sum_ffn = lax.psum(sum_ffn, "dp")
    ffn = sum_ffn[:, :hidden]
    return (
        layer_output[None], input_grad.transpose(1, 0, 2), q_grad, k_grad, v_grad,
        model[2], model[3], model[0], model[1], model[4], model[5], out_grad, model[8], model[6], model[7],
        gate_grad, up_grad, ffn[0], ffn[1], ffn[2], ffn[3], down_grad, model[9],
    )


def solution(mesh):
    rows, across, tokens = P("dp", "tensor"), P("tensor", "dp"), P("dp", "tensor", None)
    model, ffn, image = P("dp"), P("tensor"), P("dp", None)
    in_specs = (
        tokens, rows, rows, rows, model, model, model, model, model, model, across, model, model, model, rows, rows,
        ffn, ffn, ffn, ffn, across, model, tokens, image, image, image,
    )
    out_specs = (
        tokens, tokens, rows, rows, rows, model, model, model, model, model, model, across, model, model, model,
        rows, rows, ffn, ffn, ffn, ffn, across, model,
    )
    return jax.shard_map(local, mesh=mesh, in_specs=in_specs, out_specs=out_specs, check_vma=False)
```

```python
import functools
import math

import jax
import jax.numpy as jnp
from jax import lax
from jax.experimental import pallas as pl
from jax.experimental.pallas import tpu as pltpu
from jax.sharding import PartitionSpec as P

HD = 64
EPSILON = 1e-06
LOW = -1e30
BF = jnp.bfloat16
F32 = jnp.float32
HI = lax.Precision.HIGHEST
VM = pl.BlockSpec(memory_space=pltpu.VMEM)
SM = pl.BlockSpec(memory_space=pltpu.SMEM)
ANY = pl.BlockSpec(memory_space=pl.ANY)
HB = pl.BlockSpec(memory_space=pltpu.HBM)
Q_BIAS, V_BIAS, F_GAIN, F_BIAS, M_GAIN, M_BIAS, O_BIAS, S_GAIN, S_BIAS, D_BIAS = range(10)


def nn(a, b, precision=None):
    return lax.dot_general(a, b, (((1,), (0,)), ((), ())), precision, F32)


def nt(a, b, precision=None):
    return lax.dot_general(a, b, (((1,), (1,)), ((), ())), precision, F32)


def tn(a, b, precision=None):
    return lax.dot_general(a, b, (((0,), (0,)), ((), ())), precision, F32)


def call(
    body, outs, *args, specs=None, load=(), store=(), mib=8, us=1.0, name=None, after=(), scratch=(), token=False, **extra
):
    if token:
        outs = [*outs, ((8, 128), F32)]
    shapes = [jax.ShapeDtypeStruct(shape, dtype) for shape, dtype in outs]
    n_in, n_out, n_after, moved = len(args), len(outs), len(after), len(load) + len(store)
    specs = list(specs or [VM] * n_in)
    out_specs = [VM] * n_out
    for i in load:
        specs[i] = HB
    for i in store:
        out_specs[i] = HB
        shapes[i] = pltpu.HBM(*outs[i])
    args = [hbm(a) if s is HB else a for a, s in zip(args, specs)]
    held = [pltpu.VMEM(args[i].shape, args[i].dtype) for i in load] + [pltpu.VMEM(*outs[i]) for i in store]
    if moved:
        held.append(pltpu.SemaphoreType.DMA((moved,)))

    def run(*refs):
        ins, outs_ = list(refs[:n_in]), list(refs[n_in + n_after : n_in + n_after + n_out])
        rest = refs[n_in + n_after + n_out :]
        own, copies = rest[: len(scratch)], rest[len(scratch) :]
        reads = [pltpu.make_async_copy(ins[i], copies[j], copies[-1].at[j]) for j, i in enumerate(load)]
        for one in reads:
            one.start()
        for j, i in enumerate(load):
            ins[i] = copies[j]
        writes = []
        for j, i in enumerate(store, len(load)):
            writes.append(pltpu.make_async_copy(copies[j], outs_[i], copies[-1].at[j]))
            outs_[i] = copies[j]
        for one in reads:
            one.wait()
        body(*ins, *(outs_[:-1] if token else outs_), *own)
        for one in writes:
            one.start()
        for one in writes:
            one.wait()

    return pl.pallas_call(
        run,
        out_shape=shapes,
        in_specs=specs + [ANY] * n_after,
        out_specs=out_specs,
        scratch_shapes=list(scratch) + held,
        compiler_params=pltpu.CompilerParams(vmem_limit_bytes=mib << 20),
        cost_estimate=pl.CostEstimate(flops=int(us * 1.1e7), bytes_accessed=1 << 10, transcendentals=0),
        name=name,
        **extra,
    )(*args, *after)


def swap(value, axis, offset):
    count = lax.axis_size(axis)
    return lax.ppermute(value, axis, [(i, i ^ offset) for i in range(count)])


def tensor_gather(block):
    core = swap(block, "tensor", 1)
    far = swap(block, "tensor", 2)
    return [block, core, far, swap(far, "tensor", 1)]


def add_pair_body(a_ref, b_ref, out_ref):
    out_ref[...] = (a_ref[...].astype(F32) + b_ref[...].astype(F32)).astype(BF)


def tensor_scatter(parts, after=()):
    third = swap(parts[3], "tensor", 1)
    first = swap(parts[1], "tensor", 1)
    (to_far,) = call(add_pair_body, [(third.shape, BF)], parts[2], third, name="add_pair", after=after)
    return [parts[0], first, swap(to_far, "tensor", 2)], to_far


def tensor_share(value):
    return [value] + [swap(value, "tensor", k) for k in (1, 2, 3)]


def dp_column(block):
    return [block] + [swap(block, "dp", 2 * k) for k in range(1, lax.axis_size("dp") // 2)]


def dp_across(column):
    return [one for mine in column for one in (mine, swap(mine, "dp", 1))]


def hbm(value):
    return pltpu.with_memory_space_constraint(value, pltpu.HBM)


def tie(value, *others, held=False):
    def body(*refs):
        pass

    return pl.pallas_call(
        body,
        out_shape=pltpu.HBM(value.shape, value.dtype),
        in_specs=[HB] + [HB if held else ANY] * len(others),
        out_specs=HB,
        input_output_aliases={0: 0},
        cost_estimate=pl.CostEstimate(flops=1, bytes_accessed=1, transcendentals=0),
        compiler_params=pltpu.CompilerParams(vmem_limit_bytes=1 << 20),
        name="tie",
    )(hbm(value), *[hbm(v) if held else v for v in others])


def hold(values, *others, held=False):
    count = len(values)

    def body(*refs):
        refs, held, sems = refs[: -count - 1], refs[-count - 1 : -1], refs[-1]
        reads = [pltpu.make_async_copy(refs[i], held[i], sems.at[0, i]) for i in range(count)]
        writes = [pltpu.make_async_copy(held[i], refs[i - count], sems.at[1, i]) for i in range(count)]
        for one in reads:
            one.start()
        for read, write in zip(reads, writes):
            read.wait()
            write.start()
        for one in writes:
            one.wait()

    return pl.pallas_call(
        body,
        out_shape=[pltpu.HBM(v.shape, v.dtype) for v in values],
        in_specs=[ANY] * count + [HB if held else ANY] * len(others),
        out_specs=[HB] * count,
        scratch_shapes=[pltpu.VMEM(v.shape, v.dtype) for v in values] + [pltpu.SemaphoreType.DMA((2, count))],
        cost_estimate=pl.CostEstimate(flops=1, bytes_accessed=1, transcendentals=0),
        compiler_params=pltpu.CompilerParams(vmem_limit_bytes=4 << 20),
        name="hold",
    )(*values, *[hbm(v) if held else v for v in others])


def center_scale(values):
    width = values.shape[-1]
    mean = jnp.sum(values, axis=-1, keepdims=True) / width
    spread = jnp.sum(values * values, axis=-1, keepdims=True) / width - mean * mean
    return mean, lax.rsqrt(spread + EPSILON)


def unit_back(grad_hat, unit, inverse):
    width = unit.shape[-1]
    mean = jnp.sum(grad_hat, axis=-1, keepdims=True) / width
    cross = jnp.sum(grad_hat * unit, axis=-1, keepdims=True) / width
    return inverse * (grad_hat - mean - unit * cross)


def columns_to_rows(columns):
    count = columns[0].shape[0]
    lanes = lax.broadcasted_iota(jnp.int32, (count, 128), 1)
    wide = jnp.zeros((count, 128), F32)
    for k, column in enumerate(columns):
        wide = jnp.where(lanes == k, column, wide)
    return wide.T[0:8]


def rows_to_columns(rows):
    return rows.T


def summed_stats(refs, r):
    return refs[0][r] + refs[1][r ^ 1] + refs[2][r ^ 2] + refs[3][r ^ 3]


def turn(values, cosine, sine):
    lanes = lax.broadcasted_iota(jnp.int32, values.shape, 1)
    other = jnp.where(lanes % 2 == 0, pltpu.roll(values, 127, 1), pltpu.roll(values, 1, 1))
    return values * cosine + other * sine


def half_mask(s):
    lane = lax.broadcasted_iota(jnp.int32, (1, 128), 1)
    return lane < HD if s == 0 else lane >= HD


def local(
    layer_input, query_weight, key_weight, value_weight, query_bias, value_bias, first_gain, first_bias,
    mixer_gain, mixer_bias, output_weight, output_bias, second_gain, second_bias, gate_weight, up_weight,
    gate_bias, up_bias, inner_gain, inner_bias, down_weight, down_bias, cotangent, key_valid, patch_row, patch_column,
):
    ranks = lax.axis_size("tensor")
    me_t, me_d, count_d = lax.axis_index("tensor"), lax.axis_index("dp"), lax.axis_size("dp")
    block, width = layer_input.shape[1:]
    pad = -(-block // 16) * 16
    length = ranks * pad
    heads = query_weight.shape[1]
    hidden = gate_weight.shape[1]
    hidden_pad = -(-hidden // 128) * 128
    own_rows = width // count_d
    direct = own_rows % 128 == 0 and count_d & (count_d - 1) == 0
    index = jnp.stack([me_d, me_t]).astype(jnp.int32)
    x_own, cot_own = layer_input[0], cotangent[0]
    blocks = range(ranks)

    def rows_of(r):
        return slice(r * pad, (r + 1) * pad)

    lines = jnp.stack([key_valid[0], patch_row[0], patch_column[0], jnp.arange(ranks * block, dtype=jnp.int32)])
    lines = jnp.pad(lines.reshape(4, ranks, block), ((0, 4), (0, 0), (0, pad - block))).astype(F32)
    lines = jnp.stack([lax.dynamic_index_in_dim(lines, me_t ^ r, 1, False) for r in blocks])
    lane = jnp.arange(128)
    frequency = jnp.power(F32(10000.0), -((lane % HD) // 2 % (HD // 4)).astype(F32) / (HD // 4))
    frequency = jnp.broadcast_to(frequency[None, :], (8, 128))

    def table_body(line_ref, frequency_ref, cos_ref, sin_ref):
        lanes = lax.broadcasted_iota(jnp.int32, (pad, 128), 1)
        for r in blocks:
            columns = rows_to_columns(line_ref[r])
            position = jnp.where(lanes % HD < HD // 2, columns[:, 1:2], columns[:, 2:3])
            angle = jnp.where(columns[:, 3:4] > 0.0, 0.5 * (position * frequency_ref[0:1]), 0.0)
            cos_ref[rows_of(r)] = jnp.cos(angle)
            sine = jnp.sin(angle)
            sin_ref[rows_of(r)] = jnp.where(lanes % 2 == 0, -sine, sine)

    cosine, sine = call(table_body, [((length, 128), F32)] * 2, lines, frequency, name="tables", us=4)

    small = [
        v[None, :]
        for v in (
            query_bias, value_bias, first_gain, first_bias, mixer_gain, mixer_bias, output_bias, second_gain,
            second_bias, down_bias,
        )
    ]
    tiles = heads // 128
    hidden_low = -(-hidden // 16) * 16
    starts = [(k % 3) * tiles + k // 3 for k in range(3 * tiles)]
    if direct:
        o_start = 3 * tiles * own_rows + 16

        def pack_a_body(q_ref, k_ref, v_ref, w_ref, *refs):
            *small_refs, out_ref = refs
            out_ref[o_start:] = w_ref[...]
            for k in range(3 * tiles):
                ref = (q_ref, k_ref, v_ref)[k % 3]
                out_ref[k * own_rows : (k + 1) * own_rows] = ref[:, k // 3 * 128 : (k // 3 + 1) * 128]
            lines = [ref[...].astype(F32) for ref in small_refs]
            lines.append(jnp.zeros((16 - len(lines), own_rows), F32))
            out_ref[3 * tiles * own_rows : o_start] = jnp.concatenate(lines, axis=0).astype(BF)

        (pack_a,) = call(
            pack_a_body, [((o_start + heads, 128), BF)], query_weight, key_weight, value_weight, output_weight,
            *small, name="pack_a", load=tuple(range(14)),
        )
        column_a = dp_column(pack_a)
        across_a = [swap(pack_a, "dp", 1)]
        x_far = swap(x_own, "tensor", 2)
        column_a[3], across_a[0] = hold([column_a[3], *across_a], cosine)
        across_last = swap(column_a[3], "dp", 1)
        (column_a[2],) = hold([column_a[2]], column_a[3], held=True)
        column_a[1], x_held, x_far = hold([column_a[1], x_own, x_far], column_a[2], across_last, held=True)
        across_a += [swap(one, "dp", 1) for one in column_a[1:3]] + [across_last]
        x_blocks = [x_own, swap(x_held, "tensor", 1), x_far, swap(x_far, "tensor", 1)]
        got_a = [one for pair in zip(column_a, across_a) for one in pair]

        def pack_f_body(g_ref, u_ref, d_ref, out_ref):
            for j, ref in enumerate((g_ref, u_ref, d_ref)):
                out_ref[(j + 1) * hidden_low - 16 : (j + 1) * hidden_low] = jnp.zeros((16, own_rows), BF)
                out_ref[j * hidden_low : j * hidden_low + hidden] = ref[...]

        (pack_f,) = call(
            pack_f_body, [((3 * hidden_low, own_rows), BF)], gate_weight.T, up_weight.T, down_weight, name="pack_f",
            load=(0, 1, 2),
        )
        got_f = lax.all_gather(tie(pack_f, *column_a[1:], held=True), "dp")
        def copies(pairs, sems):
            started = [pltpu.make_async_copy(a, b, sems.at[i]) for i, (a, b) in enumerate(pairs)]
            for one in started:
                one.start()
            for one in started:
                one.wait()

        def chunk_at(index_ref, r):
            return pl.ds(pl.multiple_of((index_ref[0] ^ r) * own_rows, 128), own_rows)

        def assemble_a(index_ref, *refs):
            *chunks, cot_ref = refs[: count_d + 1]
            w_ref, v_ref, o_ref, cot_out, small_ref, held_ref, sems, cot_sems = refs[count_d + 1 :]
            cot_read = pltpu.make_async_copy(cot_ref, held_ref, cot_sems.at[0])
            cot_write = pltpu.make_async_copy(held_ref, cot_out, cot_sems.at[1])
            cot_read.start()
            pairs = []
            for r, chunk in enumerate(chunks):
                for k in range(3 * tiles):
                    pairs.append((
                        chunk.at[k * own_rows : (k + 1) * own_rows],
                        w_ref.at[chunk_at(index_ref, r), k * 128 : (k + 1) * 128],
                    ))
                pairs.append((chunk.at[3 * tiles * own_rows : o_start], small_ref.at[r]))
                pairs.append((chunk.at[o_start:], o_ref.at[:, chunk_at(index_ref, r)]))
            started = [pltpu.make_async_copy(a, b, sems.at[i]) for i, (a, b) in enumerate(pairs)]
            for one in started:
                one.start()
            cot_read.wait()
            cot_write.start()
            for one in started:
                one.wait()
            for r in range(count_d):
                v_ref[:, chunk_at(index_ref, r)] = small_ref[r].astype(F32)
            cot_write.wait()

        specs = [SM] + [HB] * count_d

        def dma(count):
            return pltpu.SemaphoreType.DMA((count,))

        shapes = [((width, 3 * heads), BF), ((16, width), F32), ((heads, width), BF), (cot_own.shape, BF)]
        w_qkv, vec, w_out, cot_held = pl.pallas_call(
            assemble_a,
            out_shape=[jax.ShapeDtypeStruct(*shape) for shape in shapes[:3]] + [pltpu.HBM(*shapes[3])],
            in_specs=specs + [HB],
            out_specs=[VM] * 3 + [HB],
            scratch_shapes=[
                pltpu.VMEM((count_d, 16, 128), BF), pltpu.VMEM(*shapes[3]), dma(count_d * (3 * tiles + 2)), dma(2)
            ],
            compiler_params=pltpu.CompilerParams(vmem_limit_bytes=4 << 20),
            cost_estimate=pl.CostEstimate(flops=1 << 10, bytes_accessed=1 << 10, transcendentals=0),
            name="assemble_a",
        )(index, *[hbm(v) for v in got_a], hbm(cot_own))
        cot_blocks = tensor_gather(cot_held)
    else:
        def whole(weight, axis):
            return lax.all_gather(weight, "dp", axis=axis, tiled=True)

        x_blocks = tensor_gather(x_own)
        cot_blocks = tensor_gather(cot_own)
        w_qkv = whole(jnp.concatenate(
            [(query_weight, key_weight, value_weight)[k % 3][:, k // 3 * 128 : (k // 3 + 1) * 128] for k in range(3 * tiles)],
            axis=1,
        ), 0)
        vec = jnp.pad(whole(jnp.concatenate(small), 1).astype(F32), ((0, 6), (0, 0)))
        w_out = whole(output_weight, 1)
        w_gate, w_up, w_down = (
            jnp.pad(whole(w, 1), ((0, hidden_pad - hidden), (0, 0))) for w in (gate_weight.T, up_weight.T, down_weight)
        )
    ffn_vec = jnp.pad(
        jnp.stack([gate_bias, up_bias, inner_gain, inner_bias]).astype(F32), ((0, 4), (0, hidden_pad - hidden))
    )

    def own(ref, k, index_ref):
        return ref[k : k + 1, pl.ds(pl.multiple_of(index_ref[1] * heads, 128), heads)]

    n_heads = heads // HD

    def attend_body(
        index_ref, x0, x1, x2, x3, w_ref, vec_ref, cos_ref, sin_ref, line_ref,
        unit_out, q_out, k_out, v_out, o_ref, stat_ref, unit_ref, q_ref, k_ref, v_ref, first_ref, x_ref, cos_held,
        sin_held, sems, load_sems,
    ):
        pairs = [(x0, x_ref.at[0]), (x2, x_ref.at[1]), (cos_ref, cos_held), (sin_ref, sin_held)]
        reads = [pltpu.make_async_copy(a, b, load_sems.at[i]) for i, (a, b) in enumerate(pairs)]
        for one in reads:
            one.start()
        gain, bias = vec_ref[F_GAIN : F_GAIN + 1], vec_ref[F_BIAS : F_BIAS + 1]
        q_bias, v_bias = own(vec_ref, Q_BIAS, index_ref), own(vec_ref, V_BIAS, index_ref)
        moves = []
        for r in blocks:
            if r % 2 == 0:
                reads[r // 2].wait()
            x = (x_ref[0] if r == 0 else x1[...] if r == 1 else x_ref[1] if r == 2 else x3[...]).astype(F32)
            mean, inverse = center_scale(x)
            unit = (x - mean) * inverse
            unit_ref[(r + 1) * pad - 16 : (r + 1) * pad] = jnp.zeros((16, width), BF)
            unit_ref[r * pad : r * pad + block] = unit.astype(BF)
            first_ref[pad - 16 :] = jnp.zeros((16, width), BF)
            first_ref[:block] = (unit * gain + bias).astype(BF)
            rows = rows_of(r)
            qkv = nn(first_ref[...], w_ref[...])
            if r == 0:
                reads[2].wait()
                reads[3].wait()
            c, s = cos_held[rows], sin_held[rows]
            for k in range(tiles):
                cols = slice(k * 128, (k + 1) * 128)
                q, key, v = (qkv[:, (3 * k + j) * 128 : (3 * k + j + 1) * 128] for j in range(3))
                q_ref[rows, cols] = turn(q + q_bias[:, cols], c, s).astype(BF)
                k_ref[rows, cols] = turn(key, c, s).astype(BF)
                v_ref[rows, cols] = (v + v_bias[:, cols]).astype(BF)
            for j, (held, out) in enumerate(
                ((unit_ref, unit_out), (q_ref, q_out), (k_ref, k_out), (v_ref, v_out))
            ):
                moves.append(pltpu.make_async_copy(held.at[rows], out.at[rows], sems.at[4 * r + j]))
                moves[-1].start()
        mask_line = jnp.concatenate([jnp.where(line_ref[r][0:1] == 1.0, 0.0, LOW) for r in blocks], axis=1)
        k_half, v_half = [], []
        for h in range(n_heads):
            cols = slice(h // 2 * 128, (h // 2 + 1) * 128)
            k_half.append(jnp.where(half_mask(h % 2), k_ref[:, cols], 0).astype(BF))
            v_half.append(jnp.where(half_mask(h % 2), v_ref[:, cols], 0).astype(BF))

        def step(b, _):
            rows = pl.ds(pl.multiple_of(b * pad, 16), pad)
            kept = []
            total = jnp.zeros((pad, 1), F32)
            square = jnp.zeros((pad, 1), F32)
            for pair in range(tiles):
                cols = slice(pair * 128, (pair + 1) * 128)
                q = q_ref[rows, cols]
                out = jnp.zeros((pad, 128), F32)
                for s in range(2):
                    h = 2 * pair + s
                    scores = nt(q, k_half[h]) * (1.0 / math.sqrt(HD)) + mask_line
                    top = jnp.max(scores, axis=-1, keepdims=True)
                    terms = jnp.exp(scores - top)
                    below = jnp.sum(terms, axis=-1, keepdims=True)
                    out += nn(terms.astype(BF), v_half[h]) * (1.0 / below)
                    kept.append(top + jnp.log(below))
                o_ref[rows, cols] = out
                total += jnp.sum(out, axis=-1, keepdims=True)
                square += jnp.sum(out * out, axis=-1, keepdims=True)
            stat_ref[b] = columns_to_rows(kept + [total, square])
            return 0

        lax.fori_loop(0, ranks, step, 0)
        for one in moves:
            one.wait()

    shapes = [((length, width), BF)] + [((length, heads), BF)] * 3
    unit_one, queries, keys, values, attended, stat_mix = pl.pallas_call(
        attend_body,
        out_shape=[pltpu.HBM(*shape) for shape in shapes]
        + [jax.ShapeDtypeStruct((length, heads), F32), jax.ShapeDtypeStruct((ranks, 8, pad), F32)],
        in_specs=[SM] + [HB, VM] * 2 + [VM] * 2 + [HB] * 2 + [VM],
        out_specs=[HB] * 4 + [VM] * 2,
        scratch_shapes=[pltpu.VMEM(*shape) for shape in shapes]
        + [pltpu.VMEM((pad, width), BF), pltpu.VMEM((2, block, width), BF)]
        + [pltpu.VMEM((length, 128), F32)] * 2
        + [pltpu.SemaphoreType.DMA((4 * ranks,)), pltpu.SemaphoreType.DMA((4,))],
        compiler_params=pltpu.CompilerParams(vmem_limit_bytes=22 << 20),
        cost_estimate=pl.CostEstimate(flops=1 << 17, bytes_accessed=1 << 10, transcendentals=0),
        name="attend",
    )(index, hbm(x_blocks[0]), x_blocks[1], hbm(x_blocks[2]), x_blocks[3], w_qkv, vec, hbm(cosine), hbm(sine), lines)
    shared_mix = tensor_share(stat_mix)

    def mix_body(index_ref, a_ref, s0, s1, s2, s3, w_ref, vec_ref, mixed_ref, norm_ref, *part_refs):
        gain, bias = own(vec_ref, M_GAIN, index_ref), own(vec_ref, M_BIAS, index_ref)
        for r in reversed(blocks):
            rows = rows_of(r)
            sums = summed_stats((s0, s1, s2, s3), r)
            mean = sums[n_heads : n_heads + 1] / width
            inverse = lax.rsqrt(sums[n_heads + 1 : n_heads + 2] / width - mean * mean + EPSILON)
            lines = jnp.concatenate([mean, inverse, jnp.zeros((6, pad), F32)], axis=0)
            norm_ref[r] = lines
            columns = rows_to_columns(lines)
            mixed = ((a_ref[rows] - columns[:, 0:1]) * columns[:, 1:2] * gain + bias).astype(BF)
            mixed_ref[rows] = mixed
            part_refs[r][...] = nn(mixed, w_ref[...])[:block].astype(BF)

    mixed, norm_mix, *parts = call(
        mix_body, [((length, heads), BF), ((ranks, 8, pad), F32)] + [((block, width), BF)] * ranks,
        index, attended, *shared_mix, w_out, vec, specs=[SM] + [VM] * 7, name="mix", us=2.5,
        store=(0,), after=[cot_blocks[2]],
    )
    arrived, _ = tensor_scatter(parts)

    def second_body(x_ref, p0, p1, p2, vec_ref, hidden_ref, second_ref):
        out = p0[...].astype(F32) + p1[...].astype(F32) + p2[...].astype(F32)
        state = x_ref[...].astype(F32) + out + vec_ref[O_BIAS : O_BIAS + 1]
        hidden_ref[...] = state
        mean, inverse = center_scale(state)
        unit = (state - mean) * inverse
        second_ref[...] = (unit * vec_ref[S_GAIN : S_GAIN + 1] + vec_ref[S_BIAS : S_BIAS + 1]).astype(BF)

    hidden_state, second_own = call(
        second_body, [((block, width), F32), ((block, width), BF)], x_own, *arrived, vec, name="second", store=(0, 1),
    )
    half = 2 * pad

    def half_rows(r):
        return slice(r % 2 * pad, (r % 2 + 1) * pad)

    def pad_block(ref, r, value):
        start = r * pad
        ref[start + pad - 16 : start + pad] = jnp.zeros((16, width), BF)
        ref[start : start + block] = value

    def expand(b_refs, wg_ref, wu_ref, vec_ref, grad_ref, second_ref, gate_ref, up_ref, stat_ref, base):
        for r, b_ref in enumerate(b_refs):
            rows = half_rows(r)
            pad_block(second_ref, r, b_ref[...])
            gate = nt(second_ref[rows], wg_ref[...]) + vec_ref[0:1]
            up = nt(second_ref[rows], wu_ref[...]) + vec_ref[1:2]
            gate_ref[rows] = gate
            up_ref[rows] = up
            activated = gate * jax.nn.sigmoid(gate) * up
            hat = grad_ref[rows] * vec_ref[2:3]
            stat_ref[base + r] = columns_to_rows(
                [jnp.sum(v, axis=-1, keepdims=True) for v in (activated, activated * activated, hat, hat * activated)]
            )

    def expand_first_body(c0, c1, c2, c3, b0, b1, vec_ref, *refs):
        if direct:
            chunks, *refs, down_sems, gate_sems = refs
            wg_ref, wu_ref, wd_ref = refs[:3]
            outs = refs[3:]
            moves = []
            for j, (out, sems) in enumerate(((wd_ref, down_sems), (wg_ref, gate_sems), (wu_ref, gate_sems))):
                for a in range(count_d):
                    start = (2, 0, 1)[j] * hidden_low
                    moves.append(pltpu.make_async_copy(
                        chunks.at[a, start : start + hidden_low],
                        out.at[0:hidden_low, a * own_rows : (a + 1) * own_rows],
                        sems.at[a if j < 2 else count_d + a],
                    ))
                    moves[-1].start()
            for out in (wg_ref, wu_ref, wd_ref):
                out[hidden_low:] = jnp.zeros((hidden_pad - hidden_low, width), BF)
            for one in moves[:count_d]:
                one.wait()
        else:
            wg_ref, wu_ref, wd_ref = refs[:3]
            outs = refs[3:]
        cot0, cot1, grad0, grad1, second_ref, gate_ref, up_ref, stat_ref = outs
        for r, c_ref in enumerate((c0, c1, c2, c3)):
            cot_ref, grad_ref = ((cot0, grad0), (cot1, grad1))[r // 2]
            pad_block(cot_ref, r % 2, c_ref[...])
            grad_ref[half_rows(r)] = nt(cot_ref[half_rows(r)], wd_ref[...])
        if direct:
            for one in moves[count_d:]:
                one.wait()
        expand((b0, b1), wg_ref, wu_ref, vec_ref, grad0, second_ref, gate_ref, up_ref, stat_ref, 0)

    half_outs = [((half, width), BF)] + [((half, hidden_pad), F32)] * 2
    second_far = swap(second_own, "tensor", 2)
    blocks_in = [*cot_blocks, second_own, swap(second_own, "tensor", 1), ffn_vec]
    outs = [((half, width), BF)] * 2 + [((half, hidden_pad), F32)] * 2 + half_outs + [((2, 8, pad), F32)]
    weights = [((hidden_pad, width), BF)] * 3
    if direct:
        w_gate, w_up, w_down, *made = call(
            expand_first_body, weights + outs, *blocks_in, got_f, specs=[VM] * 7 + [HB], name="expand_first",
            scratch=[dma(count_d), dma(2 * count_d)], us=10, load=tuple(range(6)),
        )
    else:
        made = call(expand_first_body, outs, *blocks_in, w_gate, w_up, w_down, name="expand_first", us=10)
    cot_halves, grad_inner, first_half = made[:2], made[2:4], made[4:]

    def expand_body(b0, b1, wg_ref, wu_ref, vec_ref, grad_ref, before_ref, second_ref, gate_ref, up_ref, stat_ref):
        stat_ref[0:2] = before_ref[...]
        expand((b0, b1), wg_ref, wu_ref, vec_ref, grad_ref, second_ref, gate_ref, up_ref, stat_ref, 2)

    second_far = tie(second_far, first_half[3])
    expanded = [first_half, call(
        expand_body, half_outs + [((4, 8, pad), F32)], second_far, swap(second_far, "tensor", 1), w_gate, w_up, ffn_vec,
        grad_inner[1], first_half[3], name="expand", us=3.7, load=(0,),
    )]
    shared_ffn = tensor_share(expanded[1][3])

    def ffn_back_body(
        first_block, g_ref, u_ref, grad_ref, s0, s1, s2, s3, vec_ref, wg_ref, wu_ref, *refs
    ):
        dg_ref, du_ref, inner_ref, sum_ref, *part_refs = refs[-6:]
        wide = hidden * ranks
        sum_ref[...] = refs[0][...] if len(refs) == 7 else jnp.zeros_like(sum_ref)
        for r in (1, 0):
            rows = half_rows(r)
            sums = summed_stats((s0, s1, s2, s3), first_block + r)
            mean = sums[0:1] / wide
            inverse = lax.rsqrt(sums[1:2] / wide - mean * mean + EPSILON)
            grad_mean = sums[2:3] / wide
            cross = inverse * (sums[3:4] / wide - mean * grad_mean)
            columns = rows_to_columns(
                jnp.concatenate([mean, inverse, grad_mean, cross, jnp.zeros((4, pad), F32)], axis=0)
            )
            mean, inverse, grad_mean, cross = (columns[:, k : k + 1] for k in range(4))
            gate, up, grad = g_ref[rows], u_ref[rows], grad_ref[rows]
            sigmoid = jax.nn.sigmoid(gate)
            silu = gate * sigmoid
            unit = (silu * up - mean) * inverse
            inner_ref[rows] = (unit * vec_ref[2:3] + vec_ref[3:4]).astype(BF)
            grad_act = inverse * (grad * vec_ref[2:3] - grad_mean - unit * cross)
            d_gate = (grad_act * up * sigmoid * (1.0 + gate - silu)).astype(BF)
            d_up = (grad_act * silu).astype(BF)
            dg_ref[rows] = d_gate
            du_ref[rows] = d_up
            totals = [d_gate.astype(F32), d_up.astype(F32), grad * unit, grad]
            sum_ref[0:4] += jnp.concatenate([jnp.sum(v, axis=0, keepdims=True) for v in totals], axis=0)
            part_refs[r][...] = (nn(d_gate, wg_ref[...]) + nn(d_up, wu_ref[...]))[:block].astype(BF)

    backed = [None, None]
    for j in (1, 0):
        before = [backed[1][3]] if j == 0 else []
        backed[j] = call(
            functools.partial(ffn_back_body, 2 * j),
            [((half, hidden_pad), BF)] * 3 + [((8, hidden_pad), F32)] + [((block, width), BF)] * 2,
            *expanded[j][1:3], grad_inner[j], *shared_ffn, ffn_vec, w_gate, w_up, *before, name="ffn_back", us=5.5,
            store=() if j else (4, 5),
        )
    sum_ffn = backed[0][3]
    arrived, to_far = tensor_scatter([*backed[0][4:], *backed[1][4:]])

    def dp_sum_step(total, k, after):
        def body(a_ref, b_ref, out_ref):
            out_ref[...] = a_ref[...] + b_ref[...]

        return call(body, [(total.shape, F32)], total, swap(total, "dp", k), name="dp_sum", after=after)[0]

    if direct:
        rows_f = 3 * hidden_low

        def ffn_grad_body(g0, g1, u0, u1, i0, i1, e0, e1, c0, c1, after_ref, out_ref, token_ref, made_ref, sems):
            moves = []
            for j, (rights, lefts) in enumerate((((g0, g1), (e0, e1)), ((u0, u1), (e0, e1)), ((i0, i1), (c0, c1)))):
                for at in range(0, hidden_low, 256):
                    stop = min(at + 256, hidden_low)
                    cols = slice(at, min(at + 256, hidden_pad))
                    total = sum(tn(a[:, cols], b[...]) for a, b in zip(rights, lefts)).astype(BF)
                    for d in range(count_d):
                        made_ref[d, j * hidden_low + at : j * hidden_low + stop] = (
                            total[: stop - at, d * own_rows : (d + 1) * own_rows]
                        )
                    rows = slice(j * hidden_low + at, j * hidden_low + stop)
                    moves.append(pltpu.make_async_copy(made_ref.at[:, rows], out_ref.at[:, rows], sems.at[len(moves)]))
                    moves[-1].start()
            for one in moves:
                one.wait()

        shape = ((count_d, rows_f, own_rows), BF)
        pieces = 3 * -(-hidden_low // 256)
        ffn_grads, ffn_token = pl.pallas_call(
            ffn_grad_body,
            out_shape=[pltpu.HBM(*shape), jax.ShapeDtypeStruct((8, 128), F32)],
            in_specs=[VM] * 10 + [ANY],
            out_specs=[HB, VM],
            scratch_shapes=[pltpu.VMEM(*shape), pltpu.SemaphoreType.DMA((pieces,))],
            compiler_params=pltpu.CompilerParams(vmem_limit_bytes=10 << 20),
            cost_estimate=pl.CostEstimate(flops=1 << 17, bytes_accessed=1 << 10, transcendentals=0),
            name="ffn_grad",
        )(
            *(backed[j][k] for k in (0, 1, 2) for j in range(2)), expanded[0][0], expanded[1][0], *cot_halves, to_far
        )
        ffn_grads = ffn_grads.reshape(count_d * rows_f, own_rows)
        ffn_grads = tie(ffn_grads, arrived[2])
        got_ffn = lax.psum_scatter(ffn_grads, "dp", scatter_dimension=0, tiled=True)

        def ffn_finish_body(p_ref, *out_refs):
            for j, ref in enumerate(out_refs):
                ref[...] = p_ref[j * hidden_low : j * hidden_low + hidden].astype(F32)

        gate_grad, up_grad, down_grad, finished_token = call(
            ffn_finish_body, [((hidden, own_rows), F32)] * 3, got_ffn, store=(0, 1, 2), load=(0,), name="ffn_finish",
            token=True,
        )
        gate_grad, up_grad = gate_grad.T, up_grad.T
    else:
        def plain_grad(left, right):
            return lax.psum_scatter(tn(left, right).astype(BF), "dp", scatter_dimension=0, tiled=True).astype(F32)

        def joined(pair):
            return jnp.concatenate(pair)

        second_all = joined([expanded[j][0] for j in range(2)])
        down_grad = plain_grad(joined(cot_halves), joined([backed[j][2] for j in range(2)]))[:, :hidden].T
        gate_grad = plain_grad(second_all, joined([backed[j][0] for j in range(2)]))[:, :hidden]
        up_grad = plain_grad(second_all, joined([backed[j][1] for j in range(2)]))[:, :hidden]

    def hidden_back_body(p0, p1, p2, h_ref, cot_ref, vec_ref, grad_ref, branch_ref, sum_ref):
        grad_second = p0[...].astype(F32) + p1[...].astype(F32) + p2[...].astype(F32)
        mean, inverse = center_scale(h_ref[...])
        unit = (h_ref[...] - mean) * inverse
        cot = cot_ref[...].astype(F32)
        grad = cot + unit_back(grad_second * vec_ref[S_GAIN : S_GAIN + 1], unit, inverse)
        branch = grad.astype(BF)
        grad_ref[...] = grad
        branch_ref[...] = branch
        lines = [grad_second * unit, grad_second, branch.astype(F32), cot]
        lines = [jnp.sum(v, axis=0, keepdims=True) for v in lines]
        sum_ref[...] = jnp.concatenate(lines + [jnp.zeros((4, width), F32)], axis=0)

    grad_hidden, branch_own, sum_two = call(
        hidden_back_body, [((block, width), F32), ((block, width), BF), ((8, width), F32)],
        *arrived, hidden_state, cot_own, vec, name="hidden_back", after=[ffn_token] if direct else [],
        store=(0,), load=(0, 2, 3, 4),
    )

    def down_body(i0, i1, w_ref, *part_refs):
        for r in reversed(blocks):
            part_refs[r][...] = nn((i0, i1)[r // 2][half_rows(r)], w_ref[...])[:block].astype(BF)

    if direct:
        sum_ffn = dp_sum_step(sum_ffn, 1, [branch_own])
    *down_parts, down_token = call(
        down_body, [((block, width), BF)] * ranks, backed[0][2], backed[1][2], w_down, name="down", us=2.5, token=True,
        after=[sum_ffn],
    )
    branch_far = swap(branch_own, "tensor", 2)
    branch_core = swap(branch_own, "tensor", 1)
    if direct:
        sum_ffn = dp_sum_step(sum_ffn, 2, [down_token])
    branch_far = tie(branch_far, sum_ffn)
    branch_blocks = [branch_own, branch_core, branch_far, swap(branch_far, "tensor", 1)]

    def mix_back_body(index_ref, b0, b1, b2, b3, w_ref, a_ref, norm_ref, vec_ref, branch_ref, grad_ref, stat_ref, sum_ref):
        gain = own(vec_ref, M_GAIN, index_ref)
        sum_ref[...] = jnp.zeros_like(sum_ref)
        for r, b_ref in enumerate((b0, b1, b2, b3)):
            rows = rows_of(r)
            branch_ref[(r + 1) * pad - 16 : (r + 1) * pad] = jnp.zeros((16, width), BF)
            branch_ref[r * pad : r * pad + block] = b_ref[...]
            grad = nt(branch_ref[rows], w_ref[...])
            columns = rows_to_columns(norm_ref[r])
            unit = (a_ref[rows] - columns[:, 0:1]) * columns[:, 1:2]
            hat = grad * gain
            grad_ref[rows] = hat
            stat_ref[r] = columns_to_rows([jnp.sum(v, axis=-1, keepdims=True) for v in (hat, hat * unit)])
            lines = [jnp.sum(v, axis=0, keepdims=True) for v in (grad * unit, grad)]
            sum_ref[0:2] += jnp.concatenate(lines, axis=0)

    branch, hat_mix, stat_back, sum_mix = call(
        mix_back_body,
        [((length, width), BF), ((length, heads), F32), ((ranks, 8, pad), F32), ((8, heads), F32)],
        index, *branch_blocks, w_out, attended, norm_mix, vec, specs=[SM] + [VM] * 8, name="mix_back", us=3,
        load=(3,),
    )

    zs = count_d // 2

    def weight_grad(index_ref, left, rights, keep_ref, send_ref, at):
        odd = index_ref[0] % 2
        for k in range(zs):
            cols = pl.ds(pl.multiple_of(((index_ref[0] // 2) ^ k) * 2 * own_rows, 128), 2 * own_rows)
            turned = left[:, cols].T
            start = at
            for right in rights:
                both = nn(turned, right[...])
                upper, lower = both[:own_rows].astype(BF), both[own_rows:].astype(BF)
                stop = start + both.shape[1]
                keep_ref[k, :own_rows, start:stop] = jnp.where(odd == 0, upper, lower)
                send_ref[k, :own_rows, start:stop] = jnp.where(odd == 0, lower, upper)
                start = stop

    def qkv_grad_body(pair, index_ref, unit_ref, d_ref, w_ref, vec_ref, *refs):
        keep_ref, send_ref, sum_ref = refs[-3:]
        odd = index_ref[0] % 2
        d_sum = jnp.sum(d_ref[...].astype(F32), axis=0, keepdims=True)
        w_cols = slice(pair * 384, (pair + 1) * 384)
        for k in range(zs):
            cols = pl.ds(pl.multiple_of(((index_ref[0] // 2) ^ k) * 2 * own_rows, 128), 2 * own_rows)
            both = nn(unit_ref[:, cols].T, d_ref[...])
            weight = w_ref[cols, w_cols].astype(F32)
            sums = [jnp.sum(weight * both, axis=-1, keepdims=True), jnp.sum(weight * d_sum, axis=-1, keepdims=True)]
            lines = columns_to_rows(sums)
            sum_ref[:, cols] = lines + refs[0][:, cols] if len(refs) == 4 else lines
            columns = vec_ref[0:8, cols].T
            both = columns[:, F_GAIN : F_GAIN + 1] * both + columns[:, F_BIAS : F_BIAS + 1] * d_sum
            upper, lower = both[:own_rows].astype(BF), both[own_rows:].astype(BF)
            keep_ref[k] = jnp.where(odd == 0, upper, lower)
            send_ref[k] = jnp.where(odd == 0, lower, upper)

    def qkv_grad(pair, d, after, *before):
        return call(
            functools.partial(qkv_grad_body, pair), [((zs, own_rows, 384), BF)] * 2 + [((8, width), F32)],
            index, unit_one, d, w_qkv, vec, *before, specs=[SM] + [VM] * (4 + len(before)), name="qkv_grad", us=2,
            after=after, token=True,
        )

    def add_body(keep_ref, across_ref, own_ref, *send_refs):
        own_ref[...] = keep_ref[0].astype(F32) + across_ref[0].astype(F32)
        for k, ref in enumerate(send_refs):
            ref[...] = (keep_ref[k + 1].astype(F32) + across_ref[k + 1].astype(F32)).astype(BF)

    def dp_add(keep, across, name, after=()):
        return call(
            add_body, [(keep.shape[1:], F32)] + [(keep.shape[1:], BF)] * (zs - 1), keep, across, name=name, us=1,
            after=after,
        )

    def dp_column_sums(added):
        return [added[0]] + [swap(one, "dp", 2 * (k + 1)) for k, one in enumerate(added[1:])]

    shared_back = tensor_share(stat_back)
    if direct:
        def out_grad_body(index_ref, b_ref, m_ref, keep_ref, send_ref):
            weight_grad(index_ref, b_ref, [m_ref], keep_ref, send_ref, 0)

        keep_out, send_out, out_token = call(
            out_grad_body, [((zs, own_rows, heads), BF)] * 2, index, branch, mixed, specs=[SM] + [VM] * 2,
            name="out_grad", token=True,
        )
        across_out = swap(send_out, "dp", 1)
    arrived_out, _ = tensor_scatter(down_parts, after=shared_back[1:])

    def finish_body(h_ref, p0, p1, p2, vec_ref, out_ref):
        out = p0[...].astype(F32) + p1[...].astype(F32) + p2[...].astype(F32)
        out_ref[...] = (h_ref[...] + out + vec_ref[D_BIAS : D_BIAS + 1]).astype(BF)

    layer_output, finish_token = call(
        finish_body, [((block, width), BF)], hidden_state, *arrived_out, vec, name="finish", store=(0,), token=True
    )


    def three(column):
        upper = column.astype(BF).astype(F32)
        middle = (column - upper).astype(BF).astype(F32)
        return [upper, middle, column - upper - middle]

    def with_lanes(value, s, columns):
        lane = lax.broadcasted_iota(jnp.int32, (1, 128), 1)
        out = jnp.where(half_mask(s), value, 0.0)
        for j, column in enumerate(columns):
            out = jnp.where(lane == HD * (1 - s) + j, column, out)
        return out.astype(BF)

    def attend_back_body(
        pair, q_ref, k_ref, v_ref, a_ref, hat_ref, norm_ref, s0, s1, s2, s3, log_ref, line_ref, cos_ref, sin_ref,
        d_ref, sum_ref, kx_ref, qx_ref, vx_ref, gx_ref, dq_ref, dk_ref, dv_ref,
    ):
        cols = slice(pair * 128, (pair + 1) * 128)
        scale = 1.0 / math.sqrt(HD)
        for r in blocks:
            rows = rows_of(r)
            columns = rows_to_columns(norm_ref[r])
            back = rows_to_columns(summed_stats((s0, s1, s2, s3), r) / width)
            attended = a_ref[rows, cols]
            unit = (attended - columns[:, 0:1]) * columns[:, 1:2]
            grad = columns[:, 1:2] * (hat_ref[rows, cols] - back[:, 0:1] - unit * back[:, 1:2])
            grad = grad.astype(BF).astype(F32)
            mask = jnp.where(rows_to_columns(line_ref[r])[:, 0:1] == 1.0, 0.0, LOW)
            logs = rows_to_columns(log_ref[r])
            q, k, v = (ref[rows, cols].astype(F32) for ref in (q_ref, k_ref, v_ref))
            for s in range(2):
                h = 2 * pair + s
                log = three(logs[:, h : h + 1])
                delta = three(jnp.sum(jnp.where(half_mask(s), grad * attended, 0.0), axis=-1, keepdims=True))
                kx_ref[s, rows] = with_lanes(k * scale, s, [1.0, 1.0, 1.0, mask])
                qx_ref[s, rows] = with_lanes(q, s, [-log[0], -log[1], -log[2], 1.0])
                vx_ref[s, rows] = with_lanes(v, s, [1.0, 1.0, 1.0])
                gx_ref[s, rows] = with_lanes(grad, s, [-delta[0], -delta[1], -delta[2]])
        for s in range(2):
            dq_ref[s] = jnp.zeros((length, 128), F32)

            def step(b, _):
                rows = pl.ds(pl.multiple_of(b * 2 * pad, 16), 2 * pad)
                k = kx_ref[s, rows]
                probs = jnp.exp(nt(k, qx_ref[s]))
                grad_scores = (probs * nt(vx_ref[s, rows], gx_ref[s])).astype(BF)
                dv = nn(probs.astype(BF), gx_ref[s])
                dk = nn(grad_scores, qx_ref[s]) * scale
                if s == 0:
                    dv_ref[rows] = dv
                    dk_ref[rows] = dk
                else:
                    dv_ref[rows] = jnp.where(half_mask(s), dv, dv_ref[rows])
                    dk_ref[rows] = jnp.where(half_mask(s), dk, dk_ref[rows])
                dq_ref[s] += tn(grad_scores, k)
                return 0

            lax.fori_loop(0, ranks // 2, step, 0)
        sum_ref[...] = jnp.zeros_like(sum_ref)
        for r in blocks:
            rows = rows_of(r)
            c, s = cos_ref[rows], -sin_ref[rows]
            dq = turn(jnp.where(half_mask(0), dq_ref[0, rows], dq_ref[1, rows]), c, s).astype(BF)
            dv = dv_ref[rows].astype(BF)
            d_ref[rows, 0:128] = dq
            d_ref[rows, 128:256] = turn(dk_ref[rows], c, s).astype(BF)
            d_ref[rows, 256:384] = dv
            totals = [jnp.sum(t.astype(F32), axis=0, keepdims=True) for t in (dq, dv)]
            sum_ref[0:2] += jnp.concatenate(totals, axis=0)

    def attend_back(pair, after):
        return call(
            functools.partial(attend_back_body, pair), [((length, 384), BF), ((8, 128), F32)],
            queries, keys, values, attended, hat_mix, norm_mix, *shared_back, stat_mix, lines, cosine, sine,
            scratch=[pltpu.VMEM((2, length, 128), BF)] * 4
            + [pltpu.VMEM((2, length, 128), F32)] + [pltpu.VMEM((length, 128), F32)] * 2,
            name="attend_back", us=11, after=after, mib=14,
        )

    d_first, sum_first = attend_back(0, [out_token] if direct else [])
    if direct:
        added_out = dp_add(keep_out, across_out, "out_add", [d_first])
        got_out = dp_column_sums(added_out)
        keep_first, send_first, sum_one, first_token = qkv_grad(0, d_first, [added_out[1]])
    d_last, sum_last = attend_back(1, [first_token, added_out[1], finish_token] if direct else [])
    if direct:
        added_first = dp_add(keep_first, swap(send_first, "dp", 1), "first_add", [d_last])
        got_first = dp_column_sums(added_first)
        sum_ffn = dp_sum_step(sum_ffn, 4, [d_last])
        keep_last, send_last, sum_one, last_token = qkv_grad(
            1, d_last, [added_first[1], *got_out[1:], sum_ffn], sum_one
        )
        across_last = swap(send_last, "dp", 1)

    def vector_body(index_ref, one_ref, first_ref, last_ref, mix_ref, two_ref, out_ref):
        out_ref[...] = jnp.zeros_like(out_ref)
        out_ref[0:2] = one_ref[0:2]
        cols = pl.ds(pl.multiple_of(index_ref[1] * heads, 128), heads)
        out_ref[2:4, cols] = jnp.concatenate([first_ref[0:2], last_ref[0:2]], axis=1)
        out_ref[4:6, cols] = mix_ref[0:2]
        out_ref[6:10] = two_ref[0:4]

    if not direct:
        d_all = joined([d.astype(F32) for d in (d_first.T, d_last.T)]).T
        unit_d = joined([tn(unit_one, d).T for d in (d_first, d_last)]).T
        d_sum = jnp.sum(d_all, axis=0, keepdims=True)
        sum_one = jnp.stack([jnp.sum(w_qkv * v, axis=1) for v in (unit_d, jnp.broadcast_to(d_sum, unit_d.shape))])
        sum_one = jnp.pad(sum_one, ((0, 6), (0, 0)))
    (vectors,) = call(
        vector_body, [((16, width), F32)], index, sum_one, sum_first, sum_last, sum_mix, sum_two, specs=[SM] + [VM] * 5,
        name="vectors",
    )
    shared_vectors = tensor_share(vectors)
    if direct:
        def vector_chunk_body(index_ref, v0, v1, v2, v3, keep_ref, send_ref):
            for k in range(zs):
                for ref, side in ((keep_ref, index_ref[0] % 2), (send_ref, 1 - index_ref[0] % 2)):
                    cols = pl.ds(pl.multiple_of((((index_ref[0] // 2) ^ k) * 2 + side) * own_rows, 128), own_rows)
                    ref[k] = v0[:, cols] + v1[:, cols] + v2[:, cols] + v3[:, cols]

        keep_vec, send_vec = call(
            vector_chunk_body, [((zs, 16, own_rows), F32)] * 2, index, *shared_vectors, specs=[SM] + [VM] * 4,
            name="vector_chunks",
        )
        across_vec = swap(send_vec, "dp", 1)

    def project_back_body(first_block, d0_ref, d1_ref, w_ref, *part_refs):
        for r in (1, 0):
            rows = rows_of(first_block + r)
            grad = nt(d0_ref[rows], w_ref[:, :384]) + nt(d1_ref[rows], w_ref[:, 384:])
            part_refs[r][...] = grad[:block].astype(BF)

    projected = [None, None]
    for j in (1, 0):
        after = [across_vec, across_last, got_first[2]] if j and direct else []
        projected[j] = call(
            functools.partial(project_back_body, 2 * j), [((block, width), BF)] * 2, d_first, d_last, w_qkv,
            name="project_back", us=2, after=after,
        )
    arrived, _ = tensor_scatter([*projected[0], *projected[1]])

    def input_body(p0, p1, p2, x_ref, grad_ref, vec_ref, out_ref):
        grad_first = p0[...].astype(F32) + p1[...].astype(F32) + p2[...].astype(F32)
        x = x_ref[...].astype(F32)
        mean, inverse = center_scale(x)
        unit = (x - mean) * inverse
        out_ref[:, 0, :] = grad_ref[...] + unit_back(grad_first * vec_ref[F_GAIN : F_GAIN + 1], unit, inverse)

    input_grad, input_token = call(
        input_body, [((block, 1, width), F32)], *arrived, x_own, grad_hidden, vec, name="input_grad", store=(0,),
        token=True,
    )

    if direct:
        def last_add_body(keep_ref, across_ref, keep_vec_ref, across_vec_ref, own_ref, *send_refs):
            for k, ref in enumerate((own_ref, *send_refs)):
                ref[:own_rows] = (keep_ref[k].astype(F32) + across_ref[k].astype(F32)).astype(ref.dtype)
                ref[own_rows:] = jnp.zeros((16, 384), ref.dtype)
                ref[own_rows:, :own_rows] = (keep_vec_ref[k] + across_vec_ref[k]).astype(ref.dtype)

        got_last = dp_column_sums(call(
            last_add_body, [((own_rows + 16, 384), F32)] + [((own_rows + 16, 384), BF)] * (zs - 1),
            keep_last, across_last, keep_vec, across_vec, name="last_add", after=got_first[1:],
        ))

        def attn_finish_body(*refs):
            def total(parts):
                return sum(ref[...].astype(F32) for ref in parts)

            early, late = total(refs[:zs]), total(refs[zs : 2 * zs])
            q_ref, k_ref, v_ref, o_ref, model_ref = refs[3 * zs :]
            for k, ref in enumerate((q_ref, k_ref, v_ref)):
                cols = slice(k * 128, (k + 1) * 128)
                ref[:, 0:128] = early[:, cols]
                ref[:, 128:256] = late[:own_rows, cols]
            o_ref[...] = total(refs[2 * zs : 3 * zs]).T
            model_ref[...] = late[own_rows:, :own_rows]

        shapes = [(own_rows, heads)] * 3 + [(heads, own_rows), (16, own_rows)]
        q_grad, k_grad, v_grad, out_grad, model = call(
            attn_finish_body, [(shape, F32) for shape in shapes], *got_first, *got_last, *got_out, store=(0, 1, 2, 3),
            name="attn_finish", after=[input_token, finished_token],
        )
    else:
        qkv_all = vec[F_GAIN][:, None] * unit_d + vec[F_BIAS][:, None] * d_sum
        qkv_all = lax.psum_scatter(qkv_all.astype(BF), "dp", scatter_dimension=0, tiled=True).astype(F32).T
        qkv_all = qkv_all.reshape(2, 3, 128, own_rows)
        q_grad, k_grad, v_grad = (joined(list(qkv_all[:, k])).T for k in range(3))
        out_grad = plain_grad(branch, mixed).T
        model = lax.psum_scatter(sum(shared_vectors), "dp", scatter_dimension=1, tiled=True)
        sum_ffn = lax.psum(sum_ffn, "dp")
    ffn = sum_ffn[:, :hidden]
    return (
        layer_output[None], input_grad.transpose(1, 0, 2), q_grad, k_grad, v_grad,
        model[2], model[3], model[0], model[1], model[4], model[5], out_grad, model[8], model[6], model[7],
        gate_grad, up_grad, ffn[0], ffn[1], ffn[2], ffn[3], down_grad, model[9],
    )


def solution(mesh):
    rows, across, tokens = P("dp", "tensor"), P("tensor", "dp"), P("dp", "tensor", None)
    model, ffn, image = P("dp"), P("tensor"), P("dp", None)
    in_specs = (
        tokens, rows, rows, rows, model, model, model, model, model, model, across, model, model, model, rows, rows,
        ffn, ffn, ffn, ffn, across, model, tokens, image, image, image,
    )
    out_specs = (
        tokens, tokens, rows, rows, rows, model, model, model, model, model, model, across, model, model, model,
        rows, rows, ffn, ffn, ffn, ffn, across, model,
    )
    return jax.shard_map(local, mesh=mesh, in_specs=in_specs, out_specs=out_specs, check_vma=False)
```

```python
import functools
import math

import jax
import jax.numpy as jnp
from jax import lax
from jax.experimental import pallas as pl
from jax.experimental.pallas import tpu as pltpu
from jax.sharding import PartitionSpec as P

HD = 64
EPSILON = 1e-06
LOW = -1e30
BF = jnp.bfloat16
F32 = jnp.float32
HI = lax.Precision.HIGHEST
VM = pl.BlockSpec(memory_space=pltpu.VMEM)
SM = pl.BlockSpec(memory_space=pltpu.SMEM)
ANY = pl.BlockSpec(memory_space=pl.ANY)
HB = pl.BlockSpec(memory_space=pltpu.HBM)
Q_BIAS, V_BIAS, F_GAIN, F_BIAS, M_GAIN, M_BIAS, O_BIAS, S_GAIN, S_BIAS, D_BIAS = range(10)


def nn(a, b, precision=None):
    return lax.dot_general(a, b, (((1,), (0,)), ((), ())), precision, F32)


def nt(a, b, precision=None):
    return lax.dot_general(a, b, (((1,), (1,)), ((), ())), precision, F32)


def tn(a, b, precision=None):
    return lax.dot_general(a, b, (((0,), (0,)), ((), ())), precision, F32)


def call(
    body, outs, *args, specs=None, load=(), store=(), mib=8, us=1.0, name=None, after=(), scratch=(), token=False, **extra
):
    if token:
        outs = [*outs, ((8, 128), F32)]
    shapes = [jax.ShapeDtypeStruct(shape, dtype) for shape, dtype in outs]
    n_in, n_out, n_after, moved = len(args), len(outs), len(after), len(load) + len(store)
    specs = list(specs or [VM] * n_in)
    out_specs = [VM] * n_out
    for i in load:
        specs[i] = HB
    for i in store:
        out_specs[i] = HB
        shapes[i] = pltpu.HBM(*outs[i])
    args = [hbm(a) if s is HB else a for a, s in zip(args, specs)]
    held = [pltpu.VMEM(args[i].shape, args[i].dtype) for i in load] + [pltpu.VMEM(*outs[i]) for i in store]
    if moved:
        held.append(pltpu.SemaphoreType.DMA((moved,)))

    def run(*refs):
        ins, outs_ = list(refs[:n_in]), list(refs[n_in + n_after : n_in + n_after + n_out])
        rest = refs[n_in + n_after + n_out :]
        own, copies = rest[: len(scratch)], rest[len(scratch) :]
        reads = [pltpu.make_async_copy(ins[i], copies[j], copies[-1].at[j]) for j, i in enumerate(load)]
        for one in reads:
            one.start()
        for j, i in enumerate(load):
            ins[i] = copies[j]
        writes = []
        for j, i in enumerate(store, len(load)):
            writes.append(pltpu.make_async_copy(copies[j], outs_[i], copies[-1].at[j]))
            outs_[i] = copies[j]
        for one in reads:
            one.wait()
        body(*ins, *(outs_[:-1] if token else outs_), *own)
        for one in writes:
            one.start()
        for one in writes:
            one.wait()

    return pl.pallas_call(
        run,
        out_shape=shapes,
        in_specs=specs + [ANY] * n_after,
        out_specs=out_specs,
        scratch_shapes=list(scratch) + held,
        compiler_params=pltpu.CompilerParams(vmem_limit_bytes=mib << 20),
        cost_estimate=pl.CostEstimate(flops=int(us * 1.1e7), bytes_accessed=1 << 10, transcendentals=0),
        name=name,
        **extra,
    )(*args, *after)


def swap(value, axis, offset):
    count = lax.axis_size(axis)
    return lax.ppermute(value, axis, [(i, i ^ offset) for i in range(count)])


def tensor_gather(block):
    core = swap(block, "tensor", 1)
    far = swap(block, "tensor", 2)
    return [block, core, far, swap(far, "tensor", 1)]


def add_pair_body(a_ref, b_ref, out_ref):
    out_ref[...] = (a_ref[...].astype(F32) + b_ref[...].astype(F32)).astype(BF)


def tensor_scatter(parts, after=()):
    third = swap(parts[3], "tensor", 1)
    first = swap(parts[1], "tensor", 1)
    (to_far,) = call(add_pair_body, [(third.shape, BF)], parts[2], third, name="add_pair", after=after)
    return [parts[0], first, swap(to_far, "tensor", 2)], to_far


def tensor_share(value):
    return [value] + [swap(value, "tensor", k) for k in (1, 2, 3)]


def dp_column(block):
    return [block] + [swap(block, "dp", 2 * k) for k in range(1, lax.axis_size("dp") // 2)]


def dp_across(column):
    return [one for mine in column for one in (mine, swap(mine, "dp", 1))]


def hbm(value):
    return pltpu.with_memory_space_constraint(value, pltpu.HBM)


def tie(value, *others, held=False):
    def body(*refs):
        pass

    return pl.pallas_call(
        body,
        out_shape=pltpu.HBM(value.shape, value.dtype),
        in_specs=[HB] + [HB if held else ANY] * len(others),
        out_specs=HB,
        input_output_aliases={0: 0},
        cost_estimate=pl.CostEstimate(flops=1, bytes_accessed=1, transcendentals=0),
        compiler_params=pltpu.CompilerParams(vmem_limit_bytes=1 << 20),
        name="tie",
    )(hbm(value), *[hbm(v) if held else v for v in others])


def hold(values, *others, held=False):
    count = len(values)

    def body(*refs):
        refs, held, sems = refs[: -count - 1], refs[-count - 1 : -1], refs[-1]
        reads = [pltpu.make_async_copy(refs[i], held[i], sems.at[0, i]) for i in range(count)]
        writes = [pltpu.make_async_copy(held[i], refs[i - count], sems.at[1, i]) for i in range(count)]
        for one in reads:
            one.start()
        for read, write in zip(reads, writes):
            read.wait()
            write.start()
        for one in writes:
            one.wait()

    return pl.pallas_call(
        body,
        out_shape=[pltpu.HBM(v.shape, v.dtype) for v in values],
        in_specs=[ANY] * count + [HB if held else ANY] * len(others),
        out_specs=[HB] * count,
        scratch_shapes=[pltpu.VMEM(v.shape, v.dtype) for v in values] + [pltpu.SemaphoreType.DMA((2, count))],
        cost_estimate=pl.CostEstimate(flops=1, bytes_accessed=1, transcendentals=0),
        compiler_params=pltpu.CompilerParams(vmem_limit_bytes=4 << 20),
        name="hold",
    )(*values, *[hbm(v) if held else v for v in others])


def center_scale(values):
    width = values.shape[-1]
    mean = jnp.sum(values, axis=-1, keepdims=True) / width
    spread = jnp.sum(values * values, axis=-1, keepdims=True) / width - mean * mean
    return mean, lax.rsqrt(spread + EPSILON)


def unit_back(grad_hat, unit, inverse):
    width = unit.shape[-1]
    mean = jnp.sum(grad_hat, axis=-1, keepdims=True) / width
    cross = jnp.sum(grad_hat * unit, axis=-1, keepdims=True) / width
    return inverse * (grad_hat - mean - unit * cross)


def columns_to_rows(columns):
    count = columns[0].shape[0]
    lanes = lax.broadcasted_iota(jnp.int32, (count, 128), 1)
    wide = jnp.zeros((count, 128), F32)
    for k, column in enumerate(columns):
        wide = jnp.where(lanes == k, column, wide)
    return wide.T[0:8]


def rows_to_columns(rows):
    return rows.T


def summed_stats(refs, r):
    return refs[0][r] + refs[1][r ^ 1] + refs[2][r ^ 2] + refs[3][r ^ 3]


def turn(values, cosine, sine):
    lanes = lax.broadcasted_iota(jnp.int32, values.shape, 1)
    other = jnp.where(lanes % 2 == 0, pltpu.roll(values, 127, 1), pltpu.roll(values, 1, 1))
    return values * cosine + other * sine


def half_mask(s):
    lane = lax.broadcasted_iota(jnp.int32, (1, 128), 1)
    return lane < HD if s == 0 else lane >= HD


def local(
    layer_input, query_weight, key_weight, value_weight, query_bias, value_bias, first_gain, first_bias,
    mixer_gain, mixer_bias, output_weight, output_bias, second_gain, second_bias, gate_weight, up_weight,
    gate_bias, up_bias, inner_gain, inner_bias, down_weight, down_bias, cotangent, key_valid, patch_row, patch_column,
):
    ranks = lax.axis_size("tensor")
    me_t, me_d, count_d = lax.axis_index("tensor"), lax.axis_index("dp"), lax.axis_size("dp")
    block, width = layer_input.shape[1:]
    pad = -(-block // 16) * 16
    length = ranks * pad
    heads = query_weight.shape[1]
    hidden = gate_weight.shape[1]
    hidden_pad = -(-hidden // 128) * 128
    own_rows = width // count_d
    direct = own_rows % 128 == 0 and count_d & (count_d - 1) == 0
    index = jnp.stack([me_d, me_t]).astype(jnp.int32)
    x_own, cot_own = layer_input[0], cotangent[0]
    blocks = range(ranks)

    def rows_of(r):
        return slice(r * pad, (r + 1) * pad)

    lines = jnp.stack([key_valid[0], patch_row[0], patch_column[0], jnp.arange(ranks * block, dtype=jnp.int32)])
    lines = jnp.pad(lines.reshape(4, ranks, block), ((0, 4), (0, 0), (0, pad - block))).astype(F32)
    lines = jnp.stack([lax.dynamic_index_in_dim(lines, me_t ^ r, 1, False) for r in blocks])
    lane = jnp.arange(128)
    frequency = jnp.power(F32(10000.0), -((lane % HD) // 2 % (HD // 4)).astype(F32) / (HD // 4))
    frequency = jnp.broadcast_to(frequency[None, :], (8, 128))

    def table_body(line_ref, frequency_ref, cos_ref, sin_ref):
        lanes = lax.broadcasted_iota(jnp.int32, (pad, 128), 1)
        for r in blocks:
            columns = rows_to_columns(line_ref[r])
            position = jnp.where(lanes % HD < HD // 2, columns[:, 1:2], columns[:, 2:3])
            angle = jnp.where(columns[:, 3:4] > 0.0, 0.5 * (position * frequency_ref[0:1]), 0.0)
            cos_ref[rows_of(r)] = jnp.cos(angle)
            sine = jnp.sin(angle)
            sin_ref[rows_of(r)] = jnp.where(lanes % 2 == 0, -sine, sine)

    cosine, sine = call(table_body, [((length, 128), F32)] * 2, lines, frequency, name="tables", us=4)

    small = [
        v[None, :]
        for v in (
            query_bias, value_bias, first_gain, first_bias, mixer_gain, mixer_bias, output_bias, second_gain,
            second_bias, down_bias,
        )
    ]
    tiles = heads // 128
    hidden_low = -(-hidden // 16) * 16
    starts = [(k % 3) * tiles + k // 3 for k in range(3 * tiles)]
    if direct:
        o_start = 3 * tiles * own_rows + 16

        def pack_a_body(q_ref, k_ref, v_ref, w_ref, *refs):
            *small_refs, out_ref = refs
            out_ref[o_start:] = w_ref[...]
            for k in range(3 * tiles):
                ref = (q_ref, k_ref, v_ref)[k % 3]
                out_ref[k * own_rows : (k + 1) * own_rows] = ref[:, k // 3 * 128 : (k // 3 + 1) * 128]
            lines = [ref[...].astype(F32) for ref in small_refs]
            lines.append(jnp.zeros((16 - len(lines), own_rows), F32))
            out_ref[3 * tiles * own_rows : o_start] = jnp.concatenate(lines, axis=0).astype(BF)

        (pack_a,) = call(
            pack_a_body, [((o_start + heads, 128), BF)], query_weight, key_weight, value_weight, output_weight,
            *small, name="pack_a", load=tuple(range(14)),
        )
        column_a = dp_column(pack_a)
        x_far = swap(x_own, "tensor", 2)
        (pack_later,) = hold([pack_a], cosine)
        across_first = swap(pack_later, "dp", 1)
        (column_a[3],) = hold([column_a[3]], cosine)
        across_last = swap(column_a[3], "dp", 1)
        (column_a[2],) = hold([column_a[2]], column_a[3], held=True)
        column_a[1], across_first, x_held, x_far = hold(
            [column_a[1], across_first, x_own, x_far], column_a[2], across_last, held=True
        )
        across_a = [across_first] + [swap(one, "dp", 1) for one in column_a[1:3]] + [across_last]
        x_blocks = [x_own, swap(x_held, "tensor", 1), x_far, swap(x_far, "tensor", 1)]
        got_a = [one for pair in zip(column_a, across_a) for one in pair]

        def pack_f_body(g_ref, u_ref, d_ref, out_ref):
            for j, ref in enumerate((g_ref, u_ref, d_ref)):
                out_ref[(j + 1) * hidden_low - 16 : (j + 1) * hidden_low] = jnp.zeros((16, own_rows), BF)
                out_ref[j * hidden_low : j * hidden_low + hidden] = ref[...]

        (pack_f,) = call(
            pack_f_body, [((3 * hidden_low, own_rows), BF)], gate_weight.T, up_weight.T, down_weight, name="pack_f",
            load=(0, 1, 2),
        )
        got_f = lax.all_gather(tie(pack_f, *column_a[1:], held=True), "dp")
        def copies(pairs, sems):
            started = [pltpu.make_async_copy(a, b, sems.at[i]) for i, (a, b) in enumerate(pairs)]
            for one in started:
                one.start()
            for one in started:
                one.wait()

        def chunk_at(index_ref, r):
            return pl.ds(pl.multiple_of((index_ref[0] ^ r) * own_rows, 128), own_rows)

        def assemble_a(index_ref, *refs):
            *chunks, cot_ref = refs[: count_d + 1]
            w_ref, v_ref, o_ref, cot_out, small_ref, held_ref, sems, cot_sems = refs[count_d + 1 :]
            cot_read = pltpu.make_async_copy(cot_ref, held_ref, cot_sems.at[0])
            cot_write = pltpu.make_async_copy(held_ref, cot_out, cot_sems.at[1])
            cot_read.start()
            pairs = []
            for r, chunk in enumerate(chunks):
                for k in range(3 * tiles):
                    pairs.append((
                        chunk.at[k * own_rows : (k + 1) * own_rows],
                        w_ref.at[chunk_at(index_ref, r), k * 128 : (k + 1) * 128],
                    ))
                pairs.append((chunk.at[3 * tiles * own_rows : o_start], small_ref.at[r]))
                pairs.append((chunk.at[o_start:], o_ref.at[:, chunk_at(index_ref, r)]))
            started = [pltpu.make_async_copy(a, b, sems.at[i]) for i, (a, b) in enumerate(pairs)]
            for one in started:
                one.start()
            cot_read.wait()
            cot_write.start()
            for one in started:
                one.wait()
            for r in range(count_d):
                v_ref[:, chunk_at(index_ref, r)] = small_ref[r].astype(F32)
            cot_write.wait()

        specs = [SM] + [HB] * count_d

        def dma(count):
            return pltpu.SemaphoreType.DMA((count,))

        shapes = [((width, 3 * heads), BF), ((16, width), F32), ((heads, width), BF), (cot_own.shape, BF)]
        w_qkv, vec, w_out, cot_held = pl.pallas_call(
            assemble_a,
            out_shape=[jax.ShapeDtypeStruct(*shape) for shape in shapes[:3]] + [pltpu.HBM(*shapes[3])],
            in_specs=specs + [HB],
            out_specs=[VM] * 3 + [HB],
            scratch_shapes=[
                pltpu.VMEM((count_d, 16, 128), BF), pltpu.VMEM(*shapes[3]), dma(count_d * (3 * tiles + 2)), dma(2)
            ],
            compiler_params=pltpu.CompilerParams(vmem_limit_bytes=4 << 20),
            cost_estimate=pl.CostEstimate(flops=1 << 10, bytes_accessed=1 << 10, transcendentals=0),
            name="assemble_a",
        )(index, *[hbm(v) for v in got_a], hbm(cot_own))
        cot_blocks = tensor_gather(cot_held)
    else:
        def whole(weight, axis):
            return lax.all_gather(weight, "dp", axis=axis, tiled=True)

        x_blocks = tensor_gather(x_own)
        cot_blocks = tensor_gather(cot_own)
        w_qkv = whole(jnp.concatenate(
            [(query_weight, key_weight, value_weight)[k % 3][:, k // 3 * 128 : (k // 3 + 1) * 128] for k in range(3 * tiles)],
            axis=1,
        ), 0)
        vec = jnp.pad(whole(jnp.concatenate(small), 1).astype(F32), ((0, 6), (0, 0)))
        w_out = whole(output_weight, 1)
        w_gate, w_up, w_down = (
            jnp.pad(whole(w, 1), ((0, hidden_pad - hidden), (0, 0))) for w in (gate_weight.T, up_weight.T, down_weight)
        )
    ffn_vec = jnp.pad(
        jnp.stack([gate_bias, up_bias, inner_gain, inner_bias]).astype(F32), ((0, 4), (0, hidden_pad - hidden))
    )

    def own(ref, k, index_ref):
        return ref[k : k + 1, pl.ds(pl.multiple_of(index_ref[1] * heads, 128), heads)]

    n_heads = heads // HD

    def attend_body(
        index_ref, x0, x1, x2, x3, w_ref, vec_ref, cos_ref, sin_ref, line_ref,
        unit_out, q_out, k_out, v_out, o_ref, stat_ref, unit_ref, q_ref, k_ref, v_ref, first_ref, x_ref, cos_held,
        sin_held, sems, load_sems,
    ):
        pairs = [(x0, x_ref.at[0]), (x2, x_ref.at[1]), (cos_ref, cos_held), (sin_ref, sin_held)]
        reads = [pltpu.make_async_copy(a, b, load_sems.at[i]) for i, (a, b) in enumerate(pairs)]
        for one in reads:
            one.start()
        gain, bias = vec_ref[F_GAIN : F_GAIN + 1], vec_ref[F_BIAS : F_BIAS + 1]
        q_bias, v_bias = own(vec_ref, Q_BIAS, index_ref), own(vec_ref, V_BIAS, index_ref)
        moves = []
        for r in blocks:
            if r % 2 == 0:
                reads[r // 2].wait()
            x = (x_ref[0] if r == 0 else x1[...] if r == 1 else x_ref[1] if r == 2 else x3[...]).astype(F32)
            mean, inverse = center_scale(x)
            unit = (x - mean) * inverse
            unit_ref[(r + 1) * pad - 16 : (r + 1) * pad] = jnp.zeros((16, width), BF)
            unit_ref[r * pad : r * pad + block] = unit.astype(BF)
            first_ref[pad - 16 :] = jnp.zeros((16, width), BF)
            first_ref[:block] = (unit * gain + bias).astype(BF)
            rows = rows_of(r)
            qkv = nn(first_ref[...], w_ref[...])
            if r == 0:
                reads[2].wait()
                reads[3].wait()
            c, s = cos_held[rows], sin_held[rows]
            for k in range(tiles):
                cols = slice(k * 128, (k + 1) * 128)
                q, key, v = (qkv[:, (3 * k + j) * 128 : (3 * k + j + 1) * 128] for j in range(3))
                q_ref[rows, cols] = turn(q + q_bias[:, cols], c, s).astype(BF)
                k_ref[rows, cols] = turn(key, c, s).astype(BF)
                v_ref[rows, cols] = (v + v_bias[:, cols]).astype(BF)
            for j, (held, out) in enumerate(
                ((unit_ref, unit_out), (q_ref, q_out), (k_ref, k_out), (v_ref, v_out))
            ):
                moves.append(pltpu.make_async_copy(held.at[rows], out.at[rows], sems.at[4 * r + j]))
                moves[-1].start()
        mask_line = jnp.concatenate([jnp.where(line_ref[r][0:1] == 1.0, 0.0, LOW) for r in blocks], axis=1)
        k_half, v_half = [], []
        for h in range(n_heads):
            cols = slice(h // 2 * 128, (h // 2 + 1) * 128)
            k_half.append(jnp.where(half_mask(h % 2), k_ref[:, cols], 0).astype(BF))
            v_half.append(jnp.where(half_mask(h % 2), v_ref[:, cols], 0).astype(BF))

        def step(b, _):
            rows = pl.ds(pl.multiple_of(b * pad, 16), pad)
            kept = []
            total = jnp.zeros((pad, 1), F32)
            square = jnp.zeros((pad, 1), F32)
            for pair in range(tiles):
                cols = slice(pair * 128, (pair + 1) * 128)
                q = q_ref[rows, cols]
                out = jnp.zeros((pad, 128), F32)
                for s in range(2):
                    h = 2 * pair + s
                    scores = nt(q, k_half[h]) * (1.0 / math.sqrt(HD)) + mask_line
                    top = jnp.max(scores, axis=-1, keepdims=True)
                    terms = jnp.exp(scores - top)
                    below = jnp.sum(terms, axis=-1, keepdims=True)
                    out += nn(terms.astype(BF), v_half[h]) * (1.0 / below)
                    kept.append(top + jnp.log(below))
                o_ref[rows, cols] = out
                total += jnp.sum(out, axis=-1, keepdims=True)
                square += jnp.sum(out * out, axis=-1, keepdims=True)
            stat_ref[b] = columns_to_rows(kept + [total, square])
            return 0

        lax.fori_loop(0, ranks, step, 0)
        for one in moves:
            one.wait()

    shapes = [((length, width), BF)] + [((length, heads), BF)] * 3
    unit_one, queries, keys, values, attended, stat_mix = pl.pallas_call(
        attend_body,
        out_shape=[pltpu.HBM(*shape) for shape in shapes]
        + [jax.ShapeDtypeStruct((length, heads), F32), jax.ShapeDtypeStruct((ranks, 8, pad), F32)],
        in_specs=[SM] + [HB, VM] * 2 + [VM] * 2 + [HB] * 2 + [VM],
        out_specs=[HB] * 4 + [VM] * 2,
        scratch_shapes=[pltpu.VMEM(*shape) for shape in shapes]
        + [pltpu.VMEM((pad, width), BF), pltpu.VMEM((2, block, width), BF)]
        + [pltpu.VMEM((length, 128), F32)] * 2
        + [pltpu.SemaphoreType.DMA((4 * ranks,)), pltpu.SemaphoreType.DMA((4,))],
        compiler_params=pltpu.CompilerParams(vmem_limit_bytes=22 << 20),
        cost_estimate=pl.CostEstimate(flops=1 << 17, bytes_accessed=1 << 10, transcendentals=0),
        name="attend",
    )(index, hbm(x_blocks[0]), x_blocks[1], hbm(x_blocks[2]), x_blocks[3], w_qkv, vec, hbm(cosine), hbm(sine), lines)
    shared_mix = tensor_share(stat_mix)

    def mix_body(index_ref, a_ref, s0, s1, s2, s3, w_ref, vec_ref, mixed_ref, norm_ref, *part_refs):
        gain, bias = own(vec_ref, M_GAIN, index_ref), own(vec_ref, M_BIAS, index_ref)
        for r in reversed(blocks):
            rows = rows_of(r)
            sums = summed_stats((s0, s1, s2, s3), r)
            mean = sums[n_heads : n_heads + 1] / width
            inverse = lax.rsqrt(sums[n_heads + 1 : n_heads + 2] / width - mean * mean + EPSILON)
            lines = jnp.concatenate([mean, inverse, jnp.zeros((6, pad), F32)], axis=0)
            norm_ref[r] = lines
            columns = rows_to_columns(lines)
            mixed = ((a_ref[rows] - columns[:, 0:1]) * columns[:, 1:2] * gain + bias).astype(BF)
            mixed_ref[rows] = mixed
            part_refs[r][...] = nn(mixed, w_ref[...])[:block].astype(BF)

    mixed, norm_mix, *parts = call(
        mix_body, [((length, heads), BF), ((ranks, 8, pad), F32)] + [((block, width), BF)] * ranks,
        index, attended, *shared_mix, w_out, vec, specs=[SM] + [VM] * 7, name="mix", us=2.5,
        store=(0,), after=[cot_blocks[2]],
    )
    arrived, _ = tensor_scatter(parts)

    def second_body(x_ref, p0, p1, p2, vec_ref, hidden_ref, second_ref):
        out = p0[...].astype(F32) + p1[...].astype(F32) + p2[...].astype(F32)
        state = x_ref[...].astype(F32) + out + vec_ref[O_BIAS : O_BIAS + 1]
        hidden_ref[...] = state
        mean, inverse = center_scale(state)
        unit = (state - mean) * inverse
        second_ref[...] = (unit * vec_ref[S_GAIN : S_GAIN + 1] + vec_ref[S_BIAS : S_BIAS + 1]).astype(BF)

    hidden_state, second_own = call(
        second_body, [((block, width), F32), ((block, width), BF)], x_own, *arrived, vec, name="second", store=(0, 1),
    )
    half = 2 * pad

    def half_rows(r):
        return slice(r % 2 * pad, (r % 2 + 1) * pad)

    def pad_block(ref, r, value):
        start = r * pad
        ref[start + pad - 16 : start + pad] = jnp.zeros((16, width), BF)
        ref[start : start + block] = value

    def expand(b_refs, wg_ref, wu_ref, vec_ref, grad_ref, second_ref, gate_ref, up_ref, stat_ref, base):
        for r, b_ref in enumerate(b_refs):
            rows = half_rows(r)
            pad_block(second_ref, r, b_ref[...])
            gate = nt(second_ref[rows], wg_ref[...]) + vec_ref[0:1]
            up = nt(second_ref[rows], wu_ref[...]) + vec_ref[1:2]
            gate_ref[rows] = gate
            up_ref[rows] = up
            activated = gate * jax.nn.sigmoid(gate) * up
            hat = grad_ref[rows] * vec_ref[2:3]
            stat_ref[base + r] = columns_to_rows(
                [jnp.sum(v, axis=-1, keepdims=True) for v in (activated, activated * activated, hat, hat * activated)]
            )

    def expand_first_body(c0, c1, c2, c3, b0, b1, vec_ref, *refs):
        if direct:
            chunks, *refs, down_sems, gate_sems = refs
            wg_ref, wu_ref, wd_ref = refs[:3]
            outs = refs[3:]
            moves = []
            for j, (out, sems) in enumerate(((wd_ref, down_sems), (wg_ref, gate_sems), (wu_ref, gate_sems))):
                for a in range(count_d):
                    start = (2, 0, 1)[j] * hidden_low
                    moves.append(pltpu.make_async_copy(
                        chunks.at[a, start : start + hidden_low],
                        out.at[0:hidden_low, a * own_rows : (a + 1) * own_rows],
                        sems.at[a if j < 2 else count_d + a],
                    ))
                    moves[-1].start()
            for out in (wg_ref, wu_ref, wd_ref):
                out[hidden_low:] = jnp.zeros((hidden_pad - hidden_low, width), BF)
            for one in moves[:count_d]:
                one.wait()
        else:
            wg_ref, wu_ref, wd_ref = refs[:3]
            outs = refs[3:]
        cot0, cot1, grad0, grad1, second_ref, gate_ref, up_ref, stat_ref = outs
        for r, c_ref in enumerate((c0, c1, c2, c3)):
            cot_ref, grad_ref = ((cot0, grad0), (cot1, grad1))[r // 2]
            pad_block(cot_ref, r % 2, c_ref[...])
            grad_ref[half_rows(r)] = nt(cot_ref[half_rows(r)], wd_ref[...])
        if direct:
            for one in moves[count_d:]:
                one.wait()
        expand((b0, b1), wg_ref, wu_ref, vec_ref, grad0, second_ref, gate_ref, up_ref, stat_ref, 0)

    half_outs = [((half, width), BF)] + [((half, hidden_pad), F32)] * 2
    second_far = swap(second_own, "tensor", 2)
    blocks_in = [*cot_blocks, second_own, swap(second_own, "tensor", 1), ffn_vec]
    outs = [((half, width), BF)] * 2 + [((half, hidden_pad), F32)] * 2 + half_outs + [((2, 8, pad), F32)]
    weights = [((hidden_pad, width), BF)] * 3
    if direct:
        w_gate, w_up, w_down, *made = call(
            expand_first_body, weights + outs, *blocks_in, got_f, specs=[VM] * 7 + [HB], name="expand_first",
            scratch=[dma(count_d), dma(2 * count_d)], us=10, load=tuple(range(6)),
        )
    else:
        made = call(expand_first_body, outs, *blocks_in, w_gate, w_up, w_down, name="expand_first", us=10)
    cot_halves, grad_inner, first_half = made[:2], made[2:4], made[4:]

    def expand_body(b0, b1, wg_ref, wu_ref, vec_ref, grad_ref, before_ref, second_ref, gate_ref, up_ref, stat_ref):
        stat_ref[0:2] = before_ref[...]
        expand((b0, b1), wg_ref, wu_ref, vec_ref, grad_ref, second_ref, gate_ref, up_ref, stat_ref, 2)

    second_far = tie(second_far, first_half[3])
    expanded = [first_half, call(
        expand_body, half_outs + [((4, 8, pad), F32)], second_far, swap(second_far, "tensor", 1), w_gate, w_up, ffn_vec,
        grad_inner[1], first_half[3], name="expand", us=3.7, load=(0,),
    )]
    shared_ffn = tensor_share(expanded[1][3])

    def ffn_back_body(
        first_block, g_ref, u_ref, grad_ref, s0, s1, s2, s3, vec_ref, wg_ref, wu_ref, *refs
    ):
        dg_ref, du_ref, inner_ref, sum_ref, *part_refs = refs[-6:]
        wide = hidden * ranks
        sum_ref[...] = refs[0][...] if len(refs) == 7 else jnp.zeros_like(sum_ref)
        for r in (1, 0):
            rows = half_rows(r)
            sums = summed_stats((s0, s1, s2, s3), first_block + r)
            mean = sums[0:1] / wide
            inverse = lax.rsqrt(sums[1:2] / wide - mean * mean + EPSILON)
            grad_mean = sums[2:3] / wide
            cross = inverse * (sums[3:4] / wide - mean * grad_mean)
            columns = rows_to_columns(
                jnp.concatenate([mean, inverse, grad_mean, cross, jnp.zeros((4, pad), F32)], axis=0)
            )
            mean, inverse, grad_mean, cross = (columns[:, k : k + 1] for k in range(4))
            gate, up, grad = g_ref[rows], u_ref[rows], grad_ref[rows]
            sigmoid = jax.nn.sigmoid(gate)
            silu = gate * sigmoid
            unit = (silu * up - mean) * inverse
            inner_ref[rows] = (unit * vec_ref[2:3] + vec_ref[3:4]).astype(BF)
            grad_act = inverse * (grad * vec_ref[2:3] - grad_mean - unit * cross)
            d_gate = (grad_act * up * sigmoid * (1.0 + gate - silu)).astype(BF)
            d_up = (grad_act * silu).astype(BF)
            dg_ref[rows] = d_gate
            du_ref[rows] = d_up
            totals = [d_gate.astype(F32), d_up.astype(F32), grad * unit, grad]
            sum_ref[0:4] += jnp.concatenate([jnp.sum(v, axis=0, keepdims=True) for v in totals], axis=0)
            part_refs[r][...] = (nn(d_gate, wg_ref[...]) + nn(d_up, wu_ref[...]))[:block].astype(BF)

    backed = [None, None]
    for j in (1, 0):
        before = [backed[1][3]] if j == 0 else []
        backed[j] = call(
            functools.partial(ffn_back_body, 2 * j),
            [((half, hidden_pad), BF)] * 3 + [((8, hidden_pad), F32)] + [((block, width), BF)] * 2,
            *expanded[j][1:3], grad_inner[j], *shared_ffn, ffn_vec, w_gate, w_up, *before, name="ffn_back", us=5.5,
            store=() if j else (4, 5),
        )
    sum_ffn = backed[0][3]
    arrived, to_far = tensor_scatter([*backed[0][4:], *backed[1][4:]])

    def dp_sum_step(total, k, after):
        def body(a_ref, b_ref, out_ref):
            out_ref[...] = a_ref[...] + b_ref[...]

        return call(body, [(total.shape, F32)], total, swap(total, "dp", k), name="dp_sum", after=after)[0]

    if direct:
        rows_f = 3 * hidden_low

        def ffn_grad_body(g0, g1, u0, u1, i0, i1, e0, e1, c0, c1, after_ref, out_ref, token_ref, made_ref, sems):
            moves = []
            for j, (rights, lefts) in enumerate((((g0, g1), (e0, e1)), ((u0, u1), (e0, e1)), ((i0, i1), (c0, c1)))):
                for at in range(0, hidden_low, 256):
                    stop = min(at + 256, hidden_low)
                    cols = slice(at, min(at + 256, hidden_pad))
                    total = sum(tn(a[:, cols], b[...]) for a, b in zip(rights, lefts)).astype(BF)
                    for d in range(count_d):
                        made_ref[d, j * hidden_low + at : j * hidden_low + stop] = (
                            total[: stop - at, d * own_rows : (d + 1) * own_rows]
                        )
                    rows = slice(j * hidden_low + at, j * hidden_low + stop)
                    moves.append(pltpu.make_async_copy(made_ref.at[:, rows], out_ref.at[:, rows], sems.at[len(moves)]))
                    moves[-1].start()
            for one in moves:
                one.wait()

        shape = ((count_d, rows_f, own_rows), BF)
        pieces = 3 * -(-hidden_low // 256)
        ffn_grads, ffn_token = pl.pallas_call(
            ffn_grad_body,
            out_shape=[pltpu.HBM(*shape), jax.ShapeDtypeStruct((8, 128), F32)],
            in_specs=[VM] * 10 + [ANY],
            out_specs=[HB, VM],
            scratch_shapes=[pltpu.VMEM(*shape), pltpu.SemaphoreType.DMA((pieces,))],
            compiler_params=pltpu.CompilerParams(vmem_limit_bytes=10 << 20),
            cost_estimate=pl.CostEstimate(flops=1 << 17, bytes_accessed=1 << 10, transcendentals=0),
            name="ffn_grad",
        )(
            *(backed[j][k] for k in (0, 1, 2) for j in range(2)), expanded[0][0], expanded[1][0], *cot_halves, to_far
        )
        ffn_grads = ffn_grads.reshape(count_d * rows_f, own_rows)
        ffn_grads = tie(ffn_grads, arrived[2])
        got_ffn = lax.psum_scatter(ffn_grads, "dp", scatter_dimension=0, tiled=True)

        def ffn_finish_body(p_ref, *out_refs):
            for j, ref in enumerate(out_refs):
                ref[...] = p_ref[j * hidden_low : j * hidden_low + hidden].astype(F32)

        gate_grad, up_grad, down_grad, finished_token = call(
            ffn_finish_body, [((hidden, own_rows), F32)] * 3, got_ffn, store=(0, 1, 2), load=(0,), name="ffn_finish",
            token=True,
        )
        gate_grad, up_grad = gate_grad.T, up_grad.T
    else:
        def plain_grad(left, right):
            return lax.psum_scatter(tn(left, right).astype(BF), "dp", scatter_dimension=0, tiled=True).astype(F32)

        def joined(pair):
            return jnp.concatenate(pair)

        second_all = joined([expanded[j][0] for j in range(2)])
        down_grad = plain_grad(joined(cot_halves), joined([backed[j][2] for j in range(2)]))[:, :hidden].T
        gate_grad = plain_grad(second_all, joined([backed[j][0] for j in range(2)]))[:, :hidden]
        up_grad = plain_grad(second_all, joined([backed[j][1] for j in range(2)]))[:, :hidden]

    def hidden_back_body(p0, p1, p2, h_ref, cot_ref, vec_ref, grad_ref, branch_ref, sum_ref):
        grad_second = p0[...].astype(F32) + p1[...].astype(F32) + p2[...].astype(F32)
        mean, inverse = center_scale(h_ref[...])
        unit = (h_ref[...] - mean) * inverse
        cot = cot_ref[...].astype(F32)
        grad = cot + unit_back(grad_second * vec_ref[S_GAIN : S_GAIN + 1], unit, inverse)
        branch = grad.astype(BF)
        grad_ref[...] = grad
        branch_ref[...] = branch
        lines = [grad_second * unit, grad_second, branch.astype(F32), cot]
        lines = [jnp.sum(v, axis=0, keepdims=True) for v in lines]
        sum_ref[...] = jnp.concatenate(lines + [jnp.zeros((4, width), F32)], axis=0)

    grad_hidden, branch_own, sum_two = call(
        hidden_back_body, [((block, width), F32), ((block, width), BF), ((8, width), F32)],
        *arrived, hidden_state, cot_own, vec, name="hidden_back", after=[ffn_token] if direct else [],
        store=(0,), load=(0, 2, 3, 4),
    )

    def down_body(i0, i1, w_ref, *part_refs):
        for r in reversed(blocks):
            part_refs[r][...] = nn((i0, i1)[r // 2][half_rows(r)], w_ref[...])[:block].astype(BF)

    if direct:
        sum_ffn = dp_sum_step(sum_ffn, 1, [branch_own])
    *down_parts, down_token = call(
        down_body, [((block, width), BF)] * ranks, backed[0][2], backed[1][2], w_down, name="down", us=2.5, token=True,
        after=[sum_ffn],
    )
    branch_far = swap(branch_own, "tensor", 2)
    branch_core = swap(branch_own, "tensor", 1)
    if direct:
        sum_ffn = dp_sum_step(sum_ffn, 2, [down_token])
    branch_far = tie(branch_far, sum_ffn)
    branch_blocks = [branch_own, branch_core, branch_far, swap(branch_far, "tensor", 1)]

    def mix_back_body(index_ref, b0, b1, b2, b3, w_ref, a_ref, norm_ref, vec_ref, branch_ref, grad_ref, stat_ref, sum_ref):
        gain = own(vec_ref, M_GAIN, index_ref)
        sum_ref[...] = jnp.zeros_like(sum_ref)
        for r, b_ref in enumerate((b0, b1, b2, b3)):
            rows = rows_of(r)
            branch_ref[(r + 1) * pad - 16 : (r + 1) * pad] = jnp.zeros((16, width), BF)
            branch_ref[r * pad : r * pad + block] = b_ref[...]
            grad = nt(branch_ref[rows], w_ref[...])
            columns = rows_to_columns(norm_ref[r])
            unit = (a_ref[rows] - columns[:, 0:1]) * columns[:, 1:2]
            hat = grad * gain
            grad_ref[rows] = hat
            stat_ref[r] = columns_to_rows([jnp.sum(v, axis=-1, keepdims=True) for v in (hat, hat * unit)])
            lines = [jnp.sum(v, axis=0, keepdims=True) for v in (grad * unit, grad)]
            sum_ref[0:2] += jnp.concatenate(lines, axis=0)

    branch, hat_mix, stat_back, sum_mix = call(
        mix_back_body,
        [((length, width), BF), ((length, heads), F32), ((ranks, 8, pad), F32), ((8, heads), F32)],
        index, *branch_blocks, w_out, attended, norm_mix, vec, specs=[SM] + [VM] * 8, name="mix_back", us=3,
        load=(3,),
    )

    zs = count_d // 2

    def weight_grad(index_ref, left, rights, keep_ref, send_ref, at):
        odd = index_ref[0] % 2
        for k in range(zs):
            cols = pl.ds(pl.multiple_of(((index_ref[0] // 2) ^ k) * 2 * own_rows, 128), 2 * own_rows)
            turned = left[:, cols].T
            start = at
            for right in rights:
                both = nn(turned, right[...])
                upper, lower = both[:own_rows].astype(BF), both[own_rows:].astype(BF)
                stop = start + both.shape[1]
                keep_ref[k, :own_rows, start:stop] = jnp.where(odd == 0, upper, lower)
                send_ref[k, :own_rows, start:stop] = jnp.where(odd == 0, lower, upper)
                start = stop

    def qkv_grad_body(pair, index_ref, unit_ref, d_ref, w_ref, vec_ref, *refs):
        keep_ref, send_ref, sum_ref = refs[-3:]
        odd = index_ref[0] % 2
        d_sum = jnp.sum(d_ref[...].astype(F32), axis=0, keepdims=True)
        w_cols = slice(pair * 384, (pair + 1) * 384)
        for k in range(zs):
            cols = pl.ds(pl.multiple_of(((index_ref[0] // 2) ^ k) * 2 * own_rows, 128), 2 * own_rows)
            both = nn(unit_ref[:, cols].T, d_ref[...])
            weight = w_ref[cols, w_cols].astype(F32)
            sums = [jnp.sum(weight * both, axis=-1, keepdims=True), jnp.sum(weight * d_sum, axis=-1, keepdims=True)]
            lines = columns_to_rows(sums)
            sum_ref[:, cols] = lines + refs[0][:, cols] if len(refs) == 4 else lines
            columns = vec_ref[0:8, cols].T
            both = columns[:, F_GAIN : F_GAIN + 1] * both + columns[:, F_BIAS : F_BIAS + 1] * d_sum
            upper, lower = both[:own_rows].astype(BF), both[own_rows:].astype(BF)
            keep_ref[k] = jnp.where(odd == 0, upper, lower)
            send_ref[k] = jnp.where(odd == 0, lower, upper)

    def qkv_grad(pair, d, after, *before):
        return call(
            functools.partial(qkv_grad_body, pair), [((zs, own_rows, 384), BF)] * 2 + [((8, width), F32)],
            index, unit_one, d, w_qkv, vec, *before, specs=[SM] + [VM] * (4 + len(before)), name="qkv_grad", us=2,
            after=after, token=True,
        )

    def add_body(keep_ref, across_ref, own_ref, *send_refs):
        own_ref[...] = keep_ref[0].astype(F32) + across_ref[0].astype(F32)
        for k, ref in enumerate(send_refs):
            ref[...] = (keep_ref[k + 1].astype(F32) + across_ref[k + 1].astype(F32)).astype(BF)

    def dp_add(keep, across, name, after=()):
        return call(
            add_body, [(keep.shape[1:], F32)] + [(keep.shape[1:], BF)] * (zs - 1), keep, across, name=name, us=1,
            after=after,
        )

    def dp_column_sums(added):
        return [added[0]] + [swap(one, "dp", 2 * (k + 1)) for k, one in enumerate(added[1:])]

    shared_back = tensor_share(stat_back)
    if direct:
        def out_grad_body(index_ref, b_ref, m_ref, keep_ref, send_ref):
            weight_grad(index_ref, b_ref, [m_ref], keep_ref, send_ref, 0)

        keep_out, send_out, out_token = call(
            out_grad_body, [((zs, own_rows, heads), BF)] * 2, index, branch, mixed, specs=[SM] + [VM] * 2,
            name="out_grad", token=True,
        )
        across_out = swap(send_out, "dp", 1)
    arrived_out, _ = tensor_scatter(down_parts, after=shared_back[1:])

    def finish_body(h_ref, p0, p1, p2, vec_ref, out_ref):
        out = p0[...].astype(F32) + p1[...].astype(F32) + p2[...].astype(F32)
        out_ref[...] = (h_ref[...] + out + vec_ref[D_BIAS : D_BIAS + 1]).astype(BF)

    layer_output, finish_token = call(
        finish_body, [((block, width), BF)], hidden_state, *arrived_out, vec, name="finish", store=(0,), token=True
    )


    def three(column):
        upper = column.astype(BF).astype(F32)
        middle = (column - upper).astype(BF).astype(F32)
        return [upper, middle, column - upper - middle]

    def with_lanes(value, s, columns):
        lane = lax.broadcasted_iota(jnp.int32, (1, 128), 1)
        out = jnp.where(half_mask(s), value, 0.0)
        for j, column in enumerate(columns):
            out = jnp.where(lane == HD * (1 - s) + j, column, out)
        return out.astype(BF)

    def attend_back_body(
        pair, q_ref, k_ref, v_ref, a_ref, hat_ref, norm_ref, s0, s1, s2, s3, log_ref, line_ref, cos_ref, sin_ref,
        d_ref, sum_ref, kx_ref, qx_ref, vx_ref, gx_ref, dq_ref, dk_ref, dv_ref,
    ):
        cols = slice(pair * 128, (pair + 1) * 128)
        scale = 1.0 / math.sqrt(HD)
        for r in blocks:
            rows = rows_of(r)
            columns = rows_to_columns(norm_ref[r])
            back = rows_to_columns(summed_stats((s0, s1, s2, s3), r) / width)
            attended = a_ref[rows, cols]
            unit = (attended - columns[:, 0:1]) * columns[:, 1:2]
            grad = columns[:, 1:2] * (hat_ref[rows, cols] - back[:, 0:1] - unit * back[:, 1:2])
            grad = grad.astype(BF).astype(F32)
            mask = jnp.where(rows_to_columns(line_ref[r])[:, 0:1] == 1.0, 0.0, LOW)
            logs = rows_to_columns(log_ref[r])
            q, k, v = (ref[rows, cols].astype(F32) for ref in (q_ref, k_ref, v_ref))
            for s in range(2):
                h = 2 * pair + s
                log = three(logs[:, h : h + 1])
                delta = three(jnp.sum(jnp.where(half_mask(s), grad * attended, 0.0), axis=-1, keepdims=True))
                kx_ref[s, rows] = with_lanes(k * scale, s, [1.0, 1.0, 1.0, mask])
                qx_ref[s, rows] = with_lanes(q, s, [-log[0], -log[1], -log[2], 1.0])
                vx_ref[s, rows] = with_lanes(v, s, [1.0, 1.0, 1.0])
                gx_ref[s, rows] = with_lanes(grad, s, [-delta[0], -delta[1], -delta[2]])
        for s in range(2):
            dq_ref[s] = jnp.zeros((length, 128), F32)

            def step(b, _):
                rows = pl.ds(pl.multiple_of(b * 2 * pad, 16), 2 * pad)
                k = kx_ref[s, rows]
                probs = jnp.exp(nt(k, qx_ref[s]))
                grad_scores = (probs * nt(vx_ref[s, rows], gx_ref[s])).astype(BF)
                dv = nn(probs.astype(BF), gx_ref[s])
                dk = nn(grad_scores, qx_ref[s]) * scale
                if s == 0:
                    dv_ref[rows] = dv
                    dk_ref[rows] = dk
                else:
                    dv_ref[rows] = jnp.where(half_mask(s), dv, dv_ref[rows])
                    dk_ref[rows] = jnp.where(half_mask(s), dk, dk_ref[rows])
                dq_ref[s] += tn(grad_scores, k)
                return 0

            lax.fori_loop(0, ranks // 2, step, 0)
        sum_ref[...] = jnp.zeros_like(sum_ref)
        for r in blocks:
            rows = rows_of(r)
            c, s = cos_ref[rows], -sin_ref[rows]
            dq = turn(jnp.where(half_mask(0), dq_ref[0, rows], dq_ref[1, rows]), c, s).astype(BF)
            dv = dv_ref[rows].astype(BF)
            d_ref[rows, 0:128] = dq
            d_ref[rows, 128:256] = turn(dk_ref[rows], c, s).astype(BF)
            d_ref[rows, 256:384] = dv
            totals = [jnp.sum(t.astype(F32), axis=0, keepdims=True) for t in (dq, dv)]
            sum_ref[0:2] += jnp.concatenate(totals, axis=0)

    def attend_back(pair, after):
        return call(
            functools.partial(attend_back_body, pair), [((length, 384), BF), ((8, 128), F32)],
            queries, keys, values, attended, hat_mix, norm_mix, *shared_back, stat_mix, lines, cosine, sine,
            scratch=[pltpu.VMEM((2, length, 128), BF)] * 4
            + [pltpu.VMEM((2, length, 128), F32)] + [pltpu.VMEM((length, 128), F32)] * 2,
            name="attend_back", us=11, after=after, mib=14,
        )

    d_first, sum_first = attend_back(0, [out_token] if direct else [])
    if direct:
        added_out = dp_add(keep_out, across_out, "out_add", [d_first])
        got_out = dp_column_sums(added_out)
        keep_first, send_first, sum_one, first_token = qkv_grad(0, d_first, [added_out[1]])
    d_last, sum_last = attend_back(1, [first_token, added_out[1], finish_token] if direct else [])
    if direct:
        added_first = dp_add(keep_first, swap(send_first, "dp", 1), "first_add", [d_last])
        got_first = dp_column_sums(added_first)
        sum_ffn = dp_sum_step(sum_ffn, 4, [d_last])
        keep_last, send_last, sum_one, last_token = qkv_grad(
            1, d_last, [added_first[1], *got_out[1:], sum_ffn], sum_one
        )
        across_last = swap(send_last, "dp", 1)

    def vector_body(index_ref, one_ref, first_ref, last_ref, mix_ref, two_ref, out_ref):
        out_ref[...] = jnp.zeros_like(out_ref)
        out_ref[0:2] = one_ref[0:2]
        cols = pl.ds(pl.multiple_of(index_ref[1] * heads, 128), heads)
        out_ref[2:4, cols] = jnp.concatenate([first_ref[0:2], last_ref[0:2]], axis=1)
        out_ref[4:6, cols] = mix_ref[0:2]
        out_ref[6:10] = two_ref[0:4]

    if not direct:
        d_all = joined([d.astype(F32) for d in (d_first.T, d_last.T)]).T
        unit_d = joined([tn(unit_one, d).T for d in (d_first, d_last)]).T
        d_sum = jnp.sum(d_all, axis=0, keepdims=True)
        sum_one = jnp.stack([jnp.sum(w_qkv * v, axis=1) for v in (unit_d, jnp.broadcast_to(d_sum, unit_d.shape))])
        sum_one = jnp.pad(sum_one, ((0, 6), (0, 0)))
    (vectors,) = call(
        vector_body, [((16, width), F32)], index, sum_one, sum_first, sum_last, sum_mix, sum_two, specs=[SM] + [VM] * 5,
        name="vectors",
    )
    shared_vectors = tensor_share(vectors)
    if direct:
        def vector_chunk_body(index_ref, v0, v1, v2, v3, keep_ref, send_ref):
            for k in range(zs):
                for ref, side in ((keep_ref, index_ref[0] % 2), (send_ref, 1 - index_ref[0] % 2)):
                    cols = pl.ds(pl.multiple_of((((index_ref[0] // 2) ^ k) * 2 + side) * own_rows, 128), own_rows)
                    ref[k] = v0[:, cols] + v1[:, cols] + v2[:, cols] + v3[:, cols]

        keep_vec, send_vec = call(
            vector_chunk_body, [((zs, 16, own_rows), F32)] * 2, index, *shared_vectors, specs=[SM] + [VM] * 4,
            name="vector_chunks",
        )
        across_vec = swap(send_vec, "dp", 1)

    def project_back_body(first_block, d0_ref, d1_ref, w_ref, *part_refs):
        for r in (1, 0):
            rows = rows_of(first_block + r)
            grad = nt(d0_ref[rows], w_ref[:, :384]) + nt(d1_ref[rows], w_ref[:, 384:])
            part_refs[r][...] = grad[:block].astype(BF)

    projected = [None, None]
    for j in (1, 0):
        after = [across_vec, across_last, got_first[2]] if j and direct else []
        projected[j] = call(
            functools.partial(project_back_body, 2 * j), [((block, width), BF)] * 2, d_first, d_last, w_qkv,
            name="project_back", us=2, after=after,
        )
    arrived, _ = tensor_scatter([*projected[0], *projected[1]])

    def input_body(p0, p1, p2, x_ref, grad_ref, vec_ref, out_ref):
        grad_first = p0[...].astype(F32) + p1[...].astype(F32) + p2[...].astype(F32)
        x = x_ref[...].astype(F32)
        mean, inverse = center_scale(x)
        unit = (x - mean) * inverse
        out_ref[:, 0, :] = grad_ref[...] + unit_back(grad_first * vec_ref[F_GAIN : F_GAIN + 1], unit, inverse)

    input_grad, input_token = call(
        input_body, [((block, 1, width), F32)], *arrived, x_own, grad_hidden, vec, name="input_grad", store=(0,),
        token=True,
    )

    if direct:
        def last_add_body(keep_ref, across_ref, keep_vec_ref, across_vec_ref, own_ref, *send_refs):
            for k, ref in enumerate((own_ref, *send_refs)):
                ref[:own_rows] = (keep_ref[k].astype(F32) + across_ref[k].astype(F32)).astype(ref.dtype)
                ref[own_rows:] = jnp.zeros((16, 384), ref.dtype)
                ref[own_rows:, :own_rows] = (keep_vec_ref[k] + across_vec_ref[k]).astype(ref.dtype)

        got_last = dp_column_sums(call(
            last_add_body, [((own_rows + 16, 384), F32)] + [((own_rows + 16, 384), BF)] * (zs - 1),
            keep_last, across_last, keep_vec, across_vec, name="last_add", after=got_first[1:],
        ))

        def attn_finish_body(*refs):
            def total(parts):
                return sum(ref[...].astype(F32) for ref in parts)

            early, late = total(refs[:zs]), total(refs[zs : 2 * zs])
            q_ref, k_ref, v_ref, o_ref, model_ref = refs[3 * zs :]
            for k, ref in enumerate((q_ref, k_ref, v_ref)):
                cols = slice(k * 128, (k + 1) * 128)
                ref[:, 0:128] = early[:, cols]
                ref[:, 128:256] = late[:own_rows, cols]
            o_ref[...] = total(refs[2 * zs : 3 * zs]).T
            model_ref[...] = late[own_rows:, :own_rows]

        shapes = [(own_rows, heads)] * 3 + [(heads, own_rows), (16, own_rows)]
        q_grad, k_grad, v_grad, out_grad, model = call(
            attn_finish_body, [(shape, F32) for shape in shapes], *got_first, *got_last, *got_out, store=(0, 1, 2, 3),
            name="attn_finish", after=[input_token, finished_token],
        )
    else:
        qkv_all = vec[F_GAIN][:, None] * unit_d + vec[F_BIAS][:, None] * d_sum
        qkv_all = lax.psum_scatter(qkv_all.astype(BF), "dp", scatter_dimension=0, tiled=True).astype(F32).T
        qkv_all = qkv_all.reshape(2, 3, 128, own_rows)
        q_grad, k_grad, v_grad = (joined(list(qkv_all[:, k])).T for k in range(3))
        out_grad = plain_grad(branch, mixed).T
        model = lax.psum_scatter(sum(shared_vectors), "dp", scatter_dimension=1, tiled=True)
        sum_ffn = lax.psum(sum_ffn, "dp")
    ffn = sum_ffn[:, :hidden]
    return (
        layer_output[None], input_grad.transpose(1, 0, 2), q_grad, k_grad, v_grad,
        model[2], model[3], model[0], model[1], model[4], model[5], out_grad, model[8], model[6], model[7],
        gate_grad, up_grad, ffn[0], ffn[1], ffn[2], ffn[3], down_grad, model[9],
    )


def solution(mesh):
    rows, across, tokens = P("dp", "tensor"), P("tensor", "dp"), P("dp", "tensor", None)
    model, ffn, image = P("dp"), P("tensor"), P("dp", None)
    in_specs = (
        tokens, rows, rows, rows, model, model, model, model, model, model, across, model, model, model, rows, rows,
        ffn, ffn, ffn, ffn, across, model, tokens, image, image, image,
    )
    out_specs = (
        tokens, tokens, rows, rows, rows, model, model, model, model, model, model, across, model, model, model,
        rows, rows, ffn, ffn, ffn, ffn, across, model,
    )
    return jax.shard_map(local, mesh=mesh, in_specs=in_specs, out_specs=out_specs, check_vma=False)
```
